128 devices in a mesh: dp: 8 (over z, core), ctx: 16 (over y, x).
Axes of the slice: x: 4, y: 4, z: 4, core: 2. Of those that a mesh axis runs over, the one named last changes fastest.
Arguments:
- layer_input: bfloat16 [8, 2048, 1536], P('dp', 'ctx'), may hold values from -6 to 6
- cotangent: bfloat16 [8, 2048, 1536], P('dp', 'ctx'), may hold values from -6 to 6
- attn_gain: bfloat16 [1536], P('dp'), may hold values from 0.25 to 1.75
- w_query: bfloat16 [1536, 1536], P('dp'), may hold values from -0.15625 to 0.15625
- w_key: bfloat16 [1536, 768], P('dp'), may hold values from -0.15625 to 0.15625
- w_value: bfloat16 [1536, 768], P('dp'), may hold values from -0.15625 to 0.15625
- w_out: bfloat16 [1536, 1536], P(None, 'dp'), may hold values from -0.625 to 0.625
- mlp_gain: bfloat16 [1536], P('dp'), may hold values from 0.25 to 1.75
- w_gate: bfloat16 [1536, 4096], P('dp'), may hold values from -0.15625 to 0.15625
- w_up: bfloat16 [1536, 4096], P('dp'), may hold values from -0.15625 to 0.15625
- w_down: bfloat16 [4096, 1536], P(None, 'dp'), may hold values from -0.09375 to 0.09375
- doc_lengths: int32 [8, 4], P('dp'), may hold values from 1 to 2045, as said below
- rope_pos: int32 [8, 2048], P('dp', 'ctx'), may hold values from 0 to 2559, as said below
- pad_lengths: int32 [8], P('dp'), may hold values from 0 to 63
Outputs:
- output: bfloat16 [8, 2048, 1536], P('dp', 'ctx')
- input_grad: bfloat16 [8, 2048, 1536], P('dp', 'ctx')
- attn_gain_grad: float32 [1536], P('dp')
- w_query_grad: float32 [1536, 1536], P('dp')
- w_key_grad: float32 [1536, 768], P('dp')
- w_value_grad: float32 [1536, 768], P('dp')
- w_out_grad: float32 [1536, 1536], P(None, 'dp')
- mlp_gain_grad: float32 [1536], P('dp')
- w_gate_grad: float32 [1536, 4096], P('dp')
- w_up_grad: float32 [1536, 4096], P('dp')
- w_down_grad: float32 [4096, 1536], P(None, 'dp')
The draws below stay inside these ranges and needn't reach their ends.
Inputs may be any that keep to these rules, and one draw needn't show every extreme that they name: `doc_lengths`: each row's lengths sum to 2048; the second document starts within the first 64 tokens and ends within the last 128 tokens. `rope_pos`: within each document positions start at 0 and rise by 1 or 2 from one token to the next.
All inputs are finite; a program needn't handle non-finite values.
Results may differ from the reference program's by a relative error of at most 0.025.
Values may be sent and summed in bfloat16 or wider, within the bound.
A program may use at most 256 MiB of HBM per device.

```python
import jax
import jax.numpy as jnp
from jax import lax

D = 1536
HQ = 16
HK = 8
HD = 96
FF = 4096
WINDOW = 1024
BLOCK = 128
SEQS = 8
LENGTH = 2048


def doc_table(key):
    first_key, third_key, fourth_key = jax.random.split(key, 3)
    leading = jax.random.randint(first_key, (SEQS, 1), 1, BLOCK // 2)
    third_len = jax.random.randint(third_key, (SEQS, 1), 1, BLOCK // 2)
    fourth_len = jax.random.randint(fourth_key, (SEQS, 1), 1, BLOCK // 2)
    second_len = LENGTH - leading - third_len - fourth_len
    return jnp.concatenate([leading, second_len, third_len, fourth_len], axis=1).astype(jnp.int32)


def draw_doc_lengths(key, part):
    return doc_table(key)


def draw_rope_pos(key, part):
    lengths = doc_table(key)
    key = jax.random.fold_in(key, 7)
    step_key, offset_key = jax.random.split(key)
    step_sizes = jax.random.randint(step_key, (SEQS, LENGTH), 1, 3).astype(jnp.int32)
    doc_ends = jnp.cumsum(lengths, axis=1).astype(jnp.int32)
    doc_starts = (doc_ends - lengths).astype(jnp.int32)
    token_index = jnp.arange(LENGTH, dtype=jnp.int32)
    second_start = doc_starts[:, 1:2]
    span = lengths[:, 1:2] - 1
    twos = LENGTH + LENGTH // 4 - 1 - span
    offset = jax.random.randint(offset_key, (SEQS, 1), 0, LENGTH).astype(jnp.int32)
    inner = token_index[None, :] - second_start
    in_second = (inner >= 0) & (inner < span)
    forced = jnp.where(jnp.mod(inner + offset, span) < twos, 2, 1).astype(jnp.int32)
    step_sizes = jnp.where(in_second, forced, step_sizes)
    running = jnp.cumsum(step_sizes, axis=1) - step_sizes
    segment = jnp.sum(token_index[None, :, None] >= doc_ends[:, None, :], axis=-1)
    first_token = jnp.take_along_axis(doc_starts, segment, axis=1)
    start_value = jnp.take_along_axis(running, first_token, axis=1)
    return (running - start_value).astype(jnp.int32)


def set_ends(values, key, low, high):
    shape = values.shape
    place = [jax.random.randint(jax.random.fold_in(key, axis), (), 0, shape[axis]) for axis in range(len(shape))]
    values = values.at[tuple(place)].set(low)
    longest = shape.index(max(shape))
    place[longest] = (place[longest] + 1) % shape[longest]
    return values.at[tuple(place)].set(high)


def level_of(stream_key, shape, cuts, least, top_value):
    factor_of = 1.0
    for position, blocks in cuts:
        draws = jax.random.uniform(jax.random.fold_in(jax.random.fold_in(stream_key, 6), position), (blocks,), jnp.float32, least / len(cuts), top_value / len(cuts))
        factor_of = factor_of * jnp.repeat(jnp.exp(draws), shape[position] // blocks).reshape((-1,) + (1,) * (len(shape) - 1 - position))
    return factor_of


def gaussian(key, extent, deviation, bound, cuts=(), kind=jnp.bfloat16):
    values = jax.random.normal(key, extent, jnp.float32) * deviation
    if len(cuts) > 0:
        values = level_of(key, extent, cuts, -0.22, 0.18) * values
    return jnp.clip(values, min=-bound, max=bound).astype(kind)


def setup_inputs(seed: int = 0) -> dict:
    splits = jax.random.split(jax.random.key(seed), 15)
    return {
        "layer_input": gaussian(splits[0], (SEQS, LENGTH, D), 1.0, 6.0, ((0, 8), (1, 16))),
        "cotangent": gaussian(splits[1], (SEQS, LENGTH, D), 1.0, 6.0, ((0, 8), (1, 16))),
        "attn_gain": jnp.clip(1.0 + 0.15 * jax.random.normal(splits[2], (D,), jnp.float32), 0.25, 1.75).astype(jnp.bfloat16),
        "w_query": gaussian(splits[3], (D, HQ * HD), D ** -0.5, 0.15625, ((0, 8),)),
        "w_key": gaussian(splits[4], (D, HK * HD), D ** -0.5, 0.15625, ((0, 8),)),
        "w_value": gaussian(splits[5], (D, HK * HD), D ** -0.5, 0.15625, ((0, 8),)),
        "w_out": gaussian(splits[6], (HQ * HD, D), (HQ * HD // 16) ** -0.5, 0.625, ((1, 8),)),
        "mlp_gain": jnp.clip(1.0 + 0.15 * jax.random.normal(splits[7], (D,), jnp.float32), 0.25, 1.75).astype(jnp.bfloat16),
        "w_gate": gaussian(splits[8], (D, FF), D ** -0.5, 0.15625, ((0, 8),)),
        "w_up": gaussian(splits[9], (D, FF), D ** -0.5, 0.15625, ((0, 8),)),
        "w_down": gaussian(splits[10], (FF, D), FF ** -0.5, 0.09375, ((1, 8),)),
        "doc_lengths": draw_doc_lengths(jax.random.fold_in(splits[14], 71), 0),
        "rope_pos": draw_rope_pos(jax.random.fold_in(splits[14], 71), 0),
        "pad_lengths": set_ends(jax.random.randint(splits[13], (SEQS,), 0, BLOCK // 2), jax.random.fold_in(splits[13], 1), 0, (BLOCK // 2) - 1).astype(jnp.int32),
    }


EPSILON = 1e-05
THETA_BASE = 100000.0
NEG_LARGE = -1e+30

@jax.custom_vjp
def low(v):
    return lax.optimization_barrier(v.astype(jnp.bfloat16)).astype(jnp.float32)

@jax.custom_vjp
def low_back(v):
    return v

def low_keep(v):
    return (low(v), None)

def low_pass(kept, grad):
    return (grad,)

def back_keep(v):
    return (v, None)

def back_low(kept, grad):
    return (low(grad),)
low.defvjp(low_keep, low_pass)
low_back.defvjp(back_keep, back_low)

def matmul_high(left, right):
    return jnp.dot(left, right, precision=lax.Precision.HIGHEST)

def rotate(values, positions):
    half_dim = values.shape[-1] // 2
    freq_table = THETA_BASE ** (-(jnp.arange(half_dim).astype(jnp.float32) * 2.0 / values.shape[-1]))
    angles = positions.astype(jnp.float32)[:, None] * freq_table[None, :]
    cosine = jnp.cos(angles)[:, None, :]
    sine = jnp.sin(angles)[:, None, :]
    first_half = values[..., :half_dim]
    second_half = values[..., half_dim:]
    return jnp.concatenate([first_half * cosine - second_half * sine, second_half * cosine + first_half * sine], axis=-1)

def permitted(query_pos, key_pos, doc_ends, pad_len, seq_len):
    seg_query = lax.optimization_barrier(jnp.sum(query_pos[:, None] >= doc_ends[None, :], axis=-1))
    seg_key = lax.optimization_barrier(jnp.sum(key_pos[:, None] >= doc_ends[None, :], axis=-1))
    behind = query_pos[:, None] - key_pos[None, :]
    usable = (key_pos < seq_len - pad_len) & (key_pos >= 0)
    return (behind >= 0) & (behind < WINDOW) & (seg_query[:, None] == seg_key[None, :]) & (usable[None, :] | (behind == 0))

def attend_block(query_blk, start, keys, values, doc_ends, pad_len):
    rows_here = query_blk.shape[0]
    query_pos = start + jnp.arange(rows_here, dtype=jnp.int32)
    key_pos = jnp.arange(keys.shape[0], dtype=jnp.int32)
    allowed = permitted(query_pos, key_pos, doc_ends, pad_len, keys.shape[0])
    scores = jnp.einsum('qgrd,kgd->grqk', query_blk, keys, precision=lax.Precision.HIGHEST) * HD ** (-0.5)
    scores = low_back(scores)
    scores = jnp.where(allowed[None, None], scores, NEG_LARGE)
    top_score = lax.optimization_barrier(jnp.max(scores, axis=-1, keepdims=True))
    expo = jnp.exp(scores - top_score)
    prob_low = low(expo / lax.optimization_barrier(jnp.sum(expo, axis=-1, keepdims=True)))
    mixed = jnp.einsum('grqk,kgd->qgrd', prob_low, values, precision=lax.Precision.HIGHEST)
    return mixed.reshape(rows_here, HQ * HD)

def attention(queries, keys, values, doc_ends, pad_len):
    rows_all = queries.shape[0]
    block_rows = min(512, rows_all)
    block_count = rows_all // block_rows
    grouped = queries.reshape(block_count, block_rows, HK, HQ // HK, HD)
    starts = (jnp.arange(block_count) * block_rows).astype(jnp.int32)
    blocked = jax.checkpoint(attend_block)
    mixed = lax.map(lambda entry_pair: blocked(entry_pair[0], entry_pair[1], keys, values, doc_ends, pad_len), (grouped, starts))
    return mixed.reshape(rows_all, HQ * HD)

def layer_forward(inputs, gain_attn, weight_query, weight_key, weight_value, weight_out, gain_mlp, weight_gate, weight_up, weight_down, doc_ends, pad_len, positions):
    seq_len = inputs.shape[0]
    inv_one = lax.rsqrt(lax.optimization_barrier(jnp.mean(inputs * inputs, axis=-1, keepdims=True)) + EPSILON)
    hidden_one = low(inputs * inv_one * gain_attn)
    queries = low(rotate(low_back(matmul_high(hidden_one, weight_query)).reshape(seq_len, HQ, HD), positions))
    keys = low(rotate(low_back(matmul_high(hidden_one, weight_key)).reshape(seq_len, HK, HD), positions))
    values = low(low_back(matmul_high(hidden_one, weight_value))).reshape(seq_len, HK, HD)
    attended = attention(queries.reshape(seq_len, HK, HQ // HK, HD), keys, values, doc_ends, pad_len)
    attended = low(low_back(attended))
    resid = inputs + low_back(matmul_high(attended, weight_out))
    inv_two = lax.rsqrt(lax.optimization_barrier(jnp.mean(resid * resid, axis=-1, keepdims=True)) + EPSILON)
    hidden_two = low(resid * inv_two * gain_mlp)
    gate_pre = low_back(matmul_high(hidden_two, weight_gate))
    up_pre = low_back(matmul_high(hidden_two, weight_up))
    mixed = low(jax.nn.silu(gate_pre) * up_pre)
    return resid + low_back(matmul_high(mixed, weight_down))

def reference(layer_input, cotangent, attn_gain, w_query, w_key, w_value, w_out, mlp_gain, w_gate, w_up, w_down, doc_lengths, rope_pos, pad_lengths):
    weights = tuple((weight_arr.astype(jnp.float32) for weight_arr in (attn_gain, w_query, w_key, w_value, w_out, mlp_gain, w_gate, w_up, w_down)))

    def per_sequence(totals, entries):
        tokens, cotan_seq, lengths_seq, pos_seq, pad_seq = entries
        doc_ends = jnp.cumsum(lengths_seq).astype(jnp.int32)

        def forward(inputs, *params):
            return layer_forward(inputs, *params, doc_ends, pad_seq, pos_seq)
        result, pullback = jax.vjp(forward, tokens.astype(jnp.float32), *weights)
        grads = pullback(cotan_seq.astype(jnp.float32))
        totals = tuple((total + grad_one for total, grad_one in zip(totals, grads[1:])))
        return (totals, (result.astype(jnp.bfloat16), grads[0].astype(jnp.bfloat16)))
    initial = tuple((jnp.zeros(weight_arr.shape, jnp.float32) for weight_arr in weights))
    totals, (outputs, input_grads) = lax.scan(per_sequence, initial, (layer_input, cotangent, doc_lengths, rope_pos, pad_lengths))
    return (outputs, input_grads, totals[0], totals[1], totals[2], totals[3], totals[4], totals[5], totals[6], totals[7], totals[8])
```

```python
import functools

import jax
import jax.numpy as jnp
from jax import lax
from jax.experimental import pallas as pl
from jax.experimental.pallas import tpu as pltpu
from jax.sharding import PartitionSpec as P

HQ = 16
HK = 8
HD = 96
WINDOW = 1024
D = 1536
FF = 4096
BLOCK = 128
LENGTH = 2048
DP = 8
CTX = 16
ZN = 4
SHARD = D // DP
FSH = FF // DP
GROUP = 4 * HD

EPSILON = 1e-05
THETA_BASE = 100000.0
NEG_LARGE = -1e30

BF = jnp.bfloat16
F32 = jnp.float32
MESH = pl.DeviceIdType.MESH
ANY = pl.BlockSpec(memory_space=pl.ANY)
VMEM = pl.BlockSpec(memory_space=pltpu.VMEM)


def mod(a, n):
    return lax.rem(a + n, n)


class Place:
    def __init__(self):
        self.dp = lax.axis_index("dp")
        self.ctx = lax.axis_index("ctx")
        self.z, self.core = self.dp // 2, lax.rem(self.dp, 2)
        self.y, self.x = self.ctx // 4, lax.rem(self.ctx, 4)

    def at_x(self, k):
        return (self.dp, self.y * 4 + mod(self.x + k, 4))

    def at_y(self, k):
        return (self.dp, mod(self.y + k, 4) * 4 + self.x)

    def at_z(self, k):
        return (mod(self.z + k, 4) * 2 + self.core, self.ctx)

    def at_dp(self, k):
        return (mod(self.dp + k, DP), self.ctx)

    def at_ctx(self, k):
        return (self.dp, mod(self.ctx + k, CTX))

    def sibling(self):
        return (self.z * 2 + 1 - self.core, self.ctx)


class Net:
    def __init__(self, send, recv, local):
        self.send, self.recv, self.local = send, recv, local
        self.n, self.m = 0, 0

    def remote(self, src, dst, peer):
        copy = pltpu.make_async_remote_copy(
            src_ref=src,
            dst_ref=dst,
            send_sem=self.send.at[self.n],
            recv_sem=self.recv.at[self.n],
            device_id=peer,
            device_id_type=MESH,
        )
        self.n += 1
        copy.start()
        return copy

    def copy(self, src, dst):
        copy = pltpu.make_async_copy(src, dst, self.local.at[self.m])
        self.m += 1
        copy.start()
        return copy


def greet(peers):
    barrier = pltpu.get_barrier_semaphore()
    for peer in peers:
        pl.semaphore_signal(barrier, inc=1, device_id=peer, device_id_type=MESH)
    pl.semaphore_wait(barrier, len(peers))


def xy_peers(p):
    return [p.at_x(k) for k in (1, 2, 3)] + [p.at_y(k) for k in (1, 2, 3)]


def z_peers(p):
    return [p.at_z(k) for k in (1, 2, 3)] + [p.sibling()]


class GatherXY:
    def __init__(self, net, p, own, slot):
        self.net, self.p, self.slot = net, p, slot
        self.kept = [net.copy(own(h), slot(h, p.y, p.x)) for h in (0, 1)]
        self.first, self.rest = {}, []
        for k in (1, 2, 3):
            for h in (0, 1):
                here = slot(h, p.y, p.x)
                along = net.remote(own(h), here, p.at_x(k) if h == 0 else p.at_y(k))
                self.first[h, k] = along
        for k in (1, 2, 3):
            for h in (0, 1):
                here = slot(h, p.y, p.x)
                self.rest.append(net.remote(own(h), here, p.at_y(k) if h == 0 else p.at_x(k)))

    def forward(self):
        net, p = self.net, self.p
        for k in (1, 3, 2):
            for h in (0, 1):
                self.first[h, k].wait_recv()
                if h == 0:
                    block = self.slot(0, p.y, mod(p.x - k, 4))
                else:
                    block = self.slot(1, mod(p.y - k, 4), p.x)
                for m in (1, 2, 3):
                    self.rest.append(net.remote(block, block, p.at_y(m) if h == 0 else p.at_x(m)))

    def end(self):
        for copy in self.first.values():
            copy.wait_send()
        for copy in self.rest:
            copy.wait()
        for copy in self.kept:
            copy.wait()


class GatherDP:
    def __init__(self, net, p, own, slot):
        self.net, self.p, self.slot = net, p, slot
        here = slot(p.dp)
        self.kept = net.copy(own, here)
        self.first = {k: net.remote(own, here, p.at_z(k)) for k in (1, 3, 2)}
        self.rest = [net.remote(own, here, p.sibling())]

    def forward(self):
        net, p = self.net, self.p
        for k in (1, 3, 2):
            self.first[k].wait_recv()
            block = self.slot(mod(p.z - k, 4) * 2 + p.core)
            self.rest.append(net.remote(block, block, p.sibling()))

    def end(self):
        for copy in self.first.values():
            copy.wait_send()
        for copy in self.rest:
            copy.wait()
        self.kept.wait()


class Exchange:
    def __init__(self, net, p, src, slot):
        self.kept = net.copy(src(p.dp), slot(p.dp))
        self.sent = [net.remote(src(mod(p.dp + k, DP)), slot(p.dp), p.at_dp(k)) for k in range(1, DP)]

    def end(self):
        for copy in self.sent:
            copy.wait()
        self.kept.wait()


def add_rows(out, terms):
    rows = out.shape[0]

    def step(r, carry):
        at = pl.ds(pl.multiple_of(r * 16, 16), 16)
        total = terms[0][at, :].astype(F32)
        for term in terms[1:]:
            total = total + term[at, :].astype(F32)
        out[at, :] = total.astype(out.dtype)
        return carry

    lax.fori_loop(0, rows // 16, step, 0)


class ScatterDP:
    def __init__(self, net, p, part, mine, sib, got, out):
        self.net, self.p = net, p
        self.mine, self.sib, self.got, self.out = mine, sib, got, out
        self.loads = [net.copy(part(2 * z + p.core), mine.at[z]) for z in range(ZN)]
        self.swaps = [net.remote(part(2 * z + 1 - p.core), sib.at[z], p.sibling()) for z in range(ZN)]

    def forward(self):
        net, p = self.net, self.p
        self.sent = []
        for copy in self.loads + self.swaps:
            copy.wait()
        for k in (2, 1, 3, 0):
            z = mod(p.z + k, 4)
            block = self.mine.at[z]
            add_rows(block, [block, self.sib.at[z]])
            if k:
                self.sent.append(net.remote(block, self.got.at[k - 1], p.at_z(k)))

    def end(self):
        for copy in self.sent:
            copy.wait()
        add_rows(self.out, [self.mine.at[self.p.z]] + [self.got.at[k] for k in range(3)])


class ScatterXY:
    def __init__(self, net, p, cut, first, second, wide, piece, along):
        self.net, self.p, self.along = net, p, along
        self.first, self.second, self.wide, self.piece = first, second, wide, piece
        self.loads = [
            net.copy(cut(0, None, p.x), wide[0]),
            net.copy(cut(1, p.y, None), wide[1]),
        ]
        self.sent = []
        for k in (1, 3, 2):
            self.sent.append(net.remote(cut(0, None, mod(p.x + k, 4)), first[0].at[k - 1], p.at_x(k)))
            self.sent.append(net.remote(cut(1, mod(p.y + k, 4), None), first[1].at[k - 1], p.at_y(k)))

    def forward(self):
        net, p = self.net, self.p
        for copy in self.loads + self.sent:
            copy.wait()
        self.sent = []
        for h in (0, 1):
            add_all(self.wide[h], [self.wide[h]] + [self.first[h].at[k] for k in range(3)])
            for k in (1, 3, 2):
                block = self.along(h, self.wide[h], mod((p.y if h == 0 else p.x) + k, 4))
                peer = p.at_y(k) if h == 0 else p.at_x(k)
                self.sent.append(net.remote(block, self.second[h].at[k - 1], peer))

    def end(self):
        p = self.p
        for copy in self.sent:
            copy.wait()
        for h in (0, 1):
            own = self.along(h, self.wide[h], p.y if h == 0 else p.x)
            add_all(self.piece(h), [own] + [self.second[h].at[k] for k in range(3)])


def add_all(out, terms):
    lead = out.shape[:-2]
    if not lead:
        return add_rows(out, terms)
    count = 1
    for n in lead:
        count *= n
    rows = out.shape[-2] // 16

    def step(i, carry):
        j, r = i // rows, lax.rem(i, rows)
        index = []
        for n in reversed(lead):
            index.insert(0, lax.rem(j, n))
            j = j // n
        at = (*index, pl.ds(pl.multiple_of(r * 16, 16), 16), slice(None))
        total = terms[0][at].astype(F32)
        for term in terms[1:]:
            total = total + term[at].astype(F32)
        out[at] = total.astype(out.dtype)
        return carry

    lax.fori_loop(0, count * rows, step, 0)


def call(body, ident, outs, out_places, remotes, locals_, scratch, *args, vmem=56):
    return pl.pallas_call(
        body,
        out_shape=outs,
        in_specs=[ANY] * len(args),
        out_specs=out_places,
        scratch_shapes=[
            *scratch,
            pltpu.SemaphoreType.DMA((remotes,)),
            pltpu.SemaphoreType.DMA((remotes,)),
            pltpu.SemaphoreType.DMA((locals_,)),
        ],
        compiler_params=pltpu.CompilerParams(
            collective_id=ident, has_side_effects=True, vmem_limit_bytes=vmem << 20
        ),
    )(*args)


def shape(*dims, dtype=BF):
    return jax.ShapeDtypeStruct(dims, dtype)


def half(ref, h, n=64):
    return ref.at[pl.ds(h * n, n)]


def first_exchange(h1, pos, wgrp, w_out_t, wpiece):
    def body(h1, pos, wgrp, w_out_t, wpiece, seq, posq, wjob, wdh, wo, wfp, send, recv, local):
        p = Place()
        net = Net(send, recv, local)
        greet(xy_peers(p) + [p.at_dp(k) for k in range(1, DP)])
        rows = GatherXY(
            net, p, lambda h: half(h1, h), lambda h, y, x: seq.at[y * 4 + x, pl.ds(h * 64, 64)]
        )
        spots = GatherXY(
            net, p, lambda h: half(pos, h, 8), lambda h, y, x: posq.at[y * 4 + x, pl.ds(h * 8, 8)]
        )
        job = GatherDP(net, p, wgrp.at[p.ctx // 2], lambda i: wjob.at[i])
        ffw = Exchange(net, p, lambda i: wpiece.at[i], lambda i: wfp.at[:, i])
        out = GatherDP(net, p, w_out_t, lambda i: wo.at[i])
        grp = Exchange(net, p, lambda i: wgrp.at[i], lambda i: wdh.at[i])
        spots.forward()
        job.forward()
        rows.forward()
        out.forward()
        for part in (rows, spots, job, ffw, out, grp):
            part.end()

    return call(
        body,
        1,
        (
            shape(CTX, BLOCK, D),
            shape(CTX, 16, BLOCK, dtype=F32),
            shape(DP, SHARD, GROUP),
            shape(DP, SHARD, GROUP),
            shape(DP, SHARD, D),
            shape(3, DP, 48, 128),
        ),
        [ANY] * 6,
        90,
        8,
        [],
        h1,
        pos,
        wgrp,
        w_out_t,
        wpiece,
    )


def heads_home(att):
    def body(att, out, send, recv, local):
        p = Place()
        net = Net(send, recv, local)
        greet([p.at_ctx(k) for k in range(1, CTX)])
        lanes = lambda c: pl.ds(pl.multiple_of(c * BLOCK, BLOCK), BLOCK)
        kept = net.copy(att.at[:, lanes(p.ctx)], out.at[p.ctx])
        sent = [
            net.remote(att.at[:, lanes(mod(p.ctx + k, CTX))], out.at[p.ctx], p.at_ctx(k))
            for k in range(1, CTX)
        ]
        for copy in sent:
            copy.wait()
        kept.wait()

    return call(body, 2, shape(CTX, HD, BLOCK), ANY, 15, 1, [], att)


def middle_exchange(h2, dd, wfp):
    def body(h2, dd, wfp, h2_all, dd_all, wf, send, recv, local):
        p = Place()
        net = Net(send, recv, local)
        greet(xy_peers(p) + z_peers(p))
        hid = GatherDP(net, p, h2, lambda i: h2_all.at[i])
        wts = GatherXY(
            net,
            p,
            lambda h: wfp.at[:, pl.ds(4 * h, 4)],
            lambda h, y, x: wf.at[
                :,
                pl.ds(4 * h, 4),
                pl.ds(pl.multiple_of(y * 48, 16), 48),
                pl.ds(pl.multiple_of(x * 128, 128), 128),
            ],
        )
        hid.forward()
        cot = GatherDP(net, p, dd, lambda i: dd_all.at[i])
        wts.forward()
        cot.forward()
        for part in (hid, cot, wts):
            part.end()

    return call(
        body,
        3,
        (shape(DP, BLOCK, D), shape(DP, BLOCK, D), shape(3, DP, SHARD, FSH)),
        [ANY] * 3,
        46,
        4,
        [],
        h2,
        dd,
        wfp,
    )


def scatter_dp_scratch():
    return [
        pltpu.VMEM((ZN, BLOCK, D), BF),
        pltpu.VMEM((ZN, BLOCK, D), BF),
        pltpu.VMEM((3, BLOCK, D), BF),
    ]


def back_exchange(dh2, dwf):
    def body(dh2, dwf, out, piece, mine, sib, got, f0, f1, s0, s1, w0, w1, send, recv, local):
        p = Place()
        net = Net(send, recv, local)
        greet(xy_peers(p) + z_peers(p))
        hid = ScatterDP(net, p, lambda i: dh2.at[i], mine, sib, got, out)

        def cut(h, y, x):
            rows = slice(None) if y is None else pl.ds(pl.multiple_of(y * 48, 16), 48)
            lanes = slice(None) if x is None else pl.ds(pl.multiple_of(x * 128, 128), 128)
            return dwf.at[:, pl.ds(4 * h, 4), rows, lanes]

        def along(h, ref, at):
            if h == 0:
                return ref.at[:, :, pl.ds(pl.multiple_of(at * 48, 16), 48), :]
            return ref.at[:, :, :, pl.ds(pl.multiple_of(at * 128, 128), 128)]

        wts = ScatterXY(
            net, p, cut, (f0, f1), (s0, s1), (w0, w1), lambda h: piece.at[:, pl.ds(4 * h, 4)], along
        )
        hid.forward()
        wts.forward()
        hid.end()
        wts.end()

    return call(
        body,
        4,
        (shape(BLOCK, D, dtype=F32), shape(3, DP, 48, 128)),
        [VMEM] * 2,
        20,
        6,
        [
            *scatter_dp_scratch(),
            pltpu.VMEM((3, 3, 4, SHARD, 128), BF),
            pltpu.VMEM((3, 3, 4, 48, FSH), BF),
            pltpu.VMEM((3, 3, 4, 48, 128), BF),
            pltpu.VMEM((3, 3, 4, 48, 128), BF),
            pltpu.VMEM((3, 4, SHARD, 128), BF),
            pltpu.VMEM((3, 4, 48, FSH), BF),
        ],
        dh2,
        dwf,
    )


def heads_out(dat, att, da_t, piece):
    def body(dat, att, da_t, piece, heads, att_all, da_all, grads, send, recv, local):
        p = Place()
        net = Net(send, recv, local)
        greet([p.at_ctx(k) for k in range(1, CTX)] + [p.at_dp(k) for k in range(1, DP)])
        kept = net.copy(dat.at[p.ctx], heads.at[p.ctx])
        sent = [
            net.remote(dat.at[mod(p.ctx + k, CTX)], heads.at[p.ctx], p.at_ctx(k))
            for k in range(1, CTX)
        ]
        atts = GatherDP(net, p, att, lambda i: att_all.at[i])
        das = Exchange(net, p, lambda i: da_t.at[i], lambda i: da_all.at[i])
        wts = Exchange(net, p, lambda i: piece.at[:, i], lambda i: grads.at[i])
        atts.forward()
        for copy in sent:
            copy.wait()
        kept.wait()
        for part in (atts, das, wts):
            part.end()

    return call(
        body,
        5,
        (
            shape(CTX, HD, BLOCK),
            shape(DP, D, BLOCK),
            shape(DP, SHARD, BLOCK),
            shape(DP, 3, 48, 128),
        ),
        [ANY] * 4,
        36,
        4,
        [],
        dat,
        att,
        da_t,
        piece,
    )


def grads_home(dqkv, dwj, dwo):
    def body(
        dqkv, dwj, dwo, out, pair, piece, full, mine, sib, got, away, f0, s0, w0, send, recv, local
    ):
        p = Place()
        net = Net(send, recv, local)
        group, rank = p.ctx // 2, lax.rem(p.ctx, 2)
        home = group == p.dp
        partner = (p.dp, p.ctx + 1 - 2 * rank)

        barrier = pltpu.get_barrier_semaphore()
        others = xy_peers(p) + z_peers(p)
        for peer in others:
            pl.semaphore_signal(barrier, inc=1, device_id=peer, device_id_type=MESH)
        for i in range(DP):
            for r in range(2):
                own = home & (p.dp == i) & (rank == r)

                @pl.when(jnp.logical_not(own))
                def _():
                    peer = (jnp.int32(i), 2 * p.dp + r)
                    pl.semaphore_signal(barrier, inc=1, device_id=peer, device_id_type=MESH)

        pl.semaphore_wait(barrier, CTX + len(others) - home.astype(jnp.int32))

        lanes = lambda c: pl.ds(pl.multiple_of(c * BLOCK, BLOCK), BLOCK)
        slot = p.dp * 2 + rank

        def message(k, spot):
            c = mod(p.ctx + k, CTX)
            return pltpu.make_async_remote_copy(
                src_ref=dqkv.at[:, lanes(c)],
                dst_ref=out.at[spot],
                send_sem=send.at[k],
                recv_sem=recv.at[spot],
                device_id=(group, c),
                device_id_type=MESH,
            )

        own = pltpu.make_async_copy(dqkv.at[:, lanes(p.ctx)], out.at[slot], local.at[0])
        net.m = 1

        @pl.when(home)
        def _():
            own.start()

        @pl.when(jnp.logical_not(home))
        def _():
            message(0, slot).start()

        for k in range(1, CTX):
            message(k, slot).start()
        net.n = CTX

        hid = ScatterDP(net, p, lambda i: dwj.at[i], mine, sib, got, full)
        wide = [net.copy(dwo.at[:, pl.ds(pl.multiple_of(p.x * 384, 128), 384)], w0)]
        for k in (1, 3, 2):
            cut = dwo.at[:, pl.ds(pl.multiple_of(mod(p.x + k, 4) * 384, 128), 384)]
            wide.append(net.remote(cut, f0.at[k - 1], p.at_x(k)))
        hid.forward()
        for copy in wide:
            copy.wait()
        add_rows(w0, [w0] + [f0.at[k] for k in range(3)])
        tall = []
        for k in (1, 3, 2):
            cut = w0.at[pl.ds(pl.multiple_of(mod(p.y + k, 4) * 48, 16), 48)]
            tall.append(net.remote(cut, s0.at[k - 1], p.at_y(k)))
        hid.end()
        theirs = full.at[pl.ds(pl.multiple_of((1 - rank) * 96, 16), 96)]
        swap = net.remote(theirs, away, partner)
        for copy in tall:
            copy.wait()
        add_rows(piece, [w0.at[pl.ds(pl.multiple_of(p.y * 48, 16), 48)]] + [s0.at[k] for k in range(3)])
        swap.wait()
        add_rows(pair, [full.at[pl.ds(pl.multiple_of(rank * 96, 16), 96)], away])

        for k in range(1, CTX):
            message(k, slot).wait_send()

        @pl.when(home)
        def _():
            own.wait()

        @pl.when(jnp.logical_not(home))
        def _():
            message(0, slot).wait_send()

        for spot in range(CTX):
            here = home & (slot == spot)

            @pl.when(jnp.logical_not(here))
            def _():
                message(0, spot).wait_recv()

    return call(
        body,
        6,
        (shape(CTX, 3 * HD, BLOCK), shape(96, GROUP), shape(48, 384)),
        [ANY, VMEM, VMEM],
        40,
        8,
        [
            pltpu.VMEM((SHARD, GROUP), BF),
            pltpu.VMEM((ZN, SHARD, GROUP), BF),
            pltpu.VMEM((ZN, SHARD, GROUP), BF),
            pltpu.VMEM((3, SHARD, GROUP), BF),
            pltpu.VMEM((96, GROUP), BF),
            pltpu.VMEM((3, SHARD, 384), BF),
            pltpu.VMEM((3, 48, 384), BF),
            pltpu.VMEM((SHARD, 384), BF),
        ],
        dqkv,
        dwj,
        dwo,
    )


def last_exchange(dh1, ypart, grads, pair, piece):
    def body(dh1, ypart, grads, pair, piece, e1, ysum, gff, gqkv, gout, *rest):
        scratch, (send, recv, local) = rest[:-3], rest[-3:]
        p = Place()
        net = Net(send, recv, local)
        greet(xy_peers(p) + z_peers(p))
        inp = ScatterDP(net, p, lambda i: dh1.at[i], *scratch[:3], e1)
        wts = GatherXY(
            net,
            p,
            lambda h: grads.at[pl.ds(4 * h, 4)],
            lambda h, y, x: gff.at[
                pl.ds(4 * h, 4),
                :,
                pl.ds(pl.multiple_of(y * 48, 16), 48),
                pl.ds(pl.multiple_of(x * 128, 128), 128),
            ],
        )
        qkv = GatherXY(
            net, p, lambda h: half(pair, h, 48), lambda h, y, x: gqkv.at[y * 4 + x, pl.ds(h * 48, 48)]
        )
        proj = GatherXY(
            net,
            p,
            lambda h: piece.at[pl.ds(32 * h, 32 - 16 * h)],
            lambda h, y, x: gout.at[
                pl.ds(pl.multiple_of(y * 48 + 32 * h, 16), 32 - 16 * h),
                pl.ds(pl.multiple_of(x * 384, 128), 384),
            ],
        )
        inp.forward()
        res = ScatterDP(net, p, lambda i: ypart.at[i], *scratch[3:6], ysum)
        wts.forward()
        qkv.forward()
        proj.forward()
        res.forward()
        inp.end()
        res.end()
        for part in (wts, qkv, proj):
            part.end()

    return call(
        body,
        7,
        (
            shape(BLOCK, D, dtype=F32),
            shape(BLOCK, D, dtype=F32),
            shape(DP, 3, SHARD, FSH),
            shape(CTX, 96, GROUP),
            shape(SHARD, D),
        ),
        [VMEM, VMEM, ANY, ANY, ANY],
        110,
        16,
        scatter_dp_scratch() + scatter_dp_scratch(),
        dh1,
        ypart,
        grads,
        pair,
        piece,
    )


CHUNK = 256
CHUNKS = LENGTH // CHUNK
SCALE = HD ** (-0.5)


def span(j):
    return max(0, j * CHUNK - WINDOW), (j + 1) * CHUNK


def score_block(k, q_t, hi, j):
    low, high = span(j)
    s = jnp.dot(k[low:high, :], q_t[:, j * CHUNK : (j + 1) * CHUNK], preferred_element_type=F32)
    s = s * SCALE
    key = low + lax.broadcasted_iota(jnp.int32, s.shape, 0)
    query = j * CHUNK + lax.broadcasted_iota(jnp.int32, s.shape, 1)
    last = hi[low:high, :]
    last = jnp.concatenate([last] * (CHUNK // 128), axis=1)
    return jnp.where((query >= key) & (query <= last), s, NEG_LARGE)


def attend(q_t, k_t, v_t, hi):
    def body(q_t, k_t, v_t, hi, out, top, total, k):
        k[...] = k_t[...].T
        for j in range(CHUNKS):
            low, high = span(j)
            at = slice(j * CHUNK, (j + 1) * CHUNK)
            s = score_block(k, q_t, hi, j)
            m = jnp.max(s, axis=0, keepdims=True)
            e = jnp.exp(s - m)
            t = jnp.sum(e, axis=0, keepdims=True)
            prob = (e * (1.0 / t)).astype(BF)
            o = jnp.dot(v_t[:, low:high], prob, preferred_element_type=F32)
            out[:, at] = o.astype(BF)
            top[:, at] = m
            total[:, at] = t

    return pl.pallas_call(
        body,
        out_shape=(shape(HD, LENGTH), shape(1, LENGTH, dtype=F32), shape(1, LENGTH, dtype=F32)),
        in_specs=[VMEM] * 4,
        out_specs=[VMEM] * 3,
        scratch_shapes=[pltpu.VMEM((LENGTH, HD), BF)],
        compiler_params=pltpu.CompilerParams(vmem_limit_bytes=56 << 20),
        cost_estimate=pl.CostEstimate(flops=800_000_000, bytes_accessed=4 << 20, transcendentals=2_000_000),
    )(q_t, k_t, v_t, hi)


def attend_back(q_t, k_t, v_t, do_blocks, hi, top, total):
    def body(q_t, k_t, v_t, do_blocks, hi, top, total, dq, dk_t, dv_t, k, v, q, do, do_t, dk, dv):
        k[...] = k_t[...].T
        v[...] = v_t[...].T
        q[...] = q_t[...].T
        for b in range(CTX):
            do_t[:, b * BLOCK : (b + 1) * BLOCK] = do_blocks[b]
        do[...] = do_t[...].T
        dk[...] = jnp.zeros_like(dk)
        dv[...] = jnp.zeros_like(dv)
        for j in range(CHUNKS):
            low, high = span(j)
            at = slice(j * CHUNK, (j + 1) * CHUNK)
            s = score_block(k, q_t, hi, j)
            prob = jnp.exp(s - top[:, at]) * (1.0 / total[:, at])
            dp = jnp.dot(v[low:high, :], do_t[:, at], preferred_element_type=F32)
            inner = jnp.sum(prob * dp, axis=0, keepdims=True)
            ds = (prob * (dp - inner)).astype(BF)
            dq[:, at] = jnp.dot(k_t[:, low:high], ds, preferred_element_type=F32) * SCALE
            dk[low:high, :] += jnp.dot(ds, q[at, :], preferred_element_type=F32)
            dv[low:high, :] += jnp.dot(prob.astype(BF), do[at, :], preferred_element_type=F32)
        dk_t[...] = dk[...].T * SCALE
        dv_t[...] = dv[...].T

    return pl.pallas_call(
        body,
        out_shape=(shape(HD, LENGTH, dtype=F32),) * 3,
        in_specs=[VMEM] * 7,
        out_specs=[VMEM] * 3,
        scratch_shapes=[
            pltpu.VMEM((LENGTH, HD), BF),
            pltpu.VMEM((LENGTH, HD), BF),
            pltpu.VMEM((LENGTH, HD), BF),
            pltpu.VMEM((LENGTH, HD), BF),
            pltpu.VMEM((HD, LENGTH), BF),
            pltpu.VMEM((LENGTH, HD), F32),
            pltpu.VMEM((LENGTH, HD), F32),
        ],
        compiler_params=pltpu.CompilerParams(vmem_limit_bytes=56 << 20),
        cost_estimate=pl.CostEstimate(flops=2_000_000_000, bytes_accessed=6 << 20, transcendentals=2_000_000),
    )(q_t, k_t, v_t, do_blocks, hi, top, total)


def dot(left, right, contract):
    return lax.dot_general(left, right, (contract, ((), ())), preferred_element_type=F32)


def turn(values, cosine, sine):
    a, b = values[: HD // 2], values[HD // 2 :]
    return jnp.concatenate([a * cosine - b * sine, b * cosine + a * sine], axis=0)


def on_device(
    layer_input,
    cotangent,
    attn_gain,
    w_query,
    w_key,
    w_value,
    w_out,
    mlp_gain,
    w_gate,
    w_up,
    w_down,
    doc_lengths,
    rope_pos,
    pad_lengths,
):
    ctx = lax.axis_index("ctx")
    row, col = ctx // 4, lax.rem(ctx, 4)
    rank = lax.rem(ctx, 2)
    gain_a = attn_gain.astype(F32)
    gain_m = mlp_gain.astype(F32)

    inputs = layer_input[0].astype(F32)
    inv_one = lax.rsqrt(jnp.mean(inputs * inputs, axis=-1, keepdims=True) + EPSILON)
    u1 = inputs * inv_one

    wgrp = jnp.concatenate(
        [w_query.reshape(SHARD, HK, 2 * HD), w_key.reshape(SHARD, HK, HD), w_value.reshape(SHARD, HK, HD)],
        axis=2,
    )
    wgrp = (wgrp.astype(F32) * gain_a[:, None, None]).astype(BF).transpose(1, 0, 2)
    w_out_t = w_out.T

    def wide_piece(w):
        rows = lax.dynamic_slice_in_dim(w, row * 48, 48, 0).reshape(48, DP, 4, 128)
        return lax.dynamic_slice_in_dim(rows, col, 1, 2)[:, :, 0].transpose(1, 0, 2)

    gains = lax.dynamic_slice_in_dim(gain_m, row * 48, 48, 0)[None, :, None]
    down = lax.dynamic_slice_in_dim(w_down.reshape(DP, 4, 128, SHARD), col, 1, 1)[:, 0]
    down = lax.dynamic_slice_in_dim(down, row * 48, 48, 2).transpose(0, 2, 1)
    wpiece = jnp.stack(
        [
            (wide_piece(w_gate).astype(F32) * gains).astype(BF),
            (wide_piece(w_up).astype(F32) * gains).astype(BF),
            down,
        ],
        axis=1,
    )
    pos = jnp.broadcast_to(rope_pos.astype(F32), (16, BLOCK))

    seq, posq, wjob, wdh, wo, wfp = first_exchange(u1.astype(BF), pos, wgrp, w_out_t, wpiece)
    seq = seq.reshape(LENGTH, D)
    wo = wo.reshape(D, D)

    freq = THETA_BASE ** (-(jnp.arange(HD // 2).astype(F32) * 2.0 / HD))
    angles = freq[:, None] * posq[:, 0, :].reshape(1, LENGTH)
    cosine, sine = jnp.cos(angles), jnp.sin(angles)

    ends = jnp.cumsum(doc_lengths[0])
    token = jnp.arange(LENGTH, dtype=jnp.int32)
    seg = jnp.sum(token[:, None] >= ends[None, :], axis=-1)
    doc_end = jnp.sum(jnp.where(seg[:, None] == jnp.arange(4)[None, :], ends[None, :], 0), axis=-1)
    hi = jnp.minimum(token + WINDOW - 1, doc_end - 1)
    hi = jnp.where(token >= LENGTH - pad_lengths[0], token, hi)
    hi = jnp.broadcast_to(hi[:, None], (LENGTH, 128)).astype(jnp.int32)

    proj = dot(wjob.reshape(D, GROUP), seq, ((0,), (1,)))
    q_t = turn(lax.dynamic_slice_in_dim(proj, rank * HD, HD, 0), cosine, sine).astype(BF)
    k_t = turn(proj[2 * HD : 3 * HD], cosine, sine).astype(BF)
    v_t = proj[3 * HD :].astype(BF)
    att_t, top, total = attend(q_t, k_t, v_t, hi)

    att = heads_home(att_t).reshape(D, BLOCK)
    resid = inputs + dot(att, wo, ((0,), (1,)))
    inv_two = lax.rsqrt(jnp.mean(resid * resid, axis=-1, keepdims=True) + EPSILON)
    u2 = resid * inv_two
    dd = cotangent[0]

    hid, cot, wf = middle_exchange(u2.astype(BF), dd, wfp)
    hid = hid.reshape(DP * BLOCK, D)
    cot = cot.reshape(DP * BLOCK, D)
    wf = wf.reshape(3, D, FSH)
    gate = dot(hid, wf[0], ((1,), (0,)))
    up = dot(hid, wf[1], ((1,), (0,)))
    sig = jax.nn.sigmoid(gate)
    act = gate * sig
    mixed = (act * up).astype(BF)
    dmix = dot(cot, wf[2], ((1,), (0,)))
    dgate = (dmix * up * sig * (1.0 + gate * (1.0 - sig))).astype(BF)
    dup = (dmix * act).astype(BF)
    ypart = dot(mixed, wf[2], ((1,), (1,))).astype(BF).reshape(DP, BLOCK, D)
    epart = dot(dgate, wf[0], ((1,), (1,))) + dot(dup, wf[1], ((1,), (1,)))
    dwf = jnp.stack(
        [
            dot(hid, dgate, ((0,), (0,))).astype(BF),
            dot(hid, dup, ((0,), (0,))).astype(BF),
            dot(cot, mixed, ((0,), (0,))).astype(BF),
        ]
    ).reshape(3, DP, SHARD, FSH)

    e2, piece = back_exchange(epart.astype(BF).reshape(DP, BLOCK, D), dwf)
    dy = dd.astype(F32)
    dresid = dy + inv_two * (e2 - u2 * jnp.mean(e2 * u2, axis=-1, keepdims=True))
    da = dresid.astype(BF)
    dat = dot(wo, da, ((0,), (1,))).astype(BF).reshape(CTX, HD, BLOCK)
    da_t = da.T.reshape(DP, SHARD, BLOCK)

    do_blocks, att_all, da_all, grads = heads_out(dat, att, da_t, piece)
    dq, dk, dv = attend_back(q_t, k_t, v_t, do_blocks, hi, top, total)
    dq = turn(dq, cosine, -sine).astype(BF)
    dk = turn(dk, cosine, -sine).astype(BF)
    dv = dv.astype(BF)
    none = jnp.zeros_like(dq)
    wide = jnp.concatenate(
        [jnp.where(rank == 0, dq, none), jnp.where(rank == 1, dq, none), dk, dv], axis=0
    )
    dwj = dot(seq, wide, ((0,), (1,))).astype(BF).reshape(DP, SHARD, GROUP)
    dwo = dot(da_all, att_all, ((0, 2), (0, 2))).astype(BF)

    back, pair, opiece = grads_home(jnp.concatenate([dq, dk, dv], axis=0), dwj, dwo)
    back = back.reshape(DP, 2, 3 * HD, BLOCK)
    both = back[:, 0, HD:].astype(F32) + back[:, 1, HD:].astype(F32)
    group = jnp.concatenate([back[:, 0, :HD], back[:, 1, :HD], both.astype(BF)], axis=1)
    dh1 = lax.dot_general(
        group.transpose(0, 2, 1).reshape(DP * BLOCK, GROUP),
        wdh.reshape(D, GROUP),
        (((1,), (1,)), ((), ())),
        preferred_element_type=F32,
    )

    e1, ysum, gff, gqkv, gout = last_exchange(
        dh1.astype(BF).reshape(DP, BLOCK, D), ypart, grads, pair, opiece
    )
    output = (resid + ysum).astype(BF)
    grad_in = dresid + inv_one * (e1 - u1 * jnp.mean(e1 * u1, axis=-1, keepdims=True))

    gqkv = gqkv.reshape(HK, 2 * 96, GROUP).astype(F32).transpose(1, 0, 2)
    dwq = gqkv[:, :, : 2 * HD].reshape(SHARD, D)
    dwk = gqkv[:, :, 2 * HD : 3 * HD].reshape(SHARD, HK * HD)
    dwv = gqkv[:, :, 3 * HD :].reshape(SHARD, HK * HD)
    dgain_a = (
        jnp.sum(dwq * w_query.astype(F32), axis=1)
        + jnp.sum(dwk * w_key.astype(F32), axis=1)
        + jnp.sum(dwv * w_value.astype(F32), axis=1)
    )
    gff = gff.astype(F32)
    dwg = gff[:, 0].transpose(1, 0, 2).reshape(SHARD, FF)
    dwu = gff[:, 1].transpose(1, 0, 2).reshape(SHARD, FF)
    dwd = gff[:, 2].transpose(0, 2, 1).reshape(FF, SHARD)
    dgain_m = jnp.sum(dwg * w_gate.astype(F32), axis=1) + jnp.sum(dwu * w_up.astype(F32), axis=1)
    rows_a, rows_m = gain_a[:, None], gain_m[:, None]
    return (
        output[None],
        grad_in.astype(BF)[None],
        dgain_a,
        dwq * rows_a,
        dwk * rows_a,
        dwv * rows_a,
        gout.astype(F32).T,
        dgain_m,
        dwg * rows_m,
        dwu * rows_m,
        dwd,
    )


def solution(mesh):
    in_specs = (
        P("dp", "ctx", None),
        P("dp", "ctx", None),
        P("dp"),
        P("dp", None),
        P("dp", None),
        P("dp", None),
        P(None, "dp"),
        P("dp"),
        P("dp", None),
        P("dp", None),
        P(None, "dp"),
        P("dp", None),
        P("dp", "ctx"),
        P("dp"),
    )
    out_specs = (
        P("dp", "ctx", None),
        P("dp", "ctx", None),
        P("dp"),
        P("dp", None),
        P("dp", None),
        P("dp", None),
        P(None, "dp"),
        P("dp"),
        P("dp", None),
        P("dp", None),
        P(None, "dp"),
    )
    return jax.shard_map(
        on_device, mesh=mesh, in_specs=in_specs, out_specs=out_specs, check_vma=False
    )
```

```python
import functools

import jax
import jax.numpy as jnp
from jax import lax
from jax.experimental import pallas as pl
from jax.experimental.pallas import tpu as pltpu
from jax.sharding import PartitionSpec as P

HQ = 16
HK = 8
HD = 96
WINDOW = 1024
D = 1536
FF = 4096
BLOCK = 128
LENGTH = 2048
DP = 8
CTX = 16
ZN = 4
SHARD = D // DP
FSH = FF // DP
GROUP = 4 * HD

EPSILON = 1e-05
THETA_BASE = 100000.0
NEG_LARGE = -1e30

BF = jnp.bfloat16
F32 = jnp.float32
MESH = pl.DeviceIdType.MESH
ANY = pl.BlockSpec(memory_space=pl.ANY)
VMEM = pl.BlockSpec(memory_space=pltpu.VMEM)


def mod(a, n):
    return lax.rem(a + n, n)


class Place:
    def __init__(self):
        self.dp = lax.axis_index("dp")
        self.ctx = lax.axis_index("ctx")
        self.z, self.core = self.dp // 2, lax.rem(self.dp, 2)
        self.y, self.x = self.ctx // 4, lax.rem(self.ctx, 4)

    def at_x(self, k):
        return (self.dp, self.y * 4 + mod(self.x + k, 4))

    def at_y(self, k):
        return (self.dp, mod(self.y + k, 4) * 4 + self.x)

    def at_z(self, k):
        return (mod(self.z + k, 4) * 2 + self.core, self.ctx)

    def at_dp(self, k):
        return (mod(self.dp + k, DP), self.ctx)

    def at_ctx(self, k):
        return (self.dp, mod(self.ctx + k, CTX))

    def sibling(self):
        return (self.z * 2 + 1 - self.core, self.ctx)


class Net:
    def __init__(self, send, recv, local):
        self.send, self.recv, self.local = send, recv, local
        self.n, self.m = 0, 0

    def remote(self, src, dst, peer):
        assert self.n < self.send.shape[0]
        copy = pltpu.make_async_remote_copy(
            src_ref=src,
            dst_ref=dst,
            send_sem=self.send.at[self.n],
            recv_sem=self.recv.at[self.n],
            device_id=peer,
            device_id_type=MESH,
        )
        self.n += 1
        copy.start()
        return copy

    def copy(self, src, dst):
        assert self.m < self.local.shape[0]
        copy = pltpu.make_async_copy(src, dst, self.local.at[self.m])
        self.m += 1
        copy.start()
        return copy


def greet(peers):
    barrier = pltpu.get_barrier_semaphore()
    for peer in peers:
        pl.semaphore_signal(barrier, inc=1, device_id=peer, device_id_type=MESH)
    pl.semaphore_wait(barrier, len(peers))


def xy_peers(p):
    return [p.at_x(k) for k in (1, 2, 3)] + [p.at_y(k) for k in (1, 2, 3)]


def z_peers(p):
    return [p.at_z(k) for k in (1, 2, 3)] + [p.sibling()]


class GatherXY:
    def __init__(self, net, p, own, slot):
        self.net, self.p, self.slot = net, p, slot
        self.kept = [net.copy(own(h), slot(h, p.y, p.x)) for h in (0, 1)]
        self.first, self.rest = {}, []
        for k in (1, 2, 3):
            for h in (0, 1):
                here = slot(h, p.y, p.x)
                along = net.remote(own(h), here, p.at_x(k) if h == 0 else p.at_y(k))
                self.first[h, k] = along
        for k in (1, 2, 3):
            for h in (0, 1):
                here = slot(h, p.y, p.x)
                self.rest.append(net.remote(own(h), here, p.at_y(k) if h == 0 else p.at_x(k)))

    def forward(self):
        net, p = self.net, self.p
        for k in (1, 3, 2):
            for h in (0, 1):
                self.first[h, k].wait_recv()
                if h == 0:
                    block = self.slot(0, p.y, mod(p.x - k, 4))
                else:
                    block = self.slot(1, mod(p.y - k, 4), p.x)
                for m in (1, 2, 3):
                    self.rest.append(net.remote(block, block, p.at_y(m) if h == 0 else p.at_x(m)))

    def end(self):
        for copy in self.first.values():
            copy.wait_send()
        for copy in self.rest:
            copy.wait()
        for copy in self.kept:
            copy.wait()


class Exchange:
    def __init__(self, net, p, src, slot):
        self.kept = net.copy(src(p.dp), slot(p.dp))
        self.sent = [net.remote(src(mod(p.dp + k, DP)), slot(p.dp), p.at_dp(k)) for k in range(1, DP)]

    def end(self):
        for copy in self.sent:
            copy.wait()
        self.kept.wait()


def near_peers(p):
    return [p.at_x(1), p.at_x(3), p.at_y(1), p.at_y(3)]


def near_z(p):
    return [p.at_z(1), p.at_z(3), p.sibling()]


class RingXY:
    def __init__(self, net, p, own, slot, part):
        self.net, self.p, self.part = net, p, part
        self.spot = lambda h, a, b: slot(h, b, a) if h == 0 else slot(h, a, b)
        self.me = [(p.x, p.y), (p.y, p.x)]
        self.first = [p.at_x, p.at_y]
        self.second = [p.at_y, p.at_x]
        self.kept = [net.copy(own(h), self.spot(h, *self.me[h])) for h in (0, 1)]
        self.near, self.far, self.side, self.last = {}, {}, {}, []
        for k in (1, 3):
            for h in (0, 1):
                here = self.spot(h, *self.me[h])
                self.near[h, k] = net.remote(own(h), here, self.first[h](k))
        for k in (1, 3):
            for h in (0, 1):
                here = self.spot(h, *self.me[h])
                self.side[h, 0, k] = net.remote(own(h), here, self.second[h](k))

    def send(self, h, a, block):
        for k in (1, 3):
            self.side[h, a, k] = self.net.remote(block, block, self.second[h](k))

    def relay(self, h, a):
        mine, other = self.me[h]
        for k in (1, 3):
            self.side[h, a, k].wait_recv()
            block = self.part(self.spot(h, mod(mine + a, 4), mod(other - k, 4)), k // 2)
            self.last.append(self.net.remote(block, block, self.second[h](k)))

    def forward(self):
        for k in (1, 3):
            for h in (0, 1):
                mine, other = self.me[h]
                self.near[h, k].wait_recv()
                block = self.spot(h, mod(mine - k, 4), other)
                cut = self.part(block, k // 2)
                self.far[h, k] = self.net.remote(cut, cut, self.first[h](k))
                self.send(h, 4 - k, block)

    def middle(self):
        for h in (0, 1):
            self.relay(h, 0)
        for h in (0, 1):
            for k in (1, 3):
                self.far[h, k].wait_recv()
            mine, other = self.me[h]
            self.send(h, 2, self.spot(h, mod(mine + 2, 4), other))

    def finish(self):
        for a in (1, 3, 2):
            for h in (0, 1):
                self.relay(h, a)

    def end(self):
        for copies in (self.near, self.far, self.side):
            for copy in copies.values():
                copy.wait_send()
        for copy in self.last:
            copy.wait()
        for copy in self.kept:
            copy.wait()


class RingDP:
    def __init__(self, net, p, own, slot, part):
        self.net, self.p, self.slot, self.part = net, p, slot, part
        here = slot(p.dp)
        self.kept = net.copy(own, here)
        self.near = {k: net.remote(own, here, p.at_z(k)) for k in (1, 3)}
        self.rest = [net.remote(own, here, p.sibling())]
        self.far = {}

    def forward(self):
        net, p = self.net, self.p
        for k in (1, 3):
            self.near[k].wait_recv()
            block = self.slot(mod(p.z - k, 4) * 2 + p.core)
            cut = self.part(block, k // 2)
            self.far[k] = net.remote(cut, cut, p.at_z(k))
            self.rest.append(net.remote(block, block, p.sibling()))

    def finish(self):
        net, p = self.net, self.p
        for k in (1, 3):
            self.far[k].wait_recv()
            cut = self.part(self.slot(mod(p.z + 2, 4) * 2 + p.core), k // 2)
            self.rest.append(net.remote(cut, cut, p.sibling()))

    def end(self):
        for copy in (*self.near.values(), *self.far.values()):
            copy.wait_send()
        for copy in self.rest:
            copy.wait()
        self.kept.wait()


class RingSum:
    def __init__(self, net, peer, block, part, through, got):
        self.net, self.peer, self.block, self.part = net, peer, block, part
        self.through, self.got = through, got
        self.far, self.near = {}, []

    def start_far(self):
        for k in (1, 3):
            cut = self.part(self.block(2), k // 2)
            self.far[k] = self.net.remote(cut, self.through[k // 2], self.peer(k))

    def start_near(self, k):
        i = 1 - k // 2
        cut = self.part(self.block(k), i)
        self.near.append(self.net.remote(cut, self.part(self.got[k // 2], i), self.peer(k)))

    def start(self):
        self.start_far()
        for k in (1, 3):
            self.start_near(k)

    def forward(self):
        for k in (1, 3):
            i = k // 2
            self.far[k].wait_recv()
            cut = self.part(self.block(k), i)
            add_all(cut, [cut, self.through[i]])
            self.near.append(self.net.remote(cut, self.part(self.got[i], i), self.peer(k)))

    def end(self, out):
        for copy in self.far.values():
            copy.wait_send()
        for copy in self.near:
            copy.wait()
        add_all(out, [self.block(0), self.got[0], self.got[1]])


class SumDP:
    def __init__(self, net, p, part, cut, mine, sib, through, got, out):
        self.net, self.p, self.mine, self.sib, self.out = net, p, mine, sib, out
        self.ring = RingSum(
            net, p.at_z, lambda k: mine.at[mod(p.z + k, 4)], cut, through, got
        )
        self.loads = {}
        for k in (2, 1, 3, 0):
            z = mod(p.z + k, 4)
            swap = net.remote(part(2 * z + 1 - p.core), sib.at[z], p.sibling())
            self.loads[k] = (net.copy(part(2 * z + p.core), mine.at[z]), swap)

    def join(self, k):
        for copy in self.loads[k]:
            copy.wait()
        z = mod(self.p.z + k, 4)
        add_all(self.mine.at[z], [self.mine.at[z], self.sib.at[z]])

    def begin(self):
        self.join(2)
        self.ring.start_far()
        for k in (1, 3):
            self.join(k)
            self.ring.start_near(k)
        self.join(0)

    def forward(self):
        self.ring.forward()

    def end(self):
        self.ring.end(self.out)


class SumXY:
    def __init__(self, net, p, cut, part, first, second, piece):
        self.p, self.piece = p, piece
        self.cut = cut
        x, y = (lambda k: mod(p.x + k, 4)), (lambda k: mod(p.y + k, 4))
        self.one = [
            RingSum(net, p.at_x, lambda k: cut(0, None, x(k)), part, *first[0]),
            RingSum(net, p.at_y, lambda k: cut(1, y(k), None), part, *first[1]),
        ]
        self.two = [
            RingSum(net, p.at_y, lambda k: cut(0, y(k), p.x), part, *second[0]),
            RingSum(net, p.at_x, lambda k: cut(1, p.y, x(k)), part, *second[1]),
        ]

    def start(self):
        for ring in self.one:
            ring.start()

    def forward(self):
        for ring in self.one:
            ring.forward()

    def turn(self):
        p = self.p
        for h, own in ((0, self.cut(0, None, p.x)), (1, self.cut(1, p.y, None))):
            self.one[h].end(own)
            self.two[h].start()

    def finish(self):
        for ring in self.two:
            ring.forward()

    def end(self):
        for h in (0, 1):
            self.two[h].end(self.piece(h))


def add_all(out, terms):
    *lead, rows, lanes = out.shape
    step_rows = min(rows, max(16, (24 * 1024 // lanes) // 16 * 16))
    while rows % step_rows:
        step_rows -= 16
    steps = rows // step_rows
    count = steps
    for n in lead:
        count *= n

    def step(i, carry):
        j, r = i // steps, lax.rem(i, steps)
        index = []
        for n in reversed(lead):
            index.insert(0, lax.rem(j, n))
            j = j // n
        at = (*index, pl.ds(pl.multiple_of(r * step_rows, 16), step_rows), slice(None))
        total = terms[0][at].astype(F32)
        for term in terms[1:]:
            total = total + term[at].astype(F32)
        out[at] = total.astype(out.dtype)
        return carry

    lax.fori_loop(0, count, step, 0)


def call(body, ident, outs, out_places, remotes, locals_, scratch, *args, vmem=56):
    return pl.pallas_call(
        body,
        out_shape=outs,
        in_specs=[ANY] * len(args),
        out_specs=out_places,
        scratch_shapes=[
            *scratch,
            pltpu.SemaphoreType.DMA((remotes,)),
            pltpu.SemaphoreType.DMA((remotes,)),
            pltpu.SemaphoreType.DMA((locals_,)),
        ],
        compiler_params=pltpu.CompilerParams(
            collective_id=ident, has_side_effects=True, vmem_limit_bytes=vmem << 20
        ),
    )(*args)


def shape(*dims, dtype=BF):
    return jax.ShapeDtypeStruct(dims, dtype)


def rows_of(n):
    return lambda ref, i: ref.at[pl.ds(0, n)] if i == 0 else ref.at[pl.ds(n, ref.shape[0] - n)]


def half(ref, h, n=64):
    return ref.at[pl.ds(h * n, n)]


def first_exchange(h1, pos, wgrp, w_out_t, wpiece):
    def body(h1, pos, wgrp, w_out_t, wpiece, seq, posq, wjob, wo, wfp, send, recv, local):
        p = Place()
        net = Net(send, recv, local)
        greet(xy_peers(p) + [p.at_dp(k) for k in range(1, DP)])
        rows = RingXY(
            net,
            p,
            lambda h: half(h1, h),
            lambda h, y, x: seq.at[y * 4 + x, pl.ds(h * 64, 64)],
            rows_of(32),
        )
        spots = GatherXY(
            net, p, lambda h: half(pos, h, 8), lambda h, y, x: posq.at[y * 4 + x, pl.ds(h * 8, 8)]
        )
        job = RingDP(net, p, wgrp.at[p.ctx // 2], lambda i: wjob.at[i], rows_of(96))
        ffw = Exchange(net, p, lambda i: wpiece.at[i], lambda i: wfp.at[:, i])
        out = RingDP(net, p, w_out_t, lambda i: wo.at[i], rows_of(96))
        job.forward()
        rows.forward()
        spots.forward()
        out.forward()
        rows.middle()
        job.finish()
        out.finish()
        rows.finish()
        for part in (rows, spots, job, ffw, out):
            part.end()

    return call(
        body,
        1,
        (
            shape(CTX, BLOCK, D),
            shape(CTX, 16, BLOCK, dtype=F32),
            shape(DP, SHARD, GROUP),
            shape(DP, SHARD, D),
            shape(3, DP, 48, 128),
        ),
        [ANY] * 5,
        95,
        8,
        [],
        h1,
        pos,
        wgrp,
        w_out_t,
        wpiece,
    )


def middle_exchange(h2):
    def body(h2, h2_all, send, recv, local):
        p = Place()
        net = Net(send, recv, local)
        greet(near_z(p))
        hid = RingDP(net, p, h2, lambda i: h2_all.at[i], rows_of(64))
        hid.forward()
        hid.finish()
        hid.end()

    return call(body, 3, shape(DP, BLOCK, D), ANY, 10, 2, [], h2)


def sum_dp_scratch(rows=BLOCK, lanes=D):
    return [
        pltpu.VMEM((ZN, rows, lanes), BF),
        pltpu.VMEM((ZN, rows, lanes), BF),
        pltpu.VMEM((rows // 2, lanes), BF),
        pltpu.VMEM((rows // 2, lanes), BF),
        pltpu.VMEM((rows, lanes), BF),
        pltpu.VMEM((rows, lanes), BF),
    ]


def sum_dp(net, p, part, scratch, out):
    mine, sib, t0, t1, g0, g1 = scratch
    return SumDP(net, p, part, rows_of(mine.shape[1] // 2), mine, sib, (t0, t1), (g0, g1), out)


def ring_scratch(rows, lanes):
    return [pltpu.VMEM((3, n, rows, lanes), BF) for n in (2, 2, 4, 4)]


def ring_buffers(refs):
    return (refs[0], refs[1]), (refs[2], refs[3])


def back_exchange(dh2, dwf):
    def body(dh2, dwf, out, piece, part, *rest):
        scratch, rings, (send, recv, local) = rest[:6], rest[6:-3], rest[-3:]
        p = Place()
        net = Net(send, recv, local)
        greet(near_peers(p) + near_z(p))
        load = net.copy(dwf, part)
        hid = sum_dp(net, p, lambda i: dh2.at[i], scratch, out)

        def cut(h, y, x):
            rows = slice(None) if y is None else pl.ds(pl.multiple_of(y * 48, 16), 48)
            lanes = slice(None) if x is None else pl.ds(pl.multiple_of(x * 128, 128), 128)
            return part.at[:, pl.ds(4 * h, 4), rows, lanes]

        buffers = [ring_buffers(rings[4 * i : 4 * i + 4]) for i in range(4)]
        wts = SumXY(
            net,
            p,
            cut,
            lambda ref, i: ref.at[:, pl.ds(2 * i, 2)],
            buffers[:2],
            buffers[2:],
            lambda h: piece.at[:, pl.ds(4 * h, 4)],
        )
        load.wait()
        wts.start()
        hid.begin()
        hid.forward()
        wts.forward()
        hid.end()
        wts.turn()
        wts.finish()
        wts.end()

    return call(
        body,
        4,
        (shape(BLOCK, D, dtype=F32), shape(3, DP, 48, 128)),
        [VMEM] * 2,
        40,
        8,
        [
            pltpu.VMEM((3, DP, SHARD, FSH), BF),
            *sum_dp_scratch(),
            *ring_scratch(SHARD, 128),
            *ring_scratch(48, FSH),
            *ring_scratch(48, 128),
            *ring_scratch(48, 128),
        ],
        dh2,
        dwf,
    )


def heads_out(dat, att, da_t, piece):
    def body(dat, att, da_t, piece, heads, att_all, da_all, grads, send, recv, local):
        p = Place()
        net = Net(send, recv, local)
        greet([p.at_ctx(k) for k in range(1, CTX)] + [p.at_dp(k) for k in range(1, DP)])
        kept = net.copy(dat.at[p.ctx], heads.at[p.ctx])
        sent = [
            net.remote(dat.at[mod(p.ctx + k, CTX)], heads.at[p.ctx], p.at_ctx(k))
            for k in range(1, CTX)
        ]
        atts = RingDP(net, p, att, lambda i: att_all.at[i], rows_of(D // 2))
        das = Exchange(net, p, lambda i: da_t.at[i], lambda i: da_all.at[i])
        wts = Exchange(net, p, lambda i: piece.at[:, i], lambda i: grads.at[i])
        atts.forward()
        for copy in sent:
            copy.wait()
        kept.wait()
        atts.finish()
        for part in (atts, das, wts):
            part.end()

    return call(
        body,
        5,
        (
            shape(CTX, HD, BLOCK),
            shape(DP, D, BLOCK),
            shape(DP, SHARD, BLOCK),
            shape(DP, 3, 48, 128),
        ),
        [ANY] * 4,
        38,
        4,
        [],
        dat,
        att,
        da_t,
        piece,
    )


def grads_home(dqkv, dwj, dwo):
    def body(
        dqkv, dwj, dwo, out, pair, piece, full, away, f0, s0, w0, *rest
    ):
        scratch, (send, recv, local) = rest[:6], rest[6:]
        p = Place()
        net = Net(send, recv, local)
        group, rank = p.ctx // 2, lax.rem(p.ctx, 2)
        home = group == p.dp
        partner = (p.dp, p.ctx + 1 - 2 * rank)

        barrier = pltpu.get_barrier_semaphore()
        others = xy_peers(p) + z_peers(p)
        for peer in others:
            pl.semaphore_signal(barrier, inc=1, device_id=peer, device_id_type=MESH)
        for i in range(DP):
            for r in range(2):
                own = home & (p.dp == i) & (rank == r)

                @pl.when(jnp.logical_not(own))
                def _():
                    peer = (jnp.int32(i), 2 * p.dp + r)
                    pl.semaphore_signal(barrier, inc=1, device_id=peer, device_id_type=MESH)

        pl.semaphore_wait(barrier, CTX + len(others) - home.astype(jnp.int32))

        lanes = lambda c: pl.ds(pl.multiple_of(c * BLOCK, BLOCK), BLOCK)
        slot = p.dp * 2 + rank

        def message(k, spot):
            c = mod(p.ctx + k, CTX)
            return pltpu.make_async_remote_copy(
                src_ref=dqkv.at[:, lanes(c)],
                dst_ref=out.at[spot],
                send_sem=send.at[k],
                recv_sem=recv.at[spot],
                device_id=(group, c),
                device_id_type=MESH,
            )

        own = pltpu.make_async_copy(dqkv.at[:, lanes(p.ctx)], out.at[slot], local.at[0])
        net.m = 1

        @pl.when(home)
        def _():
            own.start()

        @pl.when(jnp.logical_not(home))
        def _():
            message(0, slot).start()

        for k in range(1, CTX):
            message(k, slot).start()
        net.n = CTX

        hid = sum_dp(net, p, lambda i: dwj.at[i], scratch, full)
        wide = [net.copy(dwo.at[:, pl.ds(pl.multiple_of(p.x * 384, 128), 384)], w0)]
        for k in (1, 3, 2):
            cut = dwo.at[:, pl.ds(pl.multiple_of(mod(p.x + k, 4) * 384, 128), 384)]
            wide.append(net.remote(cut, f0.at[k - 1], p.at_x(k)))
        hid.begin()
        for copy in wide:
            copy.wait()
        add_all(w0, [w0] + [f0.at[k] for k in range(3)])
        tall = []
        for k in (1, 3, 2):
            cut = w0.at[pl.ds(pl.multiple_of(mod(p.y + k, 4) * 48, 16), 48)]
            tall.append(net.remote(cut, s0.at[k - 1], p.at_y(k)))
        hid.forward()
        hid.end()
        theirs = full.at[pl.ds(pl.multiple_of((1 - rank) * 96, 16), 96)]
        swap = net.remote(theirs, away, partner)
        for copy in tall:
            copy.wait()
        add_all(piece, [w0.at[pl.ds(pl.multiple_of(p.y * 48, 16), 48)]] + [s0.at[k] for k in range(3)])
        swap.wait()
        add_all(pair, [full.at[pl.ds(pl.multiple_of(rank * 96, 16), 96)], away])

        for k in range(1, CTX):
            message(k, slot).wait_send()

        @pl.when(home)
        def _():
            own.wait()

        @pl.when(jnp.logical_not(home))
        def _():
            message(0, slot).wait_send()

        for spot in range(CTX):
            here = home & (slot == spot)

            @pl.when(jnp.logical_not(here))
            def _():
                message(0, spot).wait_recv()

    return call(
        body,
        6,
        (shape(CTX, 3 * HD, BLOCK), shape(96, GROUP), shape(48, 384)),
        [ANY, VMEM, VMEM],
        40,
        8,
        [
            pltpu.VMEM((SHARD, GROUP), BF),
            pltpu.VMEM((96, GROUP), BF),
            pltpu.VMEM((3, SHARD, 384), BF),
            pltpu.VMEM((3, 48, 384), BF),
            pltpu.VMEM((SHARD, 384), BF),
            *sum_dp_scratch(SHARD, GROUP),
        ],
        dqkv,
        dwj,
        dwo,
    )


def last_exchange(dh1, ypart, grads, pair, piece):
    def body(dh1, ypart, grads, pair, piece, e1, ysum, gff, gqkv, gout, *rest):
        scratch, (send, recv, local) = rest[:-3], rest[-3:]
        p = Place()
        net = Net(send, recv, local)
        greet(xy_peers(p) + z_peers(p))
        inp = sum_dp(net, p, lambda i: dh1.at[i], scratch[:6], e1)
        wts = RingXY(
            net,
            p,
            lambda h: grads.at[pl.ds(4 * h, 4)],
            lambda h, y, x: gff.at[
                pl.ds(4 * h, 4),
                :,
                pl.ds(pl.multiple_of(y * 48, 16), 48),
                pl.ds(pl.multiple_of(x * 128, 128), 128),
            ],
            rows_of(2),
        )
        qkv = RingXY(
            net,
            p,
            lambda h: half(pair, h, 48),
            lambda h, y, x: gqkv.at[y * 4 + x, pl.ds(h * 48, 48)],
            rows_of(32),
        )
        proj = GatherXY(
            net,
            p,
            lambda h: piece.at[pl.ds(32 * h, 32 - 16 * h)],
            lambda h, y, x: gout.at[
                pl.ds(pl.multiple_of(y * 48 + 32 * h, 16), 32 - 16 * h),
                pl.ds(pl.multiple_of(x * 384, 128), 384),
            ],
        )
        inp.begin()
        res = sum_dp(net, p, lambda i: ypart.at[i], scratch[6:], ysum)
        wts.forward()
        inp.forward()
        qkv.forward()
        proj.forward()
        wts.middle()
        inp.end()
        res.begin()
        qkv.middle()
        wts.finish()
        qkv.finish()
        res.forward()
        res.end()
        for part in (wts, qkv, proj):
            part.end()

    return call(
        body,
        7,
        (
            shape(BLOCK, D, dtype=F32),
            shape(BLOCK, D, dtype=F32),
            shape(DP, 3, SHARD, FSH),
            shape(CTX, 96, GROUP),
            shape(SHARD, D),
        ),
        [VMEM, VMEM, ANY, ANY, ANY],
        140,
        24,
        sum_dp_scratch() + sum_dp_scratch(),
        dh1,
        ypart,
        grads,
        pair,
        piece,
    )


CHUNK = 256
CHUNKS = LENGTH // CHUNK
SCALE = HD ** (-0.5)


def span(j):
    return max(0, j * CHUNK - WINDOW), (j + 1) * CHUNK


def score_block(k, q_t, hi, j):
    low, high = span(j)
    s = jnp.dot(k[low:high, :], q_t[:, j * CHUNK : (j + 1) * CHUNK], preferred_element_type=F32)
    s = s * SCALE
    key = low + lax.broadcasted_iota(jnp.int32, s.shape, 0)
    query = j * CHUNK + lax.broadcasted_iota(jnp.int32, s.shape, 1)
    last = hi[low:high, :]
    last = jnp.concatenate([last] * (CHUNK // 128), axis=1)
    return jnp.where((query >= key) & (query <= last), s, NEG_LARGE)


def turn(values, cosine, sine):
    a, b = values[: HD // 2], values[HD // 2 :]
    return jnp.concatenate([a * cosine - b * sine, b * cosine + a * sine], axis=0)


def attend(seq, wjob, cosine, sine, hi, wfp, dd, wgrp):
    def body(
        seq, wjob, cosine, sine, hi, wfp, dd, wgrp,
        q_t, k_t, v_t, top, total, home, wf, dd_all, wdh,
        rows, w, w_t, k, att, load, send, recv, local,
    ):
        p = Place()
        net = Net(send, recv, local)
        greet([p.at_ctx(k) for k in range(1, CTX)] + [p.at_dp(k) for k in range(1, DP)])
        rank = lax.rem(p.ctx, 2)
        loads = [pltpu.make_async_copy(wjob, w, load.at[CHUNKS])]
        for j in range(CHUNKS):
            loads.append(
                pltpu.make_async_copy(seq.at[pl.ds(2 * j, 2)], rows.at[pl.ds(2 * j, 2)], load.at[j])
            )
        for copy in loads:
            copy.start()

        def message(b):
            return pltpu.make_async_remote_copy(
                src_ref=att.at[:, pl.ds(b * BLOCK, BLOCK)],
                dst_ref=home.at[p.ctx],
                send_sem=send.at[b],
                recv_sem=recv.at[p.ctx],
                device_id=(p.dp, jnp.int32(b)),
                device_id_type=MESH,
            )

        def arrival(c):
            return pltpu.make_async_remote_copy(
                src_ref=att.at[:, pl.ds(0, BLOCK)],
                dst_ref=home.at[c],
                send_sem=send.at[c],
                recv_sem=recv.at[c],
                device_id=(p.dp, jnp.int32(c)),
                device_id_type=MESH,
            )

        def kept(b):
            return pltpu.make_async_copy(
                att.at[:, pl.ds(b * BLOCK, BLOCK)], home.at[p.ctx], local.at[0]
            )

        net.n, net.m = CTX, 1
        wts = RingXY(
            net,
            p,
            lambda h: wfp.at[:, pl.ds(4 * h, 4)],
            lambda h, y, x: wf.at[
                :,
                pl.ds(4 * h, 4),
                pl.ds(pl.multiple_of(y * 48, 16), 48),
                pl.ds(pl.multiple_of(x * 128, 128), 128),
            ],
            lambda ref, i: ref.at[:, pl.ds(2 * i, 2)],
        )
        cot = RingDP(net, p, dd, lambda i: dd_all.at[i], rows_of(64))
        grp = Exchange(net, p, lambda i: wgrp.at[i], lambda i: wdh.at[i])

        loads[0].wait()
        w_t[...] = w[...].reshape(D, GROUP).T
        w_own = jnp.concatenate(
            [w_t[pl.ds(pl.multiple_of(rank * HD, 16), HD), :], w_t[2 * HD :, :]], axis=0
        )
        for j in range(CHUNKS):
            at = slice(j * CHUNK, (j + 1) * CHUNK)
            loads[j + 1].wait()
            tokens = rows[2 * j : 2 * j + 2].reshape(CHUNK, D)
            proj = dot(w_own, tokens, ((1,), (1,)))
            cos, sin = cosine[:, at], sine[:, at]
            q_t[:, at] = turn(proj[:HD], cos, sin).astype(BF)
            key = turn(proj[HD : 2 * HD], cos, sin).astype(BF)
            k_t[:, at] = key
            k[at, :] = key.T
            v_t[:, at] = proj[2 * HD :].astype(BF)
            low, high = span(j)
            s = score_block(k, q_t, hi, j)
            m = jnp.max(s, axis=0, keepdims=True)
            e = jnp.exp(s - m)
            t = jnp.sum(e, axis=0, keepdims=True)
            prob = (e * (1.0 / t)).astype(BF)
            att[:, at] = jnp.dot(v_t[:, low:high], prob, preferred_element_type=F32).astype(BF)
            top[:, at] = m
            total[:, at] = t
            for b in (2 * j, 2 * j + 1):

                @pl.when(p.ctx == b)
                def _():
                    kept(b).start()

                @pl.when(p.ctx != b)
                def _():
                    message(b).start()

            if j == 3:
                wts.forward()
            if j == 4:
                cot.forward()
            if j == 5:
                wts.middle()
            if j == 6:
                cot.finish()
        wts.finish()
        for b in range(CTX):

            @pl.when(p.ctx == b)
            def _():
                kept(b).wait()

            @pl.when(p.ctx != b)
            def _():
                message(b).wait_send()
                arrival(b).wait_recv()

        for part in (cot, grp, wts):
            part.end()

    return pl.pallas_call(
        body,
        out_shape=(
            shape(HD, LENGTH),
            shape(HD, LENGTH),
            shape(HD, LENGTH),
            shape(1, LENGTH, dtype=F32),
            shape(1, LENGTH, dtype=F32),
            shape(CTX, HD, BLOCK),
            shape(3, DP, SHARD, FSH),
            shape(DP, BLOCK, D),
            shape(DP, SHARD, GROUP),
        ),
        in_specs=[ANY, ANY, VMEM, VMEM, VMEM, ANY, ANY, ANY],
        out_specs=[VMEM] * 5 + [ANY] * 4,
        scratch_shapes=[
            pltpu.VMEM((CTX, BLOCK, D), BF),
            pltpu.VMEM((DP, SHARD, GROUP), BF),
            pltpu.VMEM((GROUP, D), BF),
            pltpu.VMEM((LENGTH, HD), BF),
            pltpu.VMEM((HD, LENGTH), BF),
            pltpu.SemaphoreType.DMA((CHUNKS + 1,)),
            pltpu.SemaphoreType.DMA((72,)),
            pltpu.SemaphoreType.DMA((72,)),
            pltpu.SemaphoreType.DMA((8,)),
        ],
        compiler_params=pltpu.CompilerParams(
            collective_id=2, has_side_effects=True, vmem_limit_bytes=56 << 20
        ),
    )(seq, wjob, cosine, sine, hi, wfp, dd, wgrp)


def attend_back(seq, q_t, k_t, v_t, do_blocks, hi, top, total, cosine, sine):
    def body(
        seq, q_t, k_t, v_t, do_blocks, hi, top, total, cosine, sine,
        out, dwj, rows, k, v, q, do, do_t, dk, dv, wide, load,
    ):
        rank = lax.rem(lax.axis_index("ctx"), 2)
        fetch = pltpu.make_async_copy(seq, rows, load)
        fetch.start()
        k[...] = k_t[...].T
        v[...] = v_t[...].T
        q[...] = q_t[...].T
        for b in range(CTX):
            do_t[:, b * BLOCK : (b + 1) * BLOCK] = do_blocks[b]
        do[...] = do_t[...].T
        dk[...] = jnp.zeros_like(dk)
        dv[...] = jnp.zeros_like(dv)
        for j in range(CHUNKS):
            low, high = span(j)
            at = slice(j * CHUNK, (j + 1) * CHUNK)
            s = score_block(k, q_t, hi, j)
            prob = jnp.exp(s - top[:, at]) * (1.0 / total[:, at])
            dp = jnp.dot(v[low:high, :], do_t[:, at], preferred_element_type=F32)
            inner = jnp.sum(prob * dp, axis=0, keepdims=True)
            ds = (prob * (dp - inner)).astype(BF)
            dq = jnp.dot(k_t[:, low:high], ds, preferred_element_type=F32) * SCALE
            out[:HD, at] = turn(dq, cosine[:, at], -sine[:, at]).astype(BF)
            dk[low:high, :] += jnp.dot(ds, q[at, :], preferred_element_type=F32)
            dv[low:high, :] += jnp.dot(prob.astype(BF), do[at, :], preferred_element_type=F32)
        out[HD : 2 * HD, :] = turn(dk[...].T * SCALE, cosine[...], -sine[...]).astype(BF)
        out[2 * HD :, :] = dv[...].T.astype(BF)
        mine = pl.multiple_of(rank * HD, 16)
        other = pl.multiple_of((1 - rank) * HD, 16)
        wide[pl.ds(mine, HD), :] = out[:HD, :]
        wide[pl.ds(other, HD), :] = jnp.zeros((HD, LENGTH), BF)
        wide[2 * HD :, :] = out[HD:, :]
        fetch.wait()
        grad = jnp.dot(wide[...], rows[...].reshape(LENGTH, D), preferred_element_type=F32)
        dwj[...] = grad.T.astype(BF).reshape(DP, SHARD, GROUP)

    return pl.pallas_call(
        body,
        out_shape=(shape(3 * HD, LENGTH), shape(DP, SHARD, GROUP)),
        in_specs=[ANY] + [VMEM] * 9,
        out_specs=[VMEM] * 2,
        scratch_shapes=[
            pltpu.VMEM((CTX, BLOCK, D), BF),
            pltpu.VMEM((LENGTH, HD), BF),
            pltpu.VMEM((LENGTH, HD), BF),
            pltpu.VMEM((LENGTH, HD), BF),
            pltpu.VMEM((LENGTH, HD), BF),
            pltpu.VMEM((HD, LENGTH), BF),
            pltpu.VMEM((LENGTH, HD), F32),
            pltpu.VMEM((LENGTH, HD), F32),
            pltpu.VMEM((GROUP, LENGTH), BF),
            pltpu.SemaphoreType.DMA,
        ],
        compiler_params=pltpu.CompilerParams(vmem_limit_bytes=56 << 20),
        cost_estimate=pl.CostEstimate(flops=4_400_000_000, bytes_accessed=12 << 20, transcendentals=2_000_000),
    )(seq, q_t, k_t, v_t, do_blocks, hi, top, total, cosine, sine)


def finish_ff(gff, gain, w_gate, w_up):
    def body(gff, gain, w_gate, w_up, gate, up, down, dgain, total):
        f = pl.program_id(0)
        rows = gain[...]
        g, u = gff[0, 0].astype(F32), gff[0, 1].astype(F32)
        gate[...] = g * rows
        up[...] = u * rows
        down[...] = gff[0, 2].astype(F32)
        part = g * w_gate[...].astype(F32) + u * w_up[...].astype(F32)
        part = jnp.sum(part, axis=1, keepdims=True)

        @pl.when(f == 0)
        def _():
            total[...] = part

        @pl.when(f > 0)
        def _():
            total[...] += part

        dgain[...] = jnp.broadcast_to(total[...], (SHARD, 128)).T[:1]

    block = pl.BlockSpec((SHARD, FSH), lambda f: (0, f))
    column = pl.BlockSpec((SHARD, 1), lambda f: (0, 0))
    return pl.pallas_call(
        body,
        grid=(DP,),
        out_shape=(
            shape(SHARD, FF, dtype=F32),
            shape(SHARD, FF, dtype=F32),
            shape(SHARD, FF, dtype=F32),
            shape(1, SHARD, dtype=F32),
        ),
        in_specs=[pl.BlockSpec((1, 3, SHARD, FSH), lambda f: (f, 0, 0, 0)), column, block, block],
        out_specs=[block, block, block, pl.BlockSpec((1, SHARD), lambda f: (0, 0))],
        scratch_shapes=[pltpu.VMEM((SHARD, 1), F32)],
        compiler_params=pltpu.CompilerParams(vmem_limit_bytes=56 << 20),
    )(gff, gain, w_gate, w_up)


def finish_attention(gqkv, gout, gain, w_query, w_key, w_value):
    def body(gqkv, gout, gain, w_query, w_key, w_value, dq, dk, dv, do, dgain):
        rows = gain[...]
        for g in range(HK):
            block = gqkv[2 * g : 2 * g + 2].reshape(SHARD, GROUP).astype(F32)
            dq[:, g * 2 * HD : (g + 1) * 2 * HD] = block[:, : 2 * HD]
            dk[:, g * HD : (g + 1) * HD] = block[:, 2 * HD : 3 * HD]
            dv[:, g * HD : (g + 1) * HD] = block[:, 3 * HD :]
        total = jnp.zeros((SHARD, 1), F32)
        for grad, weight in ((dq, w_query), (dk, w_key), (dv, w_value)):
            total += jnp.sum(grad[...] * weight[...].astype(F32), axis=1, keepdims=True)
            grad[...] = grad[...] * rows
        dgain[...] = jnp.broadcast_to(total, (SHARD, 128)).T[:1]
        do[...] = gout[...].astype(F32)

    return pl.pallas_call(
        body,
        out_shape=(
            shape(SHARD, D, dtype=F32),
            shape(SHARD, HK * HD, dtype=F32),
            shape(SHARD, HK * HD, dtype=F32),
            shape(SHARD, D, dtype=F32),
            shape(1, SHARD, dtype=F32),
        ),
        in_specs=[VMEM] * 6,
        out_specs=[VMEM] * 5,
        compiler_params=pltpu.CompilerParams(vmem_limit_bytes=56 << 20),
    )(gqkv, gout, gain, w_query, w_key, w_value)


def dot(left, right, contract):
    return lax.dot_general(left, right, (contract, ((), ())), preferred_element_type=F32)


def on_device(
    layer_input,
    cotangent,
    attn_gain,
    w_query,
    w_key,
    w_value,
    w_out,
    mlp_gain,
    w_gate,
    w_up,
    w_down,
    doc_lengths,
    rope_pos,
    pad_lengths,
):
    ctx = lax.axis_index("ctx")
    row, col = ctx // 4, lax.rem(ctx, 4)
    rank = lax.rem(ctx, 2)
    gain_a = attn_gain.astype(F32)
    gain_m = mlp_gain.astype(F32)

    inputs = layer_input[0].astype(F32)
    inv_one = lax.rsqrt(jnp.mean(inputs * inputs, axis=-1, keepdims=True) + EPSILON)
    u1 = inputs * inv_one

    wgrp = jnp.concatenate(
        [w_query.reshape(SHARD, HK, 2 * HD), w_key.reshape(SHARD, HK, HD), w_value.reshape(SHARD, HK, HD)],
        axis=2,
    )
    wgrp = (wgrp.astype(F32) * gain_a[:, None, None]).astype(BF).transpose(1, 0, 2)
    w_out_t = w_out.T

    def wide_piece(w):
        rows = lax.dynamic_slice_in_dim(w, row * 48, 48, 0).reshape(48, DP, 4, 128)
        return lax.dynamic_slice_in_dim(rows, col, 1, 2)[:, :, 0].transpose(1, 0, 2)

    gains = lax.dynamic_slice_in_dim(gain_m, row * 48, 48, 0)[None, :, None]
    wpiece = jnp.stack(
        [
            (wide_piece(w_gate).astype(F32) * gains).astype(BF),
            (wide_piece(w_up).astype(F32) * gains).astype(BF),
            wide_piece(w_down.T),
        ],
        axis=1,
    )
    pos = jnp.broadcast_to(rope_pos.astype(F32), (16, BLOCK))

    seq, posq, wjob, wo, wfp = first_exchange(u1.astype(BF), pos, wgrp, w_out_t, wpiece)
    wo = wo.reshape(D, D)

    freq = THETA_BASE ** (-(jnp.arange(HD // 2).astype(F32) * 2.0 / HD))
    angles = freq[:, None] * posq[:, 0, :].reshape(1, LENGTH)
    cosine, sine = jnp.cos(angles), jnp.sin(angles)

    ends = jnp.cumsum(doc_lengths[0])
    token = jnp.arange(LENGTH, dtype=jnp.int32)
    seg = jnp.sum(token[:, None] >= ends[None, :], axis=-1)
    doc_end = jnp.sum(jnp.where(seg[:, None] == jnp.arange(4)[None, :], ends[None, :], 0), axis=-1)
    hi = jnp.minimum(token + WINDOW - 1, doc_end - 1)
    hi = jnp.where(token >= LENGTH - pad_lengths[0], token, hi)
    hi = jnp.broadcast_to(hi[:, None], (LENGTH, 128)).astype(jnp.int32)

    dd = cotangent[0]
    q_t, k_t, v_t, top, total, att, wf, cot, wdh = attend(
        seq, wjob, cosine, sine, hi, wfp, dd, wgrp
    )
    att = att.reshape(D, BLOCK)
    resid = inputs + dot(att, wo, ((0,), (1,)))
    inv_two = lax.rsqrt(jnp.mean(resid * resid, axis=-1, keepdims=True) + EPSILON)
    u2 = resid * inv_two
    hid = middle_exchange(u2.astype(BF)).reshape(DP * BLOCK, D)
    cot = cot.reshape(DP * BLOCK, D)
    wf = wf.reshape(3, D, FSH)
    gate = dot(hid, wf[0], ((1,), (0,)))
    up = dot(hid, wf[1], ((1,), (0,)))
    sig = jax.nn.sigmoid(gate)
    act = gate * sig
    mixed = (act * up).astype(BF)
    dmix = dot(cot, wf[2], ((1,), (0,)))
    dgate = (dmix * up * sig * (1.0 + gate * (1.0 - sig))).astype(BF)
    dup = (dmix * act).astype(BF)
    ypart = dot(mixed, wf[2], ((1,), (1,))).astype(BF).reshape(DP, BLOCK, D)
    epart = dot(dgate, wf[0], ((1,), (1,))) + dot(dup, wf[1], ((1,), (1,)))
    dwf = jnp.stack(
        [
            dot(hid, dgate, ((0,), (0,))).astype(BF),
            dot(hid, dup, ((0,), (0,))).astype(BF),
            dot(cot, mixed, ((0,), (0,))).astype(BF),
        ]
    ).reshape(3, DP, SHARD, FSH)

    e2, piece = back_exchange(epart.astype(BF).reshape(DP, BLOCK, D), dwf)
    dy = dd.astype(F32)
    dresid = dy + inv_two * (e2 - u2 * jnp.mean(e2 * u2, axis=-1, keepdims=True))
    da = dresid.astype(BF)
    dat = dot(wo, da, ((0,), (1,))).astype(BF).reshape(CTX, HD, BLOCK)
    da_t = da.T.reshape(DP, SHARD, BLOCK)

    do_blocks, att_all, da_all, grads = heads_out(dat, att, da_t, piece)
    dqkv, dwj = attend_back(seq, q_t, k_t, v_t, do_blocks, hi, top, total, cosine, sine)
    dwo = dot(da_all, att_all, ((0, 2), (0, 2))).astype(BF)

    back, pair, opiece = grads_home(dqkv, dwj, dwo)
    back = back.reshape(DP, 2, 3 * HD, BLOCK)
    both = back[:, 0, HD:].astype(F32) + back[:, 1, HD:].astype(F32)
    group = jnp.concatenate([back[:, 0, :HD], back[:, 1, :HD], both.astype(BF)], axis=1)
    dh1 = lax.dot_general(
        group.transpose(0, 2, 1).reshape(DP * BLOCK, GROUP),
        wdh.reshape(D, GROUP),
        (((1,), (1,)), ((), ())),
        preferred_element_type=F32,
    )

    e1, ysum, gff, gqkv, gout = last_exchange(
        dh1.astype(BF).reshape(DP, BLOCK, D), ypart, grads, pair, opiece
    )
    output = (resid + ysum).astype(BF)
    grad_in = dresid + inv_one * (e1 - u1 * jnp.mean(e1 * u1, axis=-1, keepdims=True))

    dwg, dwu, dwd, dgain_m = finish_ff(gff, gain_m[:, None], w_gate, w_up)
    dwq, dwk, dwv, dwo, dgain_a = finish_attention(
        gqkv, gout, gain_a[:, None], w_query, w_key, w_value
    )
    return (
        output[None],
        grad_in.astype(BF)[None],
        dgain_a[0],
        dwq,
        dwk,
        dwv,
        dwo.T,
        dgain_m[0],
        dwg,
        dwu,
        dwd.T,
    )


def solution(mesh):
    in_specs = (
        P("dp", "ctx", None),
        P("dp", "ctx", None),
        P("dp"),
        P("dp", None),
        P("dp", None),
        P("dp", None),
        P(None, "dp"),
        P("dp"),
        P("dp", None),
        P("dp", None),
        P(None, "dp"),
        P("dp", None),
        P("dp", "ctx"),
        P("dp"),
    )
    out_specs = (
        P("dp", "ctx", None),
        P("dp", "ctx", None),
        P("dp"),
        P("dp", None),
        P("dp", None),
        P("dp", None),
        P(None, "dp"),
        P("dp"),
        P("dp", None),
        P("dp", None),
        P(None, "dp"),
    )
    return jax.shard_map(
        on_device, mesh=mesh, in_specs=in_specs, out_specs=out_specs, check_vma=False
    )
```

```python
import functools

import jax
import jax.numpy as jnp
from jax import lax
from jax.experimental import pallas as pl
from jax.experimental.pallas import tpu as pltpu
from jax.sharding import PartitionSpec as P

HQ = 16
HK = 8
HD = 96
WINDOW = 1024
D = 1536
FF = 4096
BLOCK = 128
LENGTH = 2048
DP = 8
CTX = 16
ZN = 4
SHARD = D // DP
FSH = FF // DP
GROUP = 4 * HD

EPSILON = 1e-05
THETA_BASE = 100000.0
NEG_LARGE = -1e30

BF = jnp.bfloat16
F32 = jnp.float32
MESH = pl.DeviceIdType.MESH
ANY = pl.BlockSpec(memory_space=pl.ANY)
VMEM = pl.BlockSpec(memory_space=pltpu.VMEM)


def mod(a, n):
    return lax.rem(a + n, n)


class Place:
    def __init__(self):
        self.dp = lax.axis_index("dp")
        self.ctx = lax.axis_index("ctx")
        self.z, self.core = self.dp // 2, lax.rem(self.dp, 2)
        self.y, self.x = self.ctx // 4, lax.rem(self.ctx, 4)

    def at_x(self, k):
        return (self.dp, self.y * 4 + mod(self.x + k, 4))

    def at_y(self, k):
        return (self.dp, mod(self.y + k, 4) * 4 + self.x)

    def at_z(self, k):
        return (mod(self.z + k, 4) * 2 + self.core, self.ctx)

    def at_dp(self, k):
        return (mod(self.dp + k, DP), self.ctx)

    def at_ctx(self, k):
        return (self.dp, mod(self.ctx + k, CTX))

    def sibling(self):
        return (self.z * 2 + 1 - self.core, self.ctx)


class Net:
    def __init__(self, send, recv, local):
        self.send, self.recv, self.local = send, recv, local
        self.n, self.m = 0, 0

    def remote(self, src, dst, peer):
        assert self.n < self.send.shape[0]
        copy = pltpu.make_async_remote_copy(
            src_ref=src,
            dst_ref=dst,
            send_sem=self.send.at[self.n],
            recv_sem=self.recv.at[self.n],
            device_id=peer,
            device_id_type=MESH,
        )
        self.n += 1
        copy.start()
        return copy

    def copy(self, src, dst):
        assert self.m < self.local.shape[0]
        copy = pltpu.make_async_copy(src, dst, self.local.at[self.m])
        self.m += 1
        copy.start()
        return copy


def greet(peers):
    barrier = pltpu.get_barrier_semaphore()
    for peer in peers:
        pl.semaphore_signal(barrier, inc=1, device_id=peer, device_id_type=MESH)
    pl.semaphore_wait(barrier, len(peers))


def xy_peers(p):
    return [p.at_x(k) for k in (1, 2, 3)] + [p.at_y(k) for k in (1, 2, 3)]


def z_peers(p):
    return [p.at_z(k) for k in (1, 2, 3)] + [p.sibling()]


class GatherXY:
    def __init__(self, net, p, own, slot):
        self.net, self.p, self.slot = net, p, slot
        self.kept = [net.copy(own(h), slot(h, p.y, p.x)) for h in (0, 1)]
        self.first, self.rest = {}, []
        for k in (1, 2, 3):
            for h in (0, 1):
                here = slot(h, p.y, p.x)
                along = net.remote(own(h), here, p.at_x(k) if h == 0 else p.at_y(k))
                self.first[h, k] = along
        for k in (1, 2, 3):
            for h in (0, 1):
                here = slot(h, p.y, p.x)
                self.rest.append(net.remote(own(h), here, p.at_y(k) if h == 0 else p.at_x(k)))

    def forward(self):
        net, p = self.net, self.p
        for k in (1, 3, 2):
            for h in (0, 1):
                self.first[h, k].wait_recv()
                if h == 0:
                    block = self.slot(0, p.y, mod(p.x - k, 4))
                else:
                    block = self.slot(1, mod(p.y - k, 4), p.x)
                for m in (1, 2, 3):
                    self.rest.append(net.remote(block, block, p.at_y(m) if h == 0 else p.at_x(m)))

    def end(self):
        for copy in self.first.values():
            copy.wait_send()
        for copy in self.rest:
            copy.wait()
        for copy in self.kept:
            copy.wait()


class Exchange:
    def __init__(self, net, p, src, slot):
        self.kept = net.copy(src(p.dp), slot(p.dp))
        self.sent = [net.remote(src(mod(p.dp + k, DP)), slot(p.dp), p.at_dp(k)) for k in range(1, DP)]

    def end(self):
        for copy in self.sent:
            copy.wait()
        self.kept.wait()


def near_peers(p):
    return [p.at_x(1), p.at_x(3), p.at_y(1), p.at_y(3)]


def near_z(p):
    return [p.at_z(1), p.at_z(3), p.sibling()]


class RingXY:
    def __init__(self, net, p, own, slot, part):
        self.net, self.p, self.part = net, p, part
        self.spot = lambda h, a, b: slot(h, b, a) if h == 0 else slot(h, a, b)
        self.me = [(p.x, p.y), (p.y, p.x)]
        self.first = [p.at_x, p.at_y]
        self.second = [p.at_y, p.at_x]
        self.kept = [net.copy(own(h), self.spot(h, *self.me[h])) for h in (0, 1)]
        self.near, self.far, self.side, self.last = {}, {}, {}, []
        for k in (1, 3):
            for h in (0, 1):
                here = self.spot(h, *self.me[h])
                self.near[h, k] = net.remote(own(h), here, self.first[h](k))
        for k in (1, 3):
            for h in (0, 1):
                here = self.spot(h, *self.me[h])
                self.side[h, 0, k] = net.remote(own(h), here, self.second[h](k))

    def send(self, h, a, block):
        for k in (1, 3):
            self.side[h, a, k] = self.net.remote(block, block, self.second[h](k))

    def relay(self, h, a):
        mine, other = self.me[h]
        for k in (1, 3):
            self.side[h, a, k].wait_recv()
            block = self.part(self.spot(h, mod(mine + a, 4), mod(other - k, 4)), k // 2)
            self.last.append(self.net.remote(block, block, self.second[h](k)))

    def forward(self):
        for k in (1, 3):
            for h in (0, 1):
                mine, other = self.me[h]
                self.near[h, k].wait_recv()
                block = self.spot(h, mod(mine - k, 4), other)
                cut = self.part(block, k // 2)
                self.far[h, k] = self.net.remote(cut, cut, self.first[h](k))
                self.send(h, 4 - k, block)

    def middle(self):
        for h in (0, 1):
            self.relay(h, 0)
        for h in (0, 1):
            for k in (1, 3):
                self.far[h, k].wait_recv()
            mine, other = self.me[h]
            self.send(h, 2, self.spot(h, mod(mine + 2, 4), other))

    def finish(self):
        for a in (1, 3, 2):
            for h in (0, 1):
                self.relay(h, a)

    def end(self):
        for copies in (self.near, self.far, self.side):
            for copy in copies.values():
                copy.wait_send()
        for copy in self.last:
            copy.wait()
        for copy in self.kept:
            copy.wait()


class RingDP:
    def __init__(self, net, p, own, slot, part):
        self.net, self.p, self.slot, self.part = net, p, slot, part
        here = slot(p.dp)
        self.kept = [] if own is None else [net.copy(own, here)]
        own = here if own is None else own
        self.near = {k: net.remote(own, here, p.at_z(k)) for k in (1, 3)}
        self.swap = {0: [net.remote(own, here, p.sibling())]}
        self.far = {}

    def forward(self, *ks):
        net, p = self.net, self.p
        for k in ks or (1, 3):
            self.near[k].wait_recv()
            block = self.slot(mod(p.z - k, 4) * 2 + p.core)
            cut = self.part(block, k // 2)
            self.far[k] = net.remote(cut, cut, p.at_z(k))
            self.swap[k] = [net.remote(block, block, p.sibling())]

    def finish(self):
        net, p = self.net, self.p
        self.swap[2] = []
        for k in (1, 3):
            self.far[k].wait_recv()
            cut = self.part(self.slot(mod(p.z + 2, 4) * 2 + p.core), k // 2)
            self.swap[2].append(net.remote(cut, cut, p.sibling()))

    def arrive(self, k):
        for copy in self.swap[k]:
            copy.wait_recv()

    def end(self, arrived=False):
        for copy in (*self.near.values(), *self.far.values()):
            copy.wait_send()
        for copies in self.swap.values():
            for copy in copies:
                copy.wait_send() if arrived else copy.wait()
        for copy in self.kept:
            copy.wait()


class RingSum:
    def __init__(self, net, peer, block, part, through, got):
        self.net, self.peer, self.block, self.part = net, peer, block, part
        self.through, self.got = through, got
        self.far, self.near = {}, []

    def start_far(self):
        for k in (1, 3):
            cut = self.part(self.block(2), k // 2)
            self.far[k] = self.net.remote(cut, self.through[k // 2], self.peer(k))

    def start_near(self, k):
        i = 1 - k // 2
        cut = self.part(self.block(k), i)
        self.near.append(self.net.remote(cut, self.part(self.got[k // 2], i), self.peer(k)))

    def start(self):
        self.start_far()
        for k in (1, 3):
            self.start_near(k)

    def forward(self):
        for k in (1, 3):
            i = k // 2
            self.far[k].wait_recv()
            cut = self.part(self.block(k), i)
            add_all(cut, [cut, self.through[i]])
            self.near.append(self.net.remote(cut, self.part(self.got[i], i), self.peer(k)))

    def end(self, out):
        for copy in self.far.values():
            copy.wait_send()
        for copy in self.near:
            copy.wait()
        add_all(out, [self.block(0), self.got[0], self.got[1]])


class SumDP:
    def __init__(self, net, p, part, cut, mine, sib, through, got, out, load=True):
        self.net, self.p, self.part, self.mine, self.sib, self.out = net, p, part, mine, sib, out
        self.ring = RingSum(net, p.at_z, lambda k: mine(mod(p.z + k, 4)), cut, through, got)
        self.load, self.copies = load, {}

    def swap(self, k):
        net, p = self.net, self.p
        z = mod(p.z + k, 4)
        self.copies[k] = [net.remote(self.part(2 * z + 1 - p.core), self.sib.at[z], p.sibling())]
        if self.load:
            self.copies[k].append(net.copy(self.part(2 * z + p.core), self.mine(z)))

    def join(self, k):
        for copy in self.copies[k]:
            copy.wait()
        z = mod(self.p.z + k, 4)
        add_all(self.mine(z), [self.mine(z), self.sib.at[z]])

    def begin(self):
        for k in (2, 1, 3, 0):
            self.swap(k)
        self.join(2)
        self.ring.start_far()
        for k in (1, 3):
            self.join(k)
            self.ring.start_near(k)
        self.join(0)

    def forward(self):
        self.ring.forward()

    def end(self):
        self.ring.end(self.out)


class SumXY:
    def __init__(self, net, p, cut, part, first, second, piece):
        self.p, self.piece = p, piece
        self.cut = cut
        x, y = (lambda k: mod(p.x + k, 4)), (lambda k: mod(p.y + k, 4))
        self.one = [
            RingSum(net, p.at_x, lambda k: cut(0, None, x(k)), part, *first[0]),
            RingSum(net, p.at_y, lambda k: cut(1, y(k), None), part, *first[1]),
        ]
        self.two = [
            RingSum(net, p.at_y, lambda k: cut(0, y(k), p.x), part, *second[0]),
            RingSum(net, p.at_x, lambda k: cut(1, p.y, x(k)), part, *second[1]),
        ]

    def start(self):
        for ring in self.one:
            ring.start()

    def forward(self):
        for ring in self.one:
            ring.forward()

    def turn(self):
        p = self.p
        for h, own in ((0, self.cut(0, None, p.x)), (1, self.cut(1, p.y, None))):
            self.one[h].end(own)
            self.two[h].start()

    def finish(self):
        for ring in self.two:
            ring.forward()

    def end(self):
        for h in (0, 1):
            self.two[h].end(self.piece(h))


def add_all(out, terms):
    *lead, rows, lanes = out.shape
    step_rows = min(rows, max(16, (24 * 1024 // lanes) // 16 * 16))
    while rows % step_rows:
        step_rows -= 16
    steps = rows // step_rows
    count = steps
    for n in lead:
        count *= n

    def step(i, carry):
        j, r = i // steps, lax.rem(i, steps)
        index = []
        for n in reversed(lead):
            index.insert(0, lax.rem(j, n))
            j = j // n
        at = (*index, pl.ds(pl.multiple_of(r * step_rows, 16), step_rows), slice(None))
        total = terms[0][at].astype(F32)
        for term in terms[1:]:
            total = total + term[at].astype(F32)
        out[at] = total.astype(out.dtype)
        return carry

    lax.fori_loop(0, count, step, 0)


def call(body, ident, outs, out_places, remotes, locals_, scratch, *args, vmem=56):
    return pl.pallas_call(
        body,
        out_shape=outs,
        in_specs=[ANY] * len(args),
        out_specs=out_places,
        scratch_shapes=[
            *scratch,
            pltpu.SemaphoreType.DMA((remotes,)),
            pltpu.SemaphoreType.DMA((remotes,)),
            pltpu.SemaphoreType.DMA((locals_,)),
        ],
        compiler_params=pltpu.CompilerParams(
            collective_id=ident, has_side_effects=True, vmem_limit_bytes=vmem << 20
        ),
    )(*args)


def shape(*dims, dtype=BF):
    return jax.ShapeDtypeStruct(dims, dtype)


def rows_of(n):
    return lambda ref, i: ref.at[pl.ds(0, n)] if i == 0 else ref.at[pl.ds(n, ref.shape[0] - n)]


def half(ref, h, n=64):
    return ref.at[pl.ds(h * n, n)]


def first_exchange(h1, pos, wgrp, w_out_t, wpiece):
    def body(h1, pos, wgrp, w_out_t, wpiece, seq, posq, wjob, wo, wfp, send, recv, local):
        p = Place()
        net = Net(send, recv, local)
        greet(xy_peers(p) + [p.at_dp(k) for k in range(1, DP)])
        rows = RingXY(
            net,
            p,
            lambda h: half(h1, h),
            lambda h, y, x: seq.at[y * 4 + x, pl.ds(h * 64, 64)],
            rows_of(32),
        )
        spots = GatherXY(
            net, p, lambda h: half(pos, h, 8), lambda h, y, x: posq.at[y * 4 + x, pl.ds(h * 8, 8)]
        )
        job = RingDP(net, p, wgrp.at[p.ctx // 2], lambda i: wjob.at[i], rows_of(96))
        ffw = Exchange(net, p, lambda i: wpiece.at[i], lambda i: wfp.at[:, i])
        out = RingDP(net, p, w_out_t, lambda i: wo.at[i], rows_of(96))
        job.forward()
        rows.forward()
        spots.forward()
        out.forward()
        rows.middle()
        job.finish()
        out.finish()
        rows.finish()
        for part in (rows, spots, job, ffw, out):
            part.end()

    return call(
        body,
        1,
        (
            shape(CTX, BLOCK, D),
            shape(CTX, 16, BLOCK, dtype=F32),
            shape(DP, SHARD, GROUP),
            shape(DP, SHARD, D),
            shape(3, DP, 48, 128),
        ),
        [ANY] * 5,
        95,
        8,
        [],
        h1,
        pos,
        wgrp,
        w_out_t,
        wpiece,
    )


def feed_forward(x, att, wo, cot, wf):
    def body(
        x, att, wo, cot, wf,
        resid, dresid, dat, da_t, ypart, dwf,
        xv, attv, wov, cotv, wfv, hid, mixed, dgate, dup, epart, e2, sib, t0, t1, g0, g1,
        send, recv, local,
    ):
        p = Place()
        net = Net(send, recv, local)
        greet(near_z(p))
        loads = [net.copy(a, b) for a, b in ((att, attv), (wo, wov), (x, xv))]
        later = [net.copy(a, b) for a, b in ((wf, wfv), (cot, cotv))]
        for copy in loads:
            copy.wait()
        rows = attv[...].reshape(D, BLOCK).T
        y1 = xv[...].astype(F32) + dot(rows, wov[...].reshape(D, D), ((1,), (1,)))
        resid[...] = y1
        inv = lax.rsqrt(jnp.mean(y1 * y1, axis=-1, keepdims=True) + EPSILON)
        hid[p.dp] = (y1 * inv).astype(BF)
        ring = RingDP(net, p, None, lambda i: hid.at[i], rows_of(64))
        for copy in later:
            copy.wait()
        w_gate, w_up, w_down = (wfv.at[i] for i in range(3))

        def part(i):
            return epart.at[i]

        total = SumDP(
            net, p, part, rows_of(64), lambda z: epart.at[2 * z + p.core], sib, (t0, t1), (g0, g1), e2,
            load=False,
        )

        def work(k):
            z = mod(p.z + k, 4)
            pair = pl.ds(2 * z, 2)
            rows = hid[pair].reshape(2 * BLOCK, D)
            wg, wu = w_gate[...].reshape(D, FSH), w_up[...].reshape(D, FSH)
            gate = jnp.dot(rows, wg, preferred_element_type=F32)
            up = jnp.dot(rows, wu, preferred_element_type=F32)
            sig = jax.nn.sigmoid(gate)
            act = gate * sig
            mixed[pair] = (act * up).astype(BF).reshape(2, BLOCK, FSH)
            wd = w_down[...].reshape(D, FSH)
            dmix = jnp.dot(cotv[pair].reshape(2 * BLOCK, D), wd, preferred_element_type=F32)
            dg = (dmix * up * sig * (1.0 + gate * (1.0 - sig))).astype(BF)
            du = (dmix * act).astype(BF)
            dgate[pair] = dg.reshape(2, BLOCK, FSH)
            dup[pair] = du.reshape(2, BLOCK, FSH)
            e = dot(dg, wg, ((1,), (1,))) + dot(du, wu, ((1,), (1,)))
            epart[pair] = e.astype(BF).reshape(2, BLOCK, D)
            total.swap(k)

        ring.arrive(0)
        work(0)
        ring.forward()
        ring.arrive(1)
        work(3)
        ring.finish()
        ring.arrive(3)
        work(1)
        total.join(3)
        total.ring.start_near(3)
        ring.arrive(2)
        work(2)
        total.join(1)
        total.ring.start_near(1)
        total.join(2)
        total.ring.start_far()

        def weights(i, left, right):
            right = right[...].reshape(DP * BLOCK, FSH)
            for c in range(4):
                block = left[:, :, c * 384 : (c + 1) * 384].reshape(DP * BLOCK, 384)
                grad = dot(block, right, ((0,), (0,)))
                dwf[i, 2 * c : 2 * c + 2] = grad.astype(BF).reshape(2, SHARD, FSH)

        weights(0, hid, dgate)
        total.join(0)
        total.forward()
        weights(1, hid, dup)
        total.end()
        y1 = resid[...]
        inv = lax.rsqrt(jnp.mean(y1 * y1, axis=-1, keepdims=True) + EPSILON)
        u2 = y1 * inv
        e = e2[...]
        d = cotv[p.dp].astype(F32) + inv * (e - u2 * jnp.mean(e * u2, axis=-1, keepdims=True))
        dresid[...] = d
        da = d.astype(BF)
        da_t[...] = da.T.reshape(DP, SHARD, BLOCK)
        back = jnp.dot(da, wov[...].reshape(D, D), preferred_element_type=F32).astype(BF)
        dat[...] = back.T.reshape(CTX, HD, BLOCK)
        weights(2, cotv, mixed)
        wd = w_down[...].reshape(D, FSH)
        for z in range(ZN):
            y = dot(mixed[2 * z : 2 * z + 2].reshape(2 * BLOCK, FSH), wd, ((1,), (1,)))
            ypart[2 * z : 2 * z + 2] = y.astype(BF).reshape(2, BLOCK, D)
        ring.end(arrived=True)

    tokens = (DP, BLOCK, D)
    hidden = (DP, BLOCK, FSH)
    return call(
        body,
        3,
        (
            shape(BLOCK, D, dtype=F32),
            shape(BLOCK, D, dtype=F32),
            shape(CTX, HD, BLOCK),
            shape(DP, SHARD, BLOCK),
            shape(*tokens),
            shape(3, DP, SHARD, FSH),
        ),
        [VMEM] * 6,
        22,
        6,
        [
            pltpu.VMEM((BLOCK, D), BF),
            pltpu.VMEM((CTX, HD, BLOCK), BF),
            pltpu.VMEM((DP, SHARD, D), BF),
            pltpu.VMEM(tokens, BF),
            pltpu.VMEM((3, DP, SHARD, FSH), BF),
            pltpu.VMEM(tokens, BF),
            pltpu.VMEM(hidden, BF),
            pltpu.VMEM(hidden, BF),
            pltpu.VMEM(hidden, BF),
            pltpu.VMEM(tokens, BF),
            pltpu.VMEM((BLOCK, D), F32),
            pltpu.VMEM((ZN, BLOCK, D), BF),
            pltpu.VMEM((BLOCK // 2, D), BF),
            pltpu.VMEM((BLOCK // 2, D), BF),
            pltpu.VMEM((BLOCK, D), BF),
            pltpu.VMEM((BLOCK, D), BF),
        ],
        x,
        att,
        wo,
        cot,
        wf,
    )


def sum_dp_scratch(rows=BLOCK, lanes=D):
    return [
        pltpu.VMEM((ZN, rows, lanes), BF),
        pltpu.VMEM((ZN, rows, lanes), BF),
        pltpu.VMEM((rows // 2, lanes), BF),
        pltpu.VMEM((rows // 2, lanes), BF),
        pltpu.VMEM((rows, lanes), BF),
        pltpu.VMEM((rows, lanes), BF),
    ]


def sum_dp(net, p, part, scratch, out):
    mine, sib, t0, t1, g0, g1 = scratch
    cut = rows_of(sib.shape[1] // 2)
    return SumDP(net, p, part, cut, lambda z: mine.at[z], sib, (t0, t1), (g0, g1), out)


def ring_scratch(rows, lanes):
    return [pltpu.VMEM((3, n, rows, lanes), BF) for n in (2, 2, 4, 4)]


def ring_buffers(refs):
    return (refs[0], refs[1]), (refs[2], refs[3])


CHUNK = 256
CHUNKS = LENGTH // CHUNK
SCALE = HD ** (-0.5)


def span(j):
    return max(0, j * CHUNK - WINDOW), (j + 1) * CHUNK


def score_block(k, q_t, hi, j):
    low, high = span(j)
    s = jnp.dot(k[low:high, :], q_t[:, j * CHUNK : (j + 1) * CHUNK], preferred_element_type=F32)
    s = s * SCALE
    key = low + lax.broadcasted_iota(jnp.int32, s.shape, 0)
    query = j * CHUNK + lax.broadcasted_iota(jnp.int32, s.shape, 1)
    last = hi[low:high, :]
    last = jnp.concatenate([last] * (CHUNK // 128), axis=1)
    return jnp.where((query >= key) & (query <= last), s, NEG_LARGE)


def turn(values, cosine, sine):
    a, b = values[: HD // 2], values[HD // 2 :]
    return jnp.concatenate([a * cosine - b * sine, b * cosine + a * sine], axis=0)


def attend(seq, wjob, cosine, sine, hi, wfp, dd, wgrp):
    def body(
        seq, wjob, cosine, sine, hi, wfp, dd, wgrp,
        q_t, k_t, v_t, top, total, home, wf, dd_all, wdh,
        rows, w, w_t, k, att, load, send, recv, local,
    ):
        p = Place()
        net = Net(send, recv, local)
        greet([p.at_ctx(k) for k in range(1, CTX)] + [p.at_dp(k) for k in range(1, DP)])
        rank = lax.rem(p.ctx, 2)
        loads = [pltpu.make_async_copy(wjob, w, load.at[CHUNKS])]
        for j in range(CHUNKS):
            loads.append(
                pltpu.make_async_copy(seq.at[pl.ds(2 * j, 2)], rows.at[pl.ds(2 * j, 2)], load.at[j])
            )
        for copy in loads:
            copy.start()

        def message(b):
            return pltpu.make_async_remote_copy(
                src_ref=att.at[:, pl.ds(b * BLOCK, BLOCK)],
                dst_ref=home.at[p.ctx],
                send_sem=send.at[b],
                recv_sem=recv.at[p.ctx],
                device_id=(p.dp, jnp.int32(b)),
                device_id_type=MESH,
            )

        def arrival(c):
            return pltpu.make_async_remote_copy(
                src_ref=att.at[:, pl.ds(0, BLOCK)],
                dst_ref=home.at[c],
                send_sem=send.at[c],
                recv_sem=recv.at[c],
                device_id=(p.dp, jnp.int32(c)),
                device_id_type=MESH,
            )

        def kept(b):
            return pltpu.make_async_copy(
                att.at[:, pl.ds(b * BLOCK, BLOCK)], home.at[p.ctx], local.at[0]
            )

        net.n, net.m = CTX, 1
        wts = RingXY(
            net,
            p,
            lambda h: wfp.at[:, pl.ds(4 * h, 4)],
            lambda h, y, x: wf.at[
                :,
                pl.ds(4 * h, 4),
                pl.ds(pl.multiple_of(y * 48, 16), 48),
                pl.ds(pl.multiple_of(x * 128, 128), 128),
            ],
            lambda ref, i: ref.at[:, pl.ds(2 * i, 2)],
        )
        cot = RingDP(net, p, dd, lambda i: dd_all.at[i], rows_of(64))
        grp = Exchange(net, p, lambda i: wgrp.at[i], lambda i: wdh.at[i])

        loads[0].wait()
        w_t[...] = w[...].reshape(D, GROUP).T
        w_own = jnp.concatenate(
            [w_t[pl.ds(pl.multiple_of(rank * HD, 16), HD), :], w_t[2 * HD :, :]], axis=0
        )
        for j in range(CHUNKS):
            at = slice(j * CHUNK, (j + 1) * CHUNK)
            loads[j + 1].wait()
            tokens = rows[2 * j : 2 * j + 2].reshape(CHUNK, D)
            proj = dot(w_own, tokens, ((1,), (1,)))
            cos, sin = cosine[:, at], sine[:, at]
            q_t[:, at] = turn(proj[:HD], cos, sin).astype(BF)
            key = turn(proj[HD : 2 * HD], cos, sin).astype(BF)
            k_t[:, at] = key
            k[at, :] = key.T
            v_t[:, at] = proj[2 * HD :].astype(BF)
            low, high = span(j)
            s = score_block(k, q_t, hi, j)
            m = jnp.max(s, axis=0, keepdims=True)
            e = jnp.exp(s - m)
            t = jnp.sum(e, axis=0, keepdims=True)
            prob = (e * (1.0 / t)).astype(BF)
            att[:, at] = jnp.dot(v_t[:, low:high], prob, preferred_element_type=F32).astype(BF)
            top[:, at] = m
            total[:, at] = t
            for b in (2 * j, 2 * j + 1):

                @pl.when(p.ctx == b)
                def _():
                    kept(b).start()

                @pl.when(p.ctx != b)
                def _():
                    message(b).start()

            if j == 3:
                wts.forward()
            if j == 4:
                cot.forward()
            if j == 5:
                wts.middle()
            if j == 6:
                cot.finish()
        wts.finish()
        for b in range(CTX):

            @pl.when(p.ctx == b)
            def _():
                kept(b).wait()

            @pl.when(p.ctx != b)
            def _():
                message(b).wait_send()
                arrival(b).wait_recv()

        for part in (cot, grp, wts):
            part.end()

    return pl.pallas_call(
        body,
        out_shape=(
            shape(HD, LENGTH),
            shape(HD, LENGTH),
            shape(HD, LENGTH),
            shape(1, LENGTH, dtype=F32),
            shape(1, LENGTH, dtype=F32),
            shape(CTX, HD, BLOCK),
            shape(3, DP, SHARD, FSH),
            shape(DP, BLOCK, D),
            shape(DP, SHARD, GROUP),
        ),
        in_specs=[ANY, ANY, VMEM, VMEM, VMEM, ANY, ANY, ANY],
        out_specs=[VMEM] * 5 + [ANY] * 4,
        scratch_shapes=[
            pltpu.VMEM((CTX, BLOCK, D), BF),
            pltpu.VMEM((DP, SHARD, GROUP), BF),
            pltpu.VMEM((GROUP, D), BF),
            pltpu.VMEM((LENGTH, HD), BF),
            pltpu.VMEM((HD, LENGTH), BF),
            pltpu.SemaphoreType.DMA((CHUNKS + 1,)),
            pltpu.SemaphoreType.DMA((72,)),
            pltpu.SemaphoreType.DMA((72,)),
            pltpu.SemaphoreType.DMA((8,)),
        ],
        compiler_params=pltpu.CompilerParams(
            collective_id=2, has_side_effects=True, vmem_limit_bytes=56 << 20
        ),
    )(seq, wjob, cosine, sine, hi, wfp, dd, wgrp)


def backward(dat, att, da_t, dwf, ypart, wdh, seq, q_t, k_t, v_t, hi, top, total, cosine, sine):
    def body(
        dat, att, da_t, dwf, ypart, wdh, seq, q_t, k_t, v_t, hi, top, total, cosine, sine,
        e1, ysum, gff, gatt,
        rows, k, v, q, do, do_t, dk, dv, out, wide, heads, att_all, da_all, dwj, full, away, comb,
        dwo, w0, f0, s0, back, wdh_v, dh1, part, piece, grads, *rest,
    ):
        rings, rest = rest[:16], rest[16:]
        j_sib, j_t0, j_t1, j_g0, j_g1, *rest = rest
        h_sib, h_t0, h_t1, h_g0, h_g1, *rest = rest
        y_scratch, (send, recv, local) = rest[:6], rest[6:]
        p = Place()
        net = Net(send, recv, local)
        group, rank = p.ctx // 2, lax.rem(p.ctx, 2)
        home = group == p.dp
        partner = (p.dp, p.ctx + 1 - 2 * rank)

        barrier = pltpu.get_barrier_semaphore()
        others = [p.at_ctx(i) for i in range(1, CTX)] + [p.at_dp(i) for i in range(1, DP)]
        for peer in others:
            pl.semaphore_signal(barrier, inc=1, device_id=peer, device_id_type=MESH)
        for i in range(DP):
            for r in range(2):

                @pl.when(jnp.logical_not(home & (p.dp == i) & (rank == r)))
                def _():
                    peer = (jnp.int32(i), 2 * p.dp + r)
                    pl.semaphore_signal(barrier, inc=1, device_id=peer, device_id_type=MESH)

        pl.semaphore_wait(barrier, CTX + len(others) - home.astype(jnp.int32))

        slot = p.dp * 2 + rank

        def message(b, spot):
            return pltpu.make_async_remote_copy(
                src_ref=out.at[:, pl.ds(b * BLOCK, BLOCK)],
                dst_ref=back.at[spot],
                send_sem=send.at[b],
                recv_sem=recv.at[spot],
                device_id=(group, jnp.int32(b)),
                device_id_type=MESH,
            )

        def own(b):
            return pltpu.make_async_copy(
                out.at[:, pl.ds(b * BLOCK, BLOCK)], back.at[slot], local.at[0]
            )

        net.n, net.m = CTX, 1

        kept = net.copy(dat.at[p.ctx], heads.at[p.ctx])
        sent = [
            net.remote(dat.at[mod(p.ctx + i, CTX)], heads.at[p.ctx], p.at_ctx(i))
            for i in range(1, CTX)
        ]
        load_part = net.copy(dwf, part)
        atts = RingDP(net, p, att, lambda i: att_all.at[i], rows_of(D // 2))
        das = Exchange(net, p, lambda i: da_t.at[i], lambda i: da_all.at[i])
        load_rows = net.copy(seq, rows)
        load_wdh = net.copy(wdh, wdh_v)

        def cut(h, y, x):
            at_rows = slice(None) if y is None else pl.ds(pl.multiple_of(y * 48, 16), 48)
            lanes = slice(None) if x is None else pl.ds(pl.multiple_of(x * 128, 128), 128)
            return part.at[:, pl.ds(4 * h, 4), at_rows, lanes]

        buffers = [ring_buffers(rings[4 * i : 4 * i + 4]) for i in range(4)]
        wts = SumXY(
            net,
            p,
            cut,
            lambda ref, i: ref.at[:, pl.ds(2 * i, 2)],
            buffers[:2],
            buffers[2:],
            lambda h: piece.at[:, pl.ds(4 * h, 4)],
        )
        res = sum_dp(net, p, lambda i: ypart.at[i], y_scratch, ysum)

        k[...] = k_t[...].T
        v[...] = v_t[...].T
        q[...] = q_t[...].T
        dk[...] = jnp.zeros_like(dk)
        dv[...] = jnp.zeros_like(dv)
        for copy in sent:
            copy.wait()
        kept.wait()
        load_part.wait()
        wts.start()
        for b in range(CTX):
            do_t[:, b * BLOCK : (b + 1) * BLOCK] = heads[b]
        do[...] = do_t[...].T

        def chunk(j):
            low, high = span(j)
            at = slice(j * CHUNK, (j + 1) * CHUNK)
            s = score_block(k, q_t, hi, j)
            prob = jnp.exp(s - top[:, at]) * (1.0 / total[:, at])
            dp = jnp.dot(v[low:high, :], do_t[:, at], preferred_element_type=F32)
            inner = jnp.sum(prob * dp, axis=0, keepdims=True)
            ds = (prob * (dp - inner)).astype(BF)
            dq = jnp.dot(k_t[:, low:high], ds, preferred_element_type=F32) * SCALE
            dk[low:high, :] += jnp.dot(ds, q[at, :], preferred_element_type=F32)
            dv[low:high, :] += jnp.dot(prob.astype(BF), do[at, :], preferred_element_type=F32)
            cos, sin = cosine[:, at], -sine[:, at]
            out[:HD, at] = turn(dq, cos, sin).astype(BF)
            out[HD : 2 * HD, at] = turn(dk[at, :].T * SCALE, cos, sin).astype(BF)
            out[2 * HD :, at] = dv[at, :].T.astype(BF)
            for b in (2 * j, 2 * j + 1):
                here = home & (p.ctx == b)

                @pl.when(here)
                def _():
                    own(b).start()

                @pl.when(jnp.logical_not(here))
                def _():
                    message(b, slot).start()

        for j in reversed(range(CHUNKS)):
            chunk(j)
            if j == 5:
                atts.forward()
            if j == 2:
                wts.forward()
                atts.finish()

        mine = pl.multiple_of(rank * HD, 16)
        other = pl.multiple_of((1 - rank) * HD, 16)
        wide[pl.ds(mine, HD), :] = out[:HD, :]
        wide[pl.ds(other, HD), :] = jnp.zeros((HD, LENGTH), BF)
        wide[2 * HD :, :] = out[HD:, :]
        load_rows.wait()
        grad = jnp.dot(wide[...], rows[...].reshape(LENGTH, D), preferred_element_type=F32)
        dwj[...] = grad.T.astype(BF).reshape(DP, SHARD, GROUP)
        proj = SumDP(
            net, p, lambda i: dwj.at[i], rows_of(96), lambda z: dwj.at[2 * z + p.core], j_sib,
            (j_t0, j_t1), (j_g0, j_g1), full, load=False,
        )
        proj.begin()
        wts.turn()

        for i in (1, 3, 2):
            atts.arrive(i)
        atts.arrive(0)
        atts.end(arrived=True)
        das.end()
        grad = dot(da_all[0], att_all[0], ((1,), (1,)))
        for i in range(1, DP):
            grad += dot(da_all[i], att_all[i], ((1,), (1,)))
        dwo[...] = grad.astype(BF)
        wide_cuts = [net.copy(dwo.at[:, pl.ds(pl.multiple_of(p.x * 384, 128), 384)], w0)]
        for i in (1, 3, 2):
            lanes = pl.ds(pl.multiple_of(mod(p.x + i, 4) * 384, 128), 384)
            wide_cuts.append(net.remote(dwo.at[:, lanes], f0.at[i - 1], p.at_x(i)))
        proj.forward()

        load_wdh.wait()
        for spot in range(CTX):

            @pl.when(jnp.logical_not(home & (slot == spot)))
            def _():
                message(0, spot).wait_recv()

        for b in range(CTX):
            here = home & (p.ctx == b)

            @pl.when(here)
            def _():
                own(b).wait()

            @pl.when(jnp.logical_not(here))
            def _():
                message(b, slot).wait_send()

        inp = SumDP(
            net, p, lambda i: dh1.at[i], rows_of(64), lambda z: dh1.at[2 * z + p.core], h_sib,
            (h_t0, h_t1), (h_g0, h_g1), e1, load=False,
        )
        for step in (2, 1, 3, 0):
            z = mod(p.z + step, 4)
            for core in (0, 1):
                i = 2 * z + core
                first, second = back[2 * i].astype(F32), back[2 * i + 1].astype(F32)
                turned = jnp.concatenate(
                    [first[:HD], second[:HD], first[HD:] + second[HD:]], axis=0
                ).T.astype(BF)
                grad = dot(turned, wdh_v[...].reshape(D, GROUP), ((1,), (1,)))
                dh1[i] = grad.astype(BF)
            inp.swap(step)
        inp.join(2)
        inp.ring.start_far()
        for step in (1, 3):
            inp.join(step)
            inp.ring.start_near(step)
        inp.join(0)

        wts.finish()
        wts.end()
        swap = Exchange(net, p, lambda i: piece.at[:, i], lambda i: grads.at[i])
        proj.end()
        theirs = full.at[pl.ds(pl.multiple_of((1 - rank) * 96, 16), 96)]
        trade = net.remote(theirs, away, partner)
        for copy in wide_cuts:
            copy.wait()
        add_all(w0, [w0] + [f0.at[i] for i in range(3)])
        tall = []
        for i in (1, 3, 2):
            at = pl.ds(pl.multiple_of(mod(p.y + i, 4) * 48, 16), 48)
            tall.append(net.remote(w0.at[at], s0.at[i - 1], p.at_y(i)))
        swap.end()
        gather = RingXY(
            net,
            p,
            lambda h: grads.at[pl.ds(4 * h, 4)],
            lambda h, y, x: gff.at[
                pl.ds(4 * h, 4),
                :,
                pl.ds(pl.multiple_of(y * 48, 16), 48),
                pl.ds(pl.multiple_of(x * 128, 128), 128),
            ],
            rows_of(2),
        )
        trade.wait()
        add_all(
            comb.at[pl.ds(0, 96)], [full.at[pl.ds(pl.multiple_of(rank * 96, 16), 96)], away]
        )
        for copy in tall:
            copy.wait()
        at = pl.ds(pl.multiple_of(p.y * 48, 16), 48)
        add_all(comb.at[pl.ds(96, 48)], [w0.at[at]] + [s0.at[i] for i in range(3)])
        small = RingXY(
            net,
            p,
            lambda h: comb.at[pl.ds(80 * h, 80 - 16 * h)],
            lambda h, y, x: gatt.at[y * 4 + x, pl.ds(80 * h, 80 - 16 * h)],
            rows_of(48),
        )
        inp.forward()
        gather.forward()
        small.forward()
        inp.end()
        res.begin()
        gather.middle()
        small.middle()
        res.forward()
        gather.finish()
        small.finish()
        res.end()
        gather.end()
        small.end()

    heads = pltpu.VMEM((LENGTH, HD), BF)
    return pl.pallas_call(
        body,
        out_shape=(
            shape(BLOCK, D, dtype=F32),
            shape(BLOCK, D, dtype=F32),
            shape(DP, 3, SHARD, FSH),
            shape(CTX, 144, GROUP),
        ),
        in_specs=[ANY] * 7 + [VMEM] * 8,
        out_specs=[VMEM, VMEM, ANY, ANY],
        scratch_shapes=[
            pltpu.VMEM((CTX, BLOCK, D), BF),
            heads,
            heads,
            heads,
            heads,
            pltpu.VMEM((HD, LENGTH), BF),
            pltpu.VMEM((LENGTH, HD), F32),
            pltpu.VMEM((LENGTH, HD), F32),
            pltpu.VMEM((3 * HD, LENGTH), BF),
            pltpu.VMEM((GROUP, LENGTH), BF),
            pltpu.VMEM((CTX, HD, BLOCK), BF),
            pltpu.VMEM((DP, D, BLOCK), BF),
            pltpu.VMEM((DP, SHARD, BLOCK), BF),
            pltpu.VMEM((DP, SHARD, GROUP), BF),
            pltpu.VMEM((SHARD, GROUP), BF),
            pltpu.VMEM((96, GROUP), BF),
            pltpu.VMEM((144, GROUP), BF),
            pltpu.VMEM((SHARD, D), BF),
            pltpu.VMEM((SHARD, 384), BF),
            pltpu.VMEM((3, SHARD, 384), BF),
            pltpu.VMEM((3, 48, 384), BF),
            pltpu.VMEM((CTX, 3 * HD, BLOCK), BF),
            pltpu.VMEM((DP, SHARD, GROUP), BF),
            pltpu.VMEM((DP, BLOCK, D), BF),
            pltpu.VMEM((3, DP, SHARD, FSH), BF),
            pltpu.VMEM((3, DP, 48, 128), BF),
            pltpu.VMEM((DP, 3, 48, 128), BF),
            *ring_scratch(SHARD, 128),
            *ring_scratch(48, FSH),
            *ring_scratch(48, 128),
            *ring_scratch(48, 128),
            *sum_dp_scratch(SHARD, GROUP)[1:],
            *sum_dp_scratch()[1:],
            *sum_dp_scratch(),
            pltpu.SemaphoreType.DMA((200,)),
            pltpu.SemaphoreType.DMA((200,)),
            pltpu.SemaphoreType.DMA((24,)),
        ],
        compiler_params=pltpu.CompilerParams(
            collective_id=4, has_side_effects=True, vmem_limit_bytes=60 << 20
        ),
    )(dat, att, da_t, dwf, ypart, wdh, seq, q_t, k_t, v_t, hi, top, total, cosine, sine)


def finish_ff(gff, gain, w_gate, w_up):
    def body(gff, gain, w_gate, w_up, gate, up, down, dgain, total):
        f = pl.program_id(0)
        rows = gain[...]
        g, u = gff[0, 0].astype(F32), gff[0, 1].astype(F32)
        gate[...] = g * rows
        up[...] = u * rows
        down[...] = gff[0, 2].astype(F32)
        part = g * w_gate[...].astype(F32) + u * w_up[...].astype(F32)
        part = jnp.sum(part, axis=1, keepdims=True)

        @pl.when(f == 0)
        def _():
            total[...] = part

        @pl.when(f > 0)
        def _():
            total[...] += part

        dgain[...] = jnp.broadcast_to(total[...], (SHARD, 128)).T[:1]

    block = pl.BlockSpec((SHARD, FSH), lambda f: (0, f))
    column = pl.BlockSpec((SHARD, 1), lambda f: (0, 0))
    return pl.pallas_call(
        body,
        grid=(DP,),
        out_shape=(
            shape(SHARD, FF, dtype=F32),
            shape(SHARD, FF, dtype=F32),
            shape(SHARD, FF, dtype=F32),
            shape(1, SHARD, dtype=F32),
        ),
        in_specs=[pl.BlockSpec((1, 3, SHARD, FSH), lambda f: (f, 0, 0, 0)), column, block, block],
        out_specs=[block, block, block, pl.BlockSpec((1, SHARD), lambda f: (0, 0))],
        scratch_shapes=[pltpu.VMEM((SHARD, 1), F32)],
        compiler_params=pltpu.CompilerParams(vmem_limit_bytes=56 << 20),
    )(gff, gain, w_gate, w_up)


def finish_attention(gatt, gain, w_query, w_key, w_value):
    def body(gatt, gain, w_query, w_key, w_value, dq, dk, dv, do, dgain):
        rows = gain[...]
        for c in range(CTX):
            y, x = divmod(c, 4)
            do[y * 48 : (y + 1) * 48, x * 384 : (x + 1) * 384] = gatt[c, 96:].astype(F32)
        for g in range(HK):
            block = gatt[2 * g : 2 * g + 2, :96].reshape(SHARD, GROUP).astype(F32)
            dq[:, g * 2 * HD : (g + 1) * 2 * HD] = block[:, : 2 * HD]
            dk[:, g * HD : (g + 1) * HD] = block[:, 2 * HD : 3 * HD]
            dv[:, g * HD : (g + 1) * HD] = block[:, 3 * HD :]
        total = jnp.zeros((SHARD, 1), F32)
        for grad, weight in ((dq, w_query), (dk, w_key), (dv, w_value)):
            total += jnp.sum(grad[...] * weight[...].astype(F32), axis=1, keepdims=True)
            grad[...] = grad[...] * rows
        dgain[...] = jnp.broadcast_to(total, (SHARD, 128)).T[:1]

    return pl.pallas_call(
        body,
        out_shape=(
            shape(SHARD, D, dtype=F32),
            shape(SHARD, HK * HD, dtype=F32),
            shape(SHARD, HK * HD, dtype=F32),
            shape(SHARD, D, dtype=F32),
            shape(1, SHARD, dtype=F32),
        ),
        in_specs=[VMEM] * 5,
        out_specs=[VMEM] * 5,
        compiler_params=pltpu.CompilerParams(vmem_limit_bytes=56 << 20),
    )(gatt, gain, w_query, w_key, w_value)


def dot(left, right, contract):
    return lax.dot_general(left, right, (contract, ((), ())), preferred_element_type=F32)


def on_device(
    layer_input,
    cotangent,
    attn_gain,
    w_query,
    w_key,
    w_value,
    w_out,
    mlp_gain,
    w_gate,
    w_up,
    w_down,
    doc_lengths,
    rope_pos,
    pad_lengths,
):
    ctx = lax.axis_index("ctx")
    row, col = ctx // 4, lax.rem(ctx, 4)
    rank = lax.rem(ctx, 2)
    gain_a = attn_gain.astype(F32)
    gain_m = mlp_gain.astype(F32)

    inputs = layer_input[0].astype(F32)
    inv_one = lax.rsqrt(jnp.mean(inputs * inputs, axis=-1, keepdims=True) + EPSILON)
    u1 = inputs * inv_one

    wgrp = jnp.concatenate(
        [w_query.reshape(SHARD, HK, 2 * HD), w_key.reshape(SHARD, HK, HD), w_value.reshape(SHARD, HK, HD)],
        axis=2,
    )
    wgrp = (wgrp.astype(F32) * gain_a[:, None, None]).astype(BF).transpose(1, 0, 2)
    w_out_t = w_out.T

    def wide_piece(w):
        rows = lax.dynamic_slice_in_dim(w, row * 48, 48, 0).reshape(48, DP, 4, 128)
        return lax.dynamic_slice_in_dim(rows, col, 1, 2)[:, :, 0].transpose(1, 0, 2)

    gains = lax.dynamic_slice_in_dim(gain_m, row * 48, 48, 0)[None, :, None]
    wpiece = jnp.stack(
        [
            (wide_piece(w_gate).astype(F32) * gains).astype(BF),
            (wide_piece(w_up).astype(F32) * gains).astype(BF),
            wide_piece(w_down.T),
        ],
        axis=1,
    )
    pos = jnp.broadcast_to(rope_pos.astype(F32), (16, BLOCK))

    seq, posq, wjob, wo, wfp = first_exchange(u1.astype(BF), pos, wgrp, w_out_t, wpiece)

    freq = THETA_BASE ** (-(jnp.arange(HD // 2).astype(F32) * 2.0 / HD))
    angles = freq[:, None] * posq[:, 0, :].reshape(1, LENGTH)
    cosine, sine = jnp.cos(angles), jnp.sin(angles)

    ends = jnp.cumsum(doc_lengths[0])
    token = jnp.arange(LENGTH, dtype=jnp.int32)
    seg = jnp.sum(token[:, None] >= ends[None, :], axis=-1)
    doc_end = jnp.sum(jnp.where(seg[:, None] == jnp.arange(4)[None, :], ends[None, :], 0), axis=-1)
    hi = jnp.minimum(token + WINDOW - 1, doc_end - 1)
    hi = jnp.where(token >= LENGTH - pad_lengths[0], token, hi)
    hi = jnp.broadcast_to(hi[:, None], (LENGTH, 128)).astype(jnp.int32)

    dd = cotangent[0]
    q_t, k_t, v_t, top, total, att, wf, cot, wdh = attend(
        seq, wjob, cosine, sine, hi, wfp, dd, wgrp
    )
    resid, dresid, dat, da_t, ypart, dwf = feed_forward(layer_input[0], att, wo, cot, wf)
    e1, ysum, gff, gatt = backward(
        dat, att.reshape(D, BLOCK), da_t, dwf, ypart, wdh,
        seq, q_t, k_t, v_t, hi, top, total, cosine, sine,
    )
    output = (resid + ysum).astype(BF)
    grad_in = dresid + inv_one * (e1 - u1 * jnp.mean(e1 * u1, axis=-1, keepdims=True))

    dwg, dwu, dwd, dgain_m = finish_ff(gff, gain_m[:, None], w_gate, w_up)
    dwq, dwk, dwv, dwo, dgain_a = finish_attention(gatt, gain_a[:, None], w_query, w_key, w_value)
    return (
        output[None],
        grad_in.astype(BF)[None],
        dgain_a[0],
        dwq,
        dwk,
        dwv,
        dwo.T,
        dgain_m[0],
        dwg,
        dwu,
        dwd.T,
    )


def solution(mesh):
    in_specs = (
        P("dp", "ctx", None),
        P("dp", "ctx", None),
        P("dp"),
        P("dp", None),
        P("dp", None),
        P("dp", None),
        P(None, "dp"),
        P("dp"),
        P("dp", None),
        P("dp", None),
        P(None, "dp"),
        P("dp", None),
        P("dp", "ctx"),
        P("dp"),
    )
    out_specs = (
        P("dp", "ctx", None),
        P("dp", "ctx", None),
        P("dp"),
        P("dp", None),
        P("dp", None),
        P("dp", None),
        P(None, "dp"),
        P("dp"),
        P("dp", None),
        P("dp", None),
        P(None, "dp"),
    )
    return jax.shard_map(
        on_device, mesh=mesh, in_specs=in_specs, out_specs=out_specs, check_vma=False
    )
```

```python
import functools

import jax
import jax.numpy as jnp
import numpy as np
from jax import lax
from jax.experimental import pallas as pl
from jax.experimental.pallas import tpu as pltpu
from jax.sharding import PartitionSpec as P

HQ = 16
HK = 8
HD = 96
WINDOW = 1024
D = 1536
FF = 4096
BLOCK = 128
LENGTH = 2048
DP = 8
CTX = 16
ZN = 4
SHARD = D // DP
FSH = FF // DP
GROUP = 4 * HD

EPSILON = 1e-05
THETA_BASE = 100000.0
NEG_LARGE = -1e30

BF = jnp.bfloat16
F32 = jnp.float32
MESH = pl.DeviceIdType.MESH
ANY = pl.BlockSpec(memory_space=pl.ANY)
VMEM = pl.BlockSpec(memory_space=pltpu.VMEM)
SMEM = pl.BlockSpec(memory_space=pltpu.SMEM)


def mod(a, n):
    return lax.rem(a + n, n)


class Place:
    def __init__(self):
        self.dp = lax.axis_index("dp")
        self.ctx = lax.axis_index("ctx")
        self.z, self.core = self.dp // 2, lax.rem(self.dp, 2)
        self.y, self.x = self.ctx // 4, lax.rem(self.ctx, 4)

    def at_x(self, k):
        return (self.dp, self.y * 4 + mod(self.x + k, 4))

    def at_y(self, k):
        return (self.dp, mod(self.y + k, 4) * 4 + self.x)

    def at_z(self, k):
        return (mod(self.z + k, 4) * 2 + self.core, self.ctx)

    def at_dp(self, k):
        return (mod(self.dp + k, DP), self.ctx)

    def at_ctx(self, k):
        return (self.dp, mod(self.ctx + k, CTX))

    def sibling(self):
        return (self.z * 2 + 1 - self.core, self.ctx)


class Net:
    def __init__(self, send, recv, local):
        self.send, self.recv, self.local = send, recv, local
        self.n, self.m = 0, 0

    def remote(self, src, dst, peer):
        assert self.n < self.send.shape[0]
        copy = pltpu.make_async_remote_copy(
            src_ref=src,
            dst_ref=dst,
            send_sem=self.send.at[self.n],
            recv_sem=self.recv.at[self.n],
            device_id=peer,
            device_id_type=MESH,
        )
        self.n += 1
        copy.start()
        return copy

    def copy(self, src, dst):
        assert self.m < self.local.shape[0]
        copy = pltpu.make_async_copy(src, dst, self.local.at[self.m])
        self.m += 1
        copy.start()
        return copy


def greet(peers):
    barrier = pltpu.get_barrier_semaphore()
    for peer in peers:
        pl.semaphore_signal(barrier, inc=1, device_id=peer, device_id_type=MESH)
    pl.semaphore_wait(barrier, len(peers))


def xy_peers(p):
    return [p.at_x(k) for k in (1, 2, 3)] + [p.at_y(k) for k in (1, 2, 3)]


def z_peers(p):
    return [p.at_z(k) for k in (1, 2, 3)] + [p.sibling()]


class GatherXY:
    def __init__(self, net, p, own, slot):
        self.net, self.p, self.slot = net, p, slot
        if own is None:
            own, self.kept = (lambda h: slot(h, p.y, p.x)), []
        else:
            self.kept = [net.copy(own(h), slot(h, p.y, p.x)) for h in (0, 1)]
        self.first, self.rest = {}, []
        for k in (1, 2, 3):
            for h in (0, 1):
                here = slot(h, p.y, p.x)
                along = net.remote(own(h), here, p.at_x(k) if h == 0 else p.at_y(k))
                self.first[h, k] = along
        for k in (1, 2, 3):
            for h in (0, 1):
                here = slot(h, p.y, p.x)
                self.rest.append(net.remote(own(h), here, p.at_y(k) if h == 0 else p.at_x(k)))

    def forward(self):
        net, p = self.net, self.p
        for k in (1, 3, 2):
            for h in (0, 1):
                self.first[h, k].wait_recv()
                if h == 0:
                    block = self.slot(0, p.y, mod(p.x - k, 4))
                else:
                    block = self.slot(1, mod(p.y - k, 4), p.x)
                for m in (1, 2, 3):
                    self.rest.append(net.remote(block, block, p.at_y(m) if h == 0 else p.at_x(m)))

    def end(self):
        for copy in self.first.values():
            copy.wait_send()
        for copy in self.rest:
            copy.wait()
        for copy in self.kept:
            copy.wait()


class Exchange:
    def __init__(self, net, p, src, slot):
        self.kept = net.copy(src(p.dp), slot(p.dp))
        self.sent = [net.remote(src(mod(p.dp + k, DP)), slot(p.dp), p.at_dp(k)) for k in range(1, DP)]

    def end(self):
        for copy in self.sent:
            copy.wait()
        self.kept.wait()


def near_peers(p):
    return [p.at_x(1), p.at_x(3), p.at_y(1), p.at_y(3)]


def near_z(p):
    return [p.at_z(1), p.at_z(3), p.sibling()]


class RingXY:
    def __init__(self, net, p, own, slot, part):
        self.net, self.p, self.part = net, p, part
        self.spot = lambda h, a, b: slot(h, b, a) if h == 0 else slot(h, a, b)
        self.me = [(p.x, p.y), (p.y, p.x)]
        self.first = [p.at_x, p.at_y]
        self.second = [p.at_y, p.at_x]
        if own is None:
            own, self.kept = (lambda h: self.spot(h, *self.me[h])), []
        else:
            self.kept = [net.copy(own(h), self.spot(h, *self.me[h])) for h in (0, 1)]
        self.near, self.far, self.side, self.last = {}, {}, {}, []
        for k in (1, 3):
            for h in (0, 1):
                here = self.spot(h, *self.me[h])
                self.near[h, k] = net.remote(own(h), here, self.first[h](k))
        for k in (1, 3):
            for h in (0, 1):
                here = self.spot(h, *self.me[h])
                self.side[h, 0, k] = net.remote(own(h), here, self.second[h](k))

    def send(self, h, a, block):
        for k in (1, 3):
            self.side[h, a, k] = self.net.remote(block, block, self.second[h](k))

    def relay(self, h, a):
        mine, other = self.me[h]
        for k in (1, 3):
            self.side[h, a, k].wait_recv()
            block = self.part(self.spot(h, mod(mine + a, 4), mod(other - k, 4)), k // 2)
            self.last.append(self.net.remote(block, block, self.second[h](k)))

    def forward(self):
        for k in (1, 3):
            for h in (0, 1):
                mine, other = self.me[h]
                self.near[h, k].wait_recv()
                block = self.spot(h, mod(mine - k, 4), other)
                cut = self.part(block, k // 2)
                self.far[h, k] = self.net.remote(cut, cut, self.first[h](k))
                self.send(h, 4 - k, block)

    def middle(self):
        for h in (0, 1):
            self.relay(h, 0)
        for h in (0, 1):
            for k in (1, 3):
                self.far[h, k].wait_recv()
            mine, other = self.me[h]
            self.send(h, 2, self.spot(h, mod(mine + 2, 4), other))

    def finish(self):
        for a in (1, 3, 2):
            for h in (0, 1):
                self.relay(h, a)

    def arrive(self):
        for copy in self.last:
            copy.wait_recv()
        for copy in self.kept:
            copy.wait()

    def end(self):
        for copies in (self.near, self.far, self.side):
            for copy in copies.values():
                copy.wait_send()
        for copy in self.last:
            copy.wait_send()


class RingDP:
    def __init__(self, net, p, own, slot, part):
        self.net, self.p, self.slot, self.part = net, p, slot, part
        here = slot(p.dp)
        self.kept = [] if own is None else [net.copy(own, here)]
        own = here if own is None else own
        self.near = {k: net.remote(own, here, p.at_z(k)) for k in (1, 3)}
        self.swap = {0: [net.remote(own, here, p.sibling())]}
        self.far = {}

    def forward(self, *ks):
        net, p = self.net, self.p
        for k in ks or (1, 3):
            self.near[k].wait_recv()
            block = self.slot(mod(p.z - k, 4) * 2 + p.core)
            cut = self.part(block, k // 2)
            self.far[k] = net.remote(cut, cut, p.at_z(k))
            self.swap[k] = [net.remote(block, block, p.sibling())]

    def finish(self):
        net, p = self.net, self.p
        self.swap[2] = []
        for k in (1, 3):
            self.far[k].wait_recv()
            cut = self.part(self.slot(mod(p.z + 2, 4) * 2 + p.core), k // 2)
            self.swap[2].append(net.remote(cut, cut, p.sibling()))

    def arrive(self, k):
        if k == 0:
            for copy in self.kept:
                copy.wait()
            self.kept = []
        for copy in self.swap[k]:
            copy.wait_recv()

    def end(self, arrived=False):
        for copy in (*self.near.values(), *self.far.values()):
            copy.wait_send()
        for copies in self.swap.values():
            for copy in copies:
                copy.wait_send() if arrived else copy.wait()
        for copy in self.kept:
            copy.wait()


class RingSum:
    def __init__(self, net, peer, block, part, through, got):
        self.net, self.peer, self.block, self.part = net, peer, block, part
        self.through, self.got = through, got
        self.far, self.near = {}, []

    def start_far(self):
        for k in (1, 3):
            cut = self.part(self.block(2), k // 2)
            self.far[k] = self.net.remote(cut, self.through[k // 2], self.peer(k))

    def start_near(self, k):
        i = 1 - k // 2
        cut = self.part(self.block(k), i)
        self.near.append(self.net.remote(cut, self.part(self.got[k // 2], i), self.peer(k)))

    def start(self):
        self.start_far()
        for k in (1, 3):
            self.start_near(k)

    def forward(self):
        for k in (1, 3):
            i = k // 2
            self.far[k].wait_recv()
            cut = self.part(self.block(k), i)
            add_all(cut, [cut, self.through[i]])
            self.near.append(self.net.remote(cut, self.part(self.got[i], i), self.peer(k)))

    def end(self, out):
        for copy in self.far.values():
            copy.wait_send()
        for copy in self.near:
            copy.wait()
        add_all(out, [self.block(0), self.got[0], self.got[1]])


class SumDP:
    def __init__(self, net, p, part, cut, mine, sib, through, got, out, load=True):
        self.net, self.p, self.part, self.mine, self.sib, self.out = net, p, part, mine, sib, out
        self.ring = RingSum(net, p.at_z, lambda k: mine(mod(p.z + k, 4)), cut, through, got)
        self.load, self.copies = load, {}

    def swap(self, k):
        net, p = self.net, self.p
        z = mod(p.z + k, 4)
        self.copies[k] = [net.remote(self.part(2 * z + 1 - p.core), self.sib.at[z], p.sibling())]
        if self.load:
            self.copies[k].append(net.copy(self.part(2 * z + p.core), self.mine(z)))

    def join(self, k):
        for copy in self.copies[k]:
            copy.wait()
        z = mod(self.p.z + k, 4)
        add_all(self.mine(z), [self.mine(z), self.sib.at[z]])

    def begin(self):
        for k in (2, 1, 3, 0):
            self.swap(k)
        self.join(2)
        self.ring.start_far()
        for k in (1, 3):
            self.join(k)
            self.ring.start_near(k)
        self.join(0)

    def forward(self):
        self.ring.forward()

    def end(self):
        self.ring.end(self.out)


class SumXY:
    def __init__(self, net, p, cut, part, first, second, piece):
        self.p, self.piece = p, piece
        self.cut = cut
        x, y = (lambda k: mod(p.x + k, 4)), (lambda k: mod(p.y + k, 4))
        self.one = [
            RingSum(net, p.at_x, lambda k: cut(0, None, x(k)), part, *first[0]),
            RingSum(net, p.at_y, lambda k: cut(1, y(k), None), part, *first[1]),
        ]
        self.two = [
            RingSum(net, p.at_y, lambda k: cut(0, y(k), p.x), part, *second[0]),
            RingSum(net, p.at_x, lambda k: cut(1, p.y, x(k)), part, *second[1]),
        ]

    def start(self):
        for ring in self.one:
            ring.start()

    def forward(self):
        for ring in self.one:
            ring.forward()

    def turn(self):
        p = self.p
        for h, own in ((0, self.cut(0, None, p.x)), (1, self.cut(1, p.y, None))):
            self.one[h].end(own)
            self.two[h].start()

    def finish(self):
        for ring in self.two:
            ring.forward()

    def end(self):
        for h in (0, 1):
            self.two[h].end(self.piece(h))


def add_all(out, terms):
    *lead, rows, lanes = out.shape
    step_rows = min(rows, max(16, (24 * 1024 // lanes) // 16 * 16))
    while rows % step_rows:
        step_rows -= 16
    steps = rows // step_rows
    count = steps
    for n in lead:
        count *= n

    def step(i, carry):
        j, r = i // steps, lax.rem(i, steps)
        index = []
        for n in reversed(lead):
            index.insert(0, lax.rem(j, n))
            j = j // n
        at = (*index, pl.ds(pl.multiple_of(r * step_rows, 16), step_rows), slice(None))
        total = terms[0][at].astype(F32)
        for term in terms[1:]:
            total = total + term[at].astype(F32)
        out[at] = total.astype(out.dtype)
        return carry

    lax.fori_loop(0, count, step, 0)


def call(body, ident, outs, out_places, remotes, locals_, scratch, *args, vmem=56):
    return pl.pallas_call(
        body,
        out_shape=outs,
        in_specs=[ANY] * len(args),
        out_specs=out_places,
        scratch_shapes=[
            *scratch,
            pltpu.SemaphoreType.DMA((remotes,)),
            pltpu.SemaphoreType.DMA((remotes,)),
            pltpu.SemaphoreType.DMA((locals_,)),
        ],
        compiler_params=pltpu.CompilerParams(
            collective_id=ident, has_side_effects=True, vmem_limit_bytes=vmem << 20
        ),
    )(*args)


def shape(*dims, dtype=BF):
    return jax.ShapeDtypeStruct(dims, dtype)


def rows_of(n):
    return lambda ref, i: ref.at[pl.ds(0, n)] if i == 0 else ref.at[pl.ds(n, ref.shape[0] - n)]


def half(ref, h, n=64):
    return ref.at[pl.ds(h * n, n)]


def sum_dp_scratch(rows=BLOCK, lanes=D):
    return [
        pltpu.VMEM((ZN, rows, lanes), BF),
        pltpu.VMEM((ZN, rows, lanes), BF),
        pltpu.VMEM((rows // 2, lanes), BF),
        pltpu.VMEM((rows // 2, lanes), BF),
        pltpu.VMEM((rows, lanes), BF),
        pltpu.VMEM((rows, lanes), BF),
    ]


def sum_dp(net, p, part, scratch, out):
    mine, sib, t0, t1, g0, g1 = scratch
    cut = rows_of(sib.shape[1] // 2)
    return SumDP(net, p, part, cut, lambda z: mine.at[z], sib, (t0, t1), (g0, g1), out)


def ring_scratch(rows, lanes):
    return [pltpu.VMEM((3, n, rows, lanes), BF) for n in (2, 2, 4, 4)]


def ring_buffers(refs):
    return (refs[0], refs[1]), (refs[2], refs[3])


CHUNK = 256
CHUNKS = LENGTH // CHUNK
SCALE = HD ** (-0.5)


def span(j):
    return max(0, j * CHUNK - WINDOW), (j + 1) * CHUNK


def score_block(k, q_t, hi, j):
    low, high = span(j)
    s = jnp.dot(k[low:high, :], q_t[:, j * CHUNK : (j + 1) * CHUNK], preferred_element_type=F32)
    s = s * SCALE
    key = low + lax.broadcasted_iota(jnp.int32, s.shape, 0)
    query = j * CHUNK + lax.broadcasted_iota(jnp.int32, s.shape, 1)
    last = hi[low:high, :]
    last = jnp.concatenate([last] * (CHUNK // 128), axis=1)
    return jnp.where((query >= key) & (query <= last), s, NEG_LARGE)


def last_readers(lengths, pad):
    key = lax.broadcasted_iota(jnp.int32, (LENGTH, BLOCK), 0)
    end = jnp.int32(0)
    ends = []
    for i in range(4):
        end = end + lengths[0, i]
        ends.append(end)
    doc = jnp.full(key.shape, ends[3], jnp.int32)
    for end in reversed(ends[:3]):
        doc = jnp.where(key < end, end, doc)
    hi = jnp.minimum(key + (WINDOW - 1), doc - 1)
    return jnp.where(key >= LENGTH - pad[0, 0], key, hi)


def turn(values, cosine, sine):
    a, b = values[: HD // 2], values[HD // 2 :]
    return jnp.concatenate([a * cosine - b * sine, b * cosine + a * sine], axis=0)


def forward(
    x, pos, freq, gain_a, gain_m, w_query, w_key, w_value, w_out_t, w_gate, w_up, w_down_t, dd, lengths, pad
):
    def body(
        x, pos, freq, gain_a, gain_m, w_query, w_key, w_value, w_out_t, w_gate, w_up, w_down_t, dd, lengths, pad,
        seq, wdh, home_out, q_t, k_t, v_t, top, total, cosine, sine, resid, dresid, dat, da_t, ypart, dwf,
        rows, spot, w, w_t, wfp, k, att, wo, wf, cot_all, home, xv, hi, wqv, wkv, wvv, wgrp, wraw, wpiece, gain,
        hid, mixed, dgate, dup, epart, e2, sib, t0, t1, g0, g1, grad_v, send, recv, local,
    ):
        p = Place()
        net = Net(send, recv, local)
        net.m = 1
        load_x = net.copy(x, xv)
        at_rows = pl.ds(pl.multiple_of(p.y * 48, 16), 48)
        load_pieces = [
            net.copy(
                ref.at[at_rows, pl.ds(pl.multiple_of(f * FSH + p.x * 128, 128), 128)], wraw.at[f, i]
            )
            for i, ref in enumerate((w_gate, w_up, w_down_t))
            for f in range(DP)
        ]
        load_w = [net.copy(a, b) for a, b in ((w_query, wqv), (w_key, wkv), (w_value, wvv))]
        greet([p.at_ctx(i) for i in range(1, CTX)] + [p.at_dp(i) for i in range(1, DP)])
        rank = lax.rem(p.ctx, 2)

        def message(b):
            return pltpu.make_async_remote_copy(
                src_ref=att.at[:, pl.ds(b * BLOCK, BLOCK)],
                dst_ref=home.at[p.ctx],
                send_sem=send.at[b],
                recv_sem=recv.at[p.ctx],
                device_id=(p.dp, jnp.int32(b)),
                device_id_type=MESH,
            )

        def arrival(c):
            return pltpu.make_async_remote_copy(
                src_ref=att.at[:, pl.ds(0, BLOCK)],
                dst_ref=home.at[c],
                send_sem=send.at[c],
                recv_sem=recv.at[c],
                device_id=(p.dp, jnp.int32(c)),
                device_id_type=MESH,
            )

        def kept(b):
            return pltpu.make_async_copy(
                att.at[:, pl.ds(b * BLOCK, BLOCK)], home.at[p.ctx], local.at[0]
            )

        net.n = CTX
        load_x.wait()
        first = xv[...].astype(F32)
        inv = lax.rsqrt(jnp.mean(first * first, axis=-1, keepdims=True) + EPSILON)
        rows[p.ctx] = (first * inv).astype(BF)
        tokens = RingXY(
            net, p, None, lambda h, y, x: rows.at[y * 4 + x, pl.ds(h * 64, 64)], rows_of(32)
        )
        spot[p.ctx] = jnp.broadcast_to(pos[...].astype(F32), (16, BLOCK))
        spots = GatherXY(net, p, None, lambda h, y, x: spot.at[y * 4 + x, pl.ds(h * 8, 8)])
        out = RingDP(net, p, w_out_t, lambda i: wo.at[i], rows_of(96))

        gain[0] = jnp.broadcast_to(gain_a[...].astype(F32), (BLOCK, SHARD)).T
        gain[1] = jnp.broadcast_to(gain_m[...].astype(F32), (BLOCK, SHARD)).T
        for copy in load_pieces:
            copy.wait()
        scale = gain[1, pl.ds(pl.multiple_of(p.y * 48, 16), 48), :]
        for f in range(DP):
            for i in (0, 1):
                wpiece[f, i] = (wraw[f, i].astype(F32) * scale).astype(BF)
            wpiece[f, 2] = wraw[f, 2]
        ffw = Exchange(net, p, lambda i: wpiece.at[i], lambda i: wfp.at[:, i])
        for copy in load_w:
            copy.wait()
        scale = gain[0, :, :1]
        for g in range(HK):
            block = jnp.concatenate(
                [
                    wqv[:, g * 2 * HD : (g + 1) * 2 * HD],
                    wkv[:, g * HD : (g + 1) * HD],
                    wvv[:, g * HD : (g + 1) * HD],
                ],
                axis=1,
            )
            wgrp[g] = (block.astype(F32) * scale).astype(BF)
        tokens.forward()
        spots.forward()
        job = RingDP(net, p, wgrp.at[p.ctx // 2], lambda i: w.at[i], rows_of(96))
        hi[...] = last_readers(lengths, pad)
        tokens.middle()
        spots.end()
        for j in range(CHUNKS):
            at = slice(j * CHUNK, (j + 1) * CHUNK)
            angles = freq[...] * jnp.concatenate(
                [spot[2 * j, :1, :], spot[2 * j + 1, :1, :]], axis=1
            )
            cosine[:, at], sine[:, at] = jnp.cos(angles), jnp.sin(angles)
        job.forward()
        tokens.finish()
        ffw.end()
        wts = RingXY(
            net,
            p,
            lambda h: wfp.at[:, pl.ds(4 * h, 4)],
            lambda h, y, x: wf.at[
                :,
                pl.ds(4 * h, 4),
                pl.ds(pl.multiple_of(y * 48, 16), 48),
                pl.ds(pl.multiple_of(x * 128, 128), 128),
            ],
            lambda ref, i: ref.at[:, pl.ds(2 * i, 2)],
        )
        job.finish()
        out.forward()
        cot = RingDP(net, p, dd, lambda i: cot_all.at[i], rows_of(64))
        for i in (0, 1, 3, 2):
            job.arrive(i)
        job.end(arrived=True)
        w_t[...] = w[...].reshape(D, GROUP).T
        out.finish()
        tokens.arrive()
        outs = [net.copy(rows, seq)]
        grp = Exchange(net, p, lambda i: wgrp.at[i], lambda i: wdh.at[i])
        w_own = jnp.concatenate(
            [w_t[pl.ds(pl.multiple_of(rank * HD, 16), HD), :], w_t[2 * HD :, :]], axis=0
        )
        for j in range(CHUNKS):
            at = slice(j * CHUNK, (j + 1) * CHUNK)
            block = rows[2 * j : 2 * j + 2].reshape(CHUNK, D)
            cos, sin = cosine[:, at], sine[:, at]
            proj = dot(w_own, block, ((1,), (1,)))
            q_t[:, at] = turn(proj[:HD], cos, sin).astype(BF)
            key = turn(proj[HD : 2 * HD], cos, sin).astype(BF)
            k_t[:, at] = key
            k[at, :] = key.T
            v_t[:, at] = proj[2 * HD :].astype(BF)
            low, high = span(j)
            s = score_block(k, q_t, hi, j)
            m = jnp.max(s, axis=0, keepdims=True)
            e = jnp.exp(s - m)
            t = jnp.sum(e, axis=0, keepdims=True)
            prob = (e * (1.0 / t)).astype(BF)
            att[:, at] = jnp.dot(v_t[:, low:high], prob, preferred_element_type=F32).astype(BF)
            top[:, at] = m
            total[:, at] = t
            for b in (2 * j, 2 * j + 1):

                @pl.when(p.ctx == b)
                def _():
                    kept(b).start()

                @pl.when(p.ctx != b)
                def _():
                    message(b).start()

            if j == 2:
                wts.forward()
            if j == 3:
                cot.forward()
            if j == 5:
                wts.middle()
            if j == 6:
                cot.finish()
        for i in (0, 1, 3, 2):
            out.arrive(i)
        for b in range(CTX):

            @pl.when(p.ctx == b)
            def _():
                kept(b).wait()

            @pl.when(p.ctx != b)
            def _():
                message(b).wait_send()
                arrival(b).wait_recv()

        outs.append(net.copy(home, home_out))
        own = home[...].reshape(D, BLOCK).T
        y1 = xv[...].astype(F32) + dot(own, wo[...].reshape(D, D), ((1,), (1,)))
        resid[...] = y1
        inv = lax.rsqrt(jnp.mean(y1 * y1, axis=-1, keepdims=True) + EPSILON)
        hid[p.dp] = (y1 * inv).astype(BF)
        ring = RingDP(net, p, None, lambda i: hid.at[i], rows_of(64))
        wts.finish()
        for i in (0, 1, 3, 2):
            cot.arrive(i)
        w_gate, w_up, w_down = (wf.at[i] for i in range(3))
        sums = SumDP(
            net, p, lambda i: epart.at[i], rows_of(64), lambda z: epart.at[2 * z + p.core], sib,
            (t0, t1), (g0, g1), e2, load=False,
        )

        def work(k):
            z = mod(p.z + k, 4)
            pair = pl.ds(2 * z, 2)
            block = hid[pair].reshape(2 * BLOCK, D)
            wg, wu = w_gate[...].reshape(D, FSH), w_up[...].reshape(D, FSH)
            gate = jnp.dot(block, wg, preferred_element_type=F32)
            up = jnp.dot(block, wu, preferred_element_type=F32)
            sig = jax.nn.sigmoid(gate)
            act = gate * sig
            mixed[pair] = (act * up).astype(BF).reshape(2, BLOCK, FSH)
            wd = w_down[...].reshape(D, FSH)
            dmix = jnp.dot(cot_all[pair].reshape(2 * BLOCK, D), wd, preferred_element_type=F32)
            dg = (dmix * up * sig * (1.0 + gate * (1.0 - sig))).astype(BF)
            du = (dmix * act).astype(BF)
            dgate[pair] = dg.reshape(2, BLOCK, FSH)
            dup[pair] = du.reshape(2, BLOCK, FSH)
            e = dot(dg, wg, ((1,), (1,))) + dot(du, wu, ((1,), (1,)))
            epart[pair] = e.astype(BF).reshape(2, BLOCK, D)
            sums.swap(k)

        wts.arrive()
        ring.arrive(0)
        work(0)
        ring.forward()
        ring.arrive(1)
        work(3)
        ring.finish()
        ring.arrive(3)
        work(1)
        sums.join(3)
        sums.ring.start_near(3)
        ring.arrive(2)
        work(2)
        sums.join(1)
        sums.ring.start_near(1)
        sums.join(2)
        sums.ring.start_far()

        def weights(i, left, right):
            right = right[...].reshape(DP * BLOCK, FSH)
            for c in range(4):
                block = left[:, :, c * 384 : (c + 1) * 384].reshape(DP * BLOCK, 384)
                grad = dot(block, right, ((0,), (0,)))
                grad_v[i, 2 * c : 2 * c + 2] = grad.astype(BF).reshape(2, SHARD, FSH)
            outs.append(net.copy(grad_v.at[i], dwf.at[i]))

        weights(0, hid, dgate)
        sums.join(0)
        sums.forward()
        weights(1, hid, dup)
        weights(2, cot_all, mixed)
        sums.end()
        y1 = resid[...]
        inv = lax.rsqrt(jnp.mean(y1 * y1, axis=-1, keepdims=True) + EPSILON)
        u2 = y1 * inv
        e = e2[...]
        d = cot_all[p.dp].astype(F32) + inv * (e - u2 * jnp.mean(e * u2, axis=-1, keepdims=True))
        dresid[...] = d
        da = d.astype(BF)
        da_t[...] = da.T.reshape(DP, SHARD, BLOCK)
        grad = jnp.dot(da, wo[...].reshape(D, D), preferred_element_type=F32).astype(BF)
        dat[...] = grad.T.reshape(CTX, HD, BLOCK)
        wd = w_down[...].reshape(D, FSH)
        for z in range(ZN):
            y = dot(mixed[2 * z : 2 * z + 2].reshape(2 * BLOCK, FSH), wd, ((1,), (1,)))
            epart[2 * z : 2 * z + 2] = y.astype(BF).reshape(2, BLOCK, D)
        outs.append(net.copy(epart, ypart))
        for part in (out, cot, ring):
            part.end(arrived=True)
        grp.end()
        tokens.end()
        wts.end()
        for copy in outs:
            copy.wait()

    block = (DP, BLOCK, D)
    hidden = pltpu.VMEM((DP, BLOCK, FSH), BF)
    head = shape(HD, LENGTH)
    line = shape(1, LENGTH, dtype=F32)
    angle = shape(HD // 2, LENGTH, dtype=F32)
    wide = shape(BLOCK, D, dtype=F32)
    return pl.pallas_call(
        body,
        out_shape=(
            shape(CTX, BLOCK, D),
            shape(DP, SHARD, GROUP),
            shape(CTX, HD, BLOCK),
            head,
            head,
            head,
            line,
            line,
            angle,
            angle,
            wide,
            wide,
            shape(CTX, HD, BLOCK),
            shape(DP, SHARD, BLOCK),
            shape(*block),
            shape(3, DP, SHARD, FSH),
        ),
        in_specs=[ANY, VMEM, VMEM, VMEM, VMEM, *[ANY] * 8, SMEM, SMEM],
        out_specs=[ANY] * 3 + [VMEM] * 11 + [ANY] * 2,
        scratch_shapes=[
            pltpu.VMEM((CTX, BLOCK, D), BF),
            pltpu.VMEM((CTX, 16, BLOCK), F32),
            pltpu.VMEM((DP, SHARD, GROUP), BF),
            pltpu.VMEM((GROUP, D), BF),
            pltpu.VMEM((3, DP, 48, 128), BF),
            pltpu.VMEM((LENGTH, HD), BF),
            pltpu.VMEM((HD, LENGTH), BF),
            pltpu.VMEM((DP, SHARD, D), BF),
            pltpu.VMEM((3, DP, SHARD, FSH), BF),
            pltpu.VMEM(block, BF),
            pltpu.VMEM((CTX, HD, BLOCK), BF),
            pltpu.VMEM((BLOCK, D), BF),
            pltpu.VMEM((LENGTH, BLOCK), jnp.int32),
            pltpu.VMEM((SHARD, D), BF),
            pltpu.VMEM((SHARD, HK * HD), BF),
            pltpu.VMEM((SHARD, HK * HD), BF),
            pltpu.VMEM((DP, SHARD, GROUP), BF),
            pltpu.VMEM((DP, 3, 48, 128), BF),
            pltpu.VMEM((DP, 3, 48, 128), BF),
            pltpu.VMEM((2, SHARD, BLOCK), F32),
            pltpu.VMEM(block, BF),
            hidden,
            hidden,
            hidden,
            pltpu.VMEM(block, BF),
            pltpu.VMEM((BLOCK, D), F32),
            pltpu.VMEM((ZN, BLOCK, D), BF),
            pltpu.VMEM((BLOCK // 2, D), BF),
            pltpu.VMEM((BLOCK // 2, D), BF),
            pltpu.VMEM((BLOCK, D), BF),
            pltpu.VMEM((BLOCK, D), BF),
            pltpu.VMEM((3, DP, SHARD, FSH), BF),
            pltpu.SemaphoreType.DMA((196,)),
            pltpu.SemaphoreType.DMA((196,)),
            pltpu.SemaphoreType.DMA((48,)),
        ],
        compiler_params=pltpu.CompilerParams(
            collective_id=2, has_side_effects=True, vmem_limit_bytes=60 << 20
        ),
    )(
        x, pos, freq, gain_a, gain_m, w_query, w_key, w_value, w_out_t, w_gate, w_up, w_down_t, dd, lengths, pad
    )


def backward(dat, att, da_t, dwf, ypart, wdh, seq, q_t, k_t, v_t, top, total, cosine, sine, lengths, pad):
    def body(
        dat, att, da_t, dwf, ypart, wdh, seq, q_t, k_t, v_t, top, total, cosine, sine, lengths, pad,
        e1, ysum, gff, gatt,
        hi, rows, k, v, q, do, do_t, dk, dv, out, wide, heads, att_all, da_all, dwj, full, away, comb,
        dwo, w0, f0, s0, back, wdh_v, dh1, part, piece, grads, *rest,
    ):
        rings, rest = rest[:16], rest[16:]
        j_sib, j_t0, j_t1, j_g0, j_g1, *rest = rest
        h_sib, h_t0, h_t1, h_g0, h_g1, *rest = rest
        y_scratch, (send, recv, local) = rest[:6], rest[6:]
        p = Place()
        net = Net(send, recv, local)
        group, rank = p.ctx // 2, lax.rem(p.ctx, 2)
        home = group == p.dp
        partner = (p.dp, p.ctx + 1 - 2 * rank)

        barrier = pltpu.get_barrier_semaphore()
        others = [p.at_ctx(i) for i in range(1, CTX)] + [p.at_dp(i) for i in range(1, DP)]
        for peer in others:
            pl.semaphore_signal(barrier, inc=1, device_id=peer, device_id_type=MESH)
        for i in range(DP):
            for r in range(2):

                @pl.when(jnp.logical_not(home & (p.dp == i) & (rank == r)))
                def _():
                    peer = (jnp.int32(i), 2 * p.dp + r)
                    pl.semaphore_signal(barrier, inc=1, device_id=peer, device_id_type=MESH)

        pl.semaphore_wait(barrier, CTX + len(others) - home.astype(jnp.int32))

        slot = p.dp * 2 + rank

        def message(b, spot):
            return pltpu.make_async_remote_copy(
                src_ref=out.at[:, pl.ds(b * BLOCK, BLOCK)],
                dst_ref=back.at[spot],
                send_sem=send.at[b],
                recv_sem=recv.at[spot],
                device_id=(group, jnp.int32(b)),
                device_id_type=MESH,
            )

        def own(b):
            return pltpu.make_async_copy(
                out.at[:, pl.ds(b * BLOCK, BLOCK)], back.at[slot], local.at[0]
            )

        net.n, net.m = CTX, 1

        kept = net.copy(dat.at[p.ctx], heads.at[p.ctx])
        sent = [
            net.remote(dat.at[mod(p.ctx + i, CTX)], heads.at[p.ctx], p.at_ctx(i))
            for i in range(1, CTX)
        ]
        load_part = net.copy(dwf, part)
        atts = RingDP(net, p, att, lambda i: att_all.at[i], rows_of(D // 2))
        das = Exchange(net, p, lambda i: da_t.at[i], lambda i: da_all.at[i])
        load_rows = net.copy(seq, rows)
        load_wdh = net.copy(wdh, wdh_v)

        def cut(h, y, x):
            at_rows = slice(None) if y is None else pl.ds(pl.multiple_of(y * 48, 16), 48)
            lanes = slice(None) if x is None else pl.ds(pl.multiple_of(x * 128, 128), 128)
            return part.at[:, pl.ds(4 * h, 4), at_rows, lanes]

        buffers = [ring_buffers(rings[4 * i : 4 * i + 4]) for i in range(4)]
        wts = SumXY(
            net,
            p,
            cut,
            lambda ref, i: ref.at[:, pl.ds(2 * i, 2)],
            buffers[:2],
            buffers[2:],
            lambda h: piece.at[:, pl.ds(4 * h, 4)],
        )
        res = sum_dp(net, p, lambda i: ypart.at[i], y_scratch, ysum)

        hi[...] = last_readers(lengths, pad)
        k[...] = k_t[...].T
        v[...] = v_t[...].T
        q[...] = q_t[...].T
        dk[...] = jnp.zeros_like(dk)
        dv[...] = jnp.zeros_like(dv)
        load_part.wait()
        wts.start()
        res.begin()
        for copy in sent:
            copy.wait()
        kept.wait()
        for b in range(CTX):
            do_t[:, b * BLOCK : (b + 1) * BLOCK] = heads[b]
        do[...] = do_t[...].T

        def chunk(j):
            low, high = span(j)
            at = slice(j * CHUNK, (j + 1) * CHUNK)
            s = score_block(k, q_t, hi, j)
            prob = jnp.exp(s - top[:, at]) * (1.0 / total[:, at])
            dp = jnp.dot(v[low:high, :], do_t[:, at], preferred_element_type=F32)
            inner = jnp.sum(prob * dp, axis=0, keepdims=True)
            ds = (prob * (dp - inner)).astype(BF)
            dq = jnp.dot(k_t[:, low:high], ds, preferred_element_type=F32) * SCALE
            dk[low:high, :] += jnp.dot(ds, q[at, :], preferred_element_type=F32)
            dv[low:high, :] += jnp.dot(prob.astype(BF), do[at, :], preferred_element_type=F32)
            cos, sin = cosine[:, at], -sine[:, at]
            out[:HD, at] = turn(dq, cos, sin).astype(BF)
            out[HD : 2 * HD, at] = turn(dk[at, :].T * SCALE, cos, sin).astype(BF)
            out[2 * HD :, at] = dv[at, :].T.astype(BF)
            for b in (2 * j, 2 * j + 1):
                here = home & (p.ctx == b)

                @pl.when(here)
                def _():
                    own(b).start()

                @pl.when(jnp.logical_not(here))
                def _():
                    message(b, slot).start()

        for j in reversed(range(CHUNKS)):
            chunk(j)
            if j == 6:
                wts.forward()
            if j == 5:
                atts.forward()
            if j == 3:
                res.forward()
            if j == 2:
                atts.finish()
        wts.turn()

        mine = pl.multiple_of(rank * HD, 16)
        other = pl.multiple_of((1 - rank) * HD, 16)
        wide[pl.ds(mine, HD), :] = out[:HD, :]
        wide[pl.ds(other, HD), :] = jnp.zeros((HD, LENGTH), BF)
        wide[2 * HD :, :] = out[HD:, :]
        load_rows.wait()
        grad = jnp.dot(wide[...], rows[...].reshape(LENGTH, D), preferred_element_type=F32)
        dwj[...] = grad.T.astype(BF).reshape(DP, SHARD, GROUP)
        proj = SumDP(
            net, p, lambda i: dwj.at[i], rows_of(96), lambda z: dwj.at[2 * z + p.core], j_sib,
            (j_t0, j_t1), (j_g0, j_g1), full, load=False,
        )
        proj.begin()
        wts.finish()

        for i in (1, 3, 2):
            atts.arrive(i)
        atts.arrive(0)
        atts.end(arrived=True)
        das.end()
        grad = dot(da_all[0], att_all[0], ((1,), (1,)))
        for i in range(1, DP):
            grad += dot(da_all[i], att_all[i], ((1,), (1,)))
        dwo[...] = grad.astype(BF)
        wide_cuts = [net.copy(dwo.at[:, pl.ds(pl.multiple_of(p.x * 384, 128), 384)], w0)]
        for i in (1, 3, 2):
            lanes = pl.ds(pl.multiple_of(mod(p.x + i, 4) * 384, 128), 384)
            wide_cuts.append(net.remote(dwo.at[:, lanes], f0.at[i - 1], p.at_x(i)))

        wts.end()
        swap = Exchange(net, p, lambda i: piece.at[:, i], lambda i: grads.at[i])
        proj.forward()

        load_wdh.wait()
        for spot in range(CTX):

            @pl.when(jnp.logical_not(home & (slot == spot)))
            def _():
                message(0, spot).wait_recv()

        for b in range(CTX):
            here = home & (p.ctx == b)

            @pl.when(here)
            def _():
                own(b).wait()

            @pl.when(jnp.logical_not(here))
            def _():
                message(b, slot).wait_send()

        inp = SumDP(
            net, p, lambda i: dh1.at[i], rows_of(64), lambda z: dh1.at[2 * z + p.core], h_sib,
            (h_t0, h_t1), (h_g0, h_g1), e1, load=False,
        )

        def inputs(step):
            z = mod(p.z + step, 4)
            for core in (0, 1):
                i = 2 * z + core
                first, second = back[2 * i].astype(F32), back[2 * i + 1].astype(F32)
                turned = jnp.concatenate(
                    [first[:HD], second[:HD], first[HD:] + second[HD:]], axis=0
                ).T.astype(BF)
                grad = dot(turned, wdh_v[...].reshape(D, GROUP), ((1,), (1,)))
                dh1[i] = grad.astype(BF)
            inp.swap(step)

        inputs(2)
        swap.end()
        gather = RingXY(
            net,
            p,
            lambda h: grads.at[pl.ds(4 * h, 4)],
            lambda h, y, x: gff.at[
                pl.ds(4 * h, 4),
                :,
                pl.ds(pl.multiple_of(y * 48, 16), 48),
                pl.ds(pl.multiple_of(x * 128, 128), 128),
            ],
            rows_of(2),
        )
        inputs(1)
        inp.join(2)
        inp.ring.start_far()
        inputs(3)
        inp.join(1)
        inp.ring.start_near(1)
        gather.forward()
        inputs(0)
        inp.join(3)
        inp.ring.start_near(3)
        proj.end()
        theirs = full.at[pl.ds(pl.multiple_of((1 - rank) * 96, 16), 96)]
        trade = net.remote(theirs, away, partner)
        for copy in wide_cuts:
            copy.wait()
        add_all(w0, [w0] + [f0.at[i] for i in range(3)])
        tall = []
        for i in (1, 3, 2):
            at = pl.ds(pl.multiple_of(mod(p.y + i, 4) * 48, 16), 48)
            tall.append(net.remote(w0.at[at], s0.at[i - 1], p.at_y(i)))
        gather.middle()
        trade.wait()
        add_all(
            comb.at[pl.ds(0, 96)], [full.at[pl.ds(pl.multiple_of(rank * 96, 16), 96)], away]
        )
        for copy in tall:
            copy.wait()
        at = pl.ds(pl.multiple_of(p.y * 48, 16), 48)
        add_all(comb.at[pl.ds(96, 48)], [w0.at[at]] + [s0.at[i] for i in range(3)])
        small = RingXY(
            net,
            p,
            lambda h: comb.at[pl.ds(80 * h, 80 - 16 * h)],
            lambda h, y, x: gatt.at[y * 4 + x, pl.ds(80 * h, 80 - 16 * h)],
            rows_of(48),
        )
        inp.join(0)
        inp.forward()
        small.forward()
        inp.end()
        res.end()
        gather.finish()
        small.middle()
        small.finish()
        for part in (gather, small):
            part.arrive()
            part.end()

    heads = pltpu.VMEM((LENGTH, HD), BF)
    return pl.pallas_call(
        body,
        out_shape=(
            shape(BLOCK, D, dtype=F32),
            shape(BLOCK, D, dtype=F32),
            shape(DP, 3, SHARD, FSH),
            shape(CTX, 144, GROUP),
        ),
        in_specs=[ANY] * 7 + [VMEM] * 7 + [SMEM] * 2,
        out_specs=[VMEM, VMEM, ANY, ANY],
        scratch_shapes=[
            pltpu.VMEM((LENGTH, BLOCK), jnp.int32),
            pltpu.VMEM((CTX, BLOCK, D), BF),
            heads,
            heads,
            heads,
            heads,
            pltpu.VMEM((HD, LENGTH), BF),
            pltpu.VMEM((LENGTH, HD), F32),
            pltpu.VMEM((LENGTH, HD), F32),
            pltpu.VMEM((3 * HD, LENGTH), BF),
            pltpu.VMEM((GROUP, LENGTH), BF),
            pltpu.VMEM((CTX, HD, BLOCK), BF),
            pltpu.VMEM((DP, D, BLOCK), BF),
            pltpu.VMEM((DP, SHARD, BLOCK), BF),
            pltpu.VMEM((DP, SHARD, GROUP), BF),
            pltpu.VMEM((SHARD, GROUP), BF),
            pltpu.VMEM((96, GROUP), BF),
            pltpu.VMEM((144, GROUP), BF),
            pltpu.VMEM((SHARD, D), BF),
            pltpu.VMEM((SHARD, 384), BF),
            pltpu.VMEM((3, SHARD, 384), BF),
            pltpu.VMEM((3, 48, 384), BF),
            pltpu.VMEM((CTX, 3 * HD, BLOCK), BF),
            pltpu.VMEM((DP, SHARD, GROUP), BF),
            pltpu.VMEM((DP, BLOCK, D), BF),
            pltpu.VMEM((3, DP, SHARD, FSH), BF),
            pltpu.VMEM((3, DP, 48, 128), BF),
            pltpu.VMEM((DP, 3, 48, 128), BF),
            *ring_scratch(SHARD, 128),
            *ring_scratch(48, FSH),
            *ring_scratch(48, 128),
            *ring_scratch(48, 128),
            *sum_dp_scratch(SHARD, GROUP)[1:],
            *sum_dp_scratch()[1:],
            *sum_dp_scratch(),
            pltpu.SemaphoreType.DMA((200,)),
            pltpu.SemaphoreType.DMA((200,)),
            pltpu.SemaphoreType.DMA((24,)),
        ],
        compiler_params=pltpu.CompilerParams(
            collective_id=4, has_side_effects=True, vmem_limit_bytes=60 << 20
        ),
    )(dat, att, da_t, dwf, ypart, wdh, seq, q_t, k_t, v_t, top, total, cosine, sine, lengths, pad)


def finish_ff(gff, gain, w_gate, w_up):
    def body(gff, gain, w_gate, w_up, gate, up, down, dgain, total):
        f = pl.program_id(0)
        rows = jnp.broadcast_to(gain[...].astype(F32), (BLOCK, SHARD)).T[:, :1]
        g, u = gff[0, 0].astype(F32), gff[0, 1].astype(F32)
        gate[...] = g * rows
        up[...] = u * rows
        down[...] = gff[0, 2].astype(F32)
        part = g * w_gate[...].astype(F32) + u * w_up[...].astype(F32)
        part = jnp.sum(part, axis=1, keepdims=True)

        @pl.when(f == 0)
        def _():
            total[...] = part

        @pl.when(f > 0)
        def _():
            total[...] += part

        dgain[...] = jnp.broadcast_to(total[...], (SHARD, 128)).T[:1]

    block = pl.BlockSpec((SHARD, FSH), lambda f: (0, f))
    row = pl.BlockSpec((1, SHARD), lambda f: (0, 0))
    return pl.pallas_call(
        body,
        grid=(DP,),
        out_shape=(
            shape(SHARD, FF, dtype=F32),
            shape(SHARD, FF, dtype=F32),
            shape(SHARD, FF, dtype=F32),
            shape(1, SHARD, dtype=F32),
        ),
        in_specs=[pl.BlockSpec((1, 3, SHARD, FSH), lambda f: (f, 0, 0, 0)), row, block, block],
        out_specs=[block, block, block, row],
        scratch_shapes=[pltpu.VMEM((SHARD, 1), F32)],
        compiler_params=pltpu.CompilerParams(vmem_limit_bytes=56 << 20),
    )(gff, gain, w_gate, w_up)


def finish_attention(gatt, gain, w_query, w_key, w_value):
    def body(gatt, gain, w_query, w_key, w_value, dq, dk, dv, do, dgain):
        rows = jnp.broadcast_to(gain[...].astype(F32), (BLOCK, SHARD)).T[:, :1]
        for c in range(CTX):
            y, x = divmod(c, 4)
            do[y * 48 : (y + 1) * 48, x * 384 : (x + 1) * 384] = gatt[c, 96:].astype(F32)
        for g in range(HK):
            block = gatt[2 * g : 2 * g + 2, :96].reshape(SHARD, GROUP).astype(F32)
            dq[:, g * 2 * HD : (g + 1) * 2 * HD] = block[:, : 2 * HD]
            dk[:, g * HD : (g + 1) * HD] = block[:, 2 * HD : 3 * HD]
            dv[:, g * HD : (g + 1) * HD] = block[:, 3 * HD :]
        total = jnp.zeros((SHARD, 1), F32)
        for grad, weight in ((dq, w_query), (dk, w_key), (dv, w_value)):
            total += jnp.sum(grad[...] * weight[...].astype(F32), axis=1, keepdims=True)
            grad[...] = grad[...] * rows
        dgain[...] = jnp.broadcast_to(total, (SHARD, 128)).T[:1]

    return pl.pallas_call(
        body,
        out_shape=(
            shape(SHARD, D, dtype=F32),
            shape(SHARD, HK * HD, dtype=F32),
            shape(SHARD, HK * HD, dtype=F32),
            shape(SHARD, D, dtype=F32),
            shape(1, SHARD, dtype=F32),
        ),
        in_specs=[VMEM] * 5,
        out_specs=[VMEM] * 5,
        compiler_params=pltpu.CompilerParams(vmem_limit_bytes=56 << 20),
    )(gatt, gain, w_query, w_key, w_value)


def dot(left, right, contract):
    return lax.dot_general(left, right, (contract, ((), ())), preferred_element_type=F32)


def on_device(
    layer_input,
    cotangent,
    attn_gain,
    w_query,
    w_key,
    w_value,
    w_out,
    mlp_gain,
    w_gate,
    w_up,
    w_down,
    doc_lengths,
    rope_pos,
    pad_lengths,
):
    inputs = layer_input[0].astype(F32)
    inv_one = lax.rsqrt(jnp.mean(inputs * inputs, axis=-1, keepdims=True) + EPSILON)
    u1 = inputs * inv_one
    freq = np.float32(THETA_BASE) ** (-(np.arange(HD // 2, dtype=np.float32) * np.float32(2.0) / np.float32(HD)))
    pad = pad_lengths[:, None]
    (
        seq, wdh, att, q_t, k_t, v_t, top, total, cosine, sine, resid, dresid, dat, da_t, ypart, dwf,
    ) = forward(
        layer_input[0], rope_pos, jnp.asarray(freq[:, None]), attn_gain[None], mlp_gain[None],
        w_query, w_key, w_value, w_out.T, w_gate, w_up, w_down.T, cotangent[0], doc_lengths, pad,
    )
    e1, ysum, gff, gatt = backward(
        dat, att.reshape(D, BLOCK), da_t, dwf, ypart, wdh,
        seq, q_t, k_t, v_t, top, total, cosine, sine, doc_lengths, pad,
    )
    output = (resid + ysum).astype(BF)
    grad_in = dresid + inv_one * (e1 - u1 * jnp.mean(e1 * u1, axis=-1, keepdims=True))

    dwg, dwu, dwd, dgain_m = finish_ff(gff, mlp_gain[None], w_gate, w_up)
    dwq, dwk, dwv, dwo, dgain_a = finish_attention(gatt, attn_gain[None], w_query, w_key, w_value)
    return (
        output[None],
        grad_in.astype(BF)[None],
        dgain_a[0],
        dwq,
        dwk,
        dwv,
        dwo.T,
        dgain_m[0],
        dwg,
        dwu,
        dwd.T,
    )


def solution(mesh):
    in_specs = (
        P("dp", "ctx", None),
        P("dp", "ctx", None),
        P("dp"),
        P("dp", None),
        P("dp", None),
        P("dp", None),
        P(None, "dp"),
        P("dp"),
        P("dp", None),
        P("dp", None),
        P(None, "dp"),
        P("dp", None),
        P("dp", "ctx"),
        P("dp"),
    )
    out_specs = (
        P("dp", "ctx", None),
        P("dp", "ctx", None),
        P("dp"),
        P("dp", None),
        P("dp", None),
        P("dp", None),
        P(None, "dp"),
        P("dp"),
        P("dp", None),
        P("dp", None),
        P(None, "dp"),
    )
    return jax.shard_map(
        on_device, mesh=mesh, in_specs=in_specs, out_specs=out_specs, check_vma=False
    )
```

```python
import functools

import jax
import jax.numpy as jnp
import numpy as np
from jax import lax
from jax.experimental import pallas as pl
from jax.experimental.pallas import tpu as pltpu
from jax.sharding import PartitionSpec as P

HQ = 16
HK = 8
HD = 96
WINDOW = 1024
D = 1536
FF = 4096
BLOCK = 128
LENGTH = 2048
DP = 8
CTX = 16
ZN = 4
SHARD = D // DP
FSH = FF // DP
GROUP = 4 * HD

EPSILON = 1e-05
THETA_BASE = 100000.0
NEG_LARGE = -1e30

BF = jnp.bfloat16
F32 = jnp.float32
MESH = pl.DeviceIdType.MESH
ANY = pl.BlockSpec(memory_space=pl.ANY)
VMEM = pl.BlockSpec(memory_space=pltpu.VMEM)
SMEM = pl.BlockSpec(memory_space=pltpu.SMEM)


def mod(a, n):
    return lax.rem(a + n, n)


class Place:
    def __init__(self):
        self.dp = lax.axis_index("dp")
        self.ctx = lax.axis_index("ctx")
        self.z, self.core = self.dp // 2, lax.rem(self.dp, 2)
        self.y, self.x = self.ctx // 4, lax.rem(self.ctx, 4)

    def at_x(self, k):
        return (self.dp, self.y * 4 + mod(self.x + k, 4))

    def at_y(self, k):
        return (self.dp, mod(self.y + k, 4) * 4 + self.x)

    def at_z(self, k):
        return (mod(self.z + k, 4) * 2 + self.core, self.ctx)

    def at_dp(self, k):
        return (mod(self.dp + k, DP), self.ctx)

    def at_ctx(self, k):
        return (self.dp, mod(self.ctx + k, CTX))

    def sibling(self):
        return (self.z * 2 + 1 - self.core, self.ctx)


class Net:
    def __init__(self, send, recv, local):
        self.send, self.recv, self.local = send, recv, local
        self.n, self.m = 0, 0

    def remote(self, src, dst, peer):
        assert self.n < self.send.shape[0]
        copy = pltpu.make_async_remote_copy(
            src_ref=src,
            dst_ref=dst,
            send_sem=self.send.at[self.n],
            recv_sem=self.recv.at[self.n],
            device_id=peer,
            device_id_type=MESH,
        )
        self.n += 1
        copy.start()
        return copy

    def copy(self, src, dst):
        assert self.m < self.local.shape[0]
        copy = pltpu.make_async_copy(src, dst, self.local.at[self.m])
        self.m += 1
        copy.start()
        return copy


def greet(peers):
    barrier = pltpu.get_barrier_semaphore()
    for peer in peers:
        pl.semaphore_signal(barrier, inc=1, device_id=peer, device_id_type=MESH)
    pl.semaphore_wait(barrier, len(peers))


def xy_peers(p):
    return [p.at_x(k) for k in (1, 2, 3)] + [p.at_y(k) for k in (1, 2, 3)]


def z_peers(p):
    return [p.at_z(k) for k in (1, 2, 3)] + [p.sibling()]


class GatherXY:
    def __init__(self, net, p, own, slot):
        self.net, self.p, self.slot = net, p, slot
        if own is None:
            own, self.kept = (lambda h: slot(h, p.y, p.x)), []
        else:
            self.kept = [net.copy(own(h), slot(h, p.y, p.x)) for h in (0, 1)]
        self.first, self.rest = {}, []
        for k in (1, 2, 3):
            for h in (0, 1):
                here = slot(h, p.y, p.x)
                along = net.remote(own(h), here, p.at_x(k) if h == 0 else p.at_y(k))
                self.first[h, k] = along
        for k in (1, 2, 3):
            for h in (0, 1):
                here = slot(h, p.y, p.x)
                self.rest.append(net.remote(own(h), here, p.at_y(k) if h == 0 else p.at_x(k)))

    def forward(self):
        net, p = self.net, self.p
        for k in (1, 3, 2):
            for h in (0, 1):
                self.first[h, k].wait_recv()
                if h == 0:
                    block = self.slot(0, p.y, mod(p.x - k, 4))
                else:
                    block = self.slot(1, mod(p.y - k, 4), p.x)
                for m in (1, 2, 3):
                    self.rest.append(net.remote(block, block, p.at_y(m) if h == 0 else p.at_x(m)))

    def end(self):
        for copy in self.first.values():
            copy.wait_send()
        for copy in self.rest:
            copy.wait()
        for copy in self.kept:
            copy.wait()


class Exchange:
    def __init__(self, net, p, src, slot):
        self.kept = net.copy(src(p.dp), slot(p.dp))
        self.sent = [net.remote(src(mod(p.dp + k, DP)), slot(p.dp), p.at_dp(k)) for k in range(1, DP)]

    def end(self):
        for copy in self.sent:
            copy.wait()
        self.kept.wait()


def near_peers(p):
    return [p.at_x(1), p.at_x(3), p.at_y(1), p.at_y(3)]


def near_z(p):
    return [p.at_z(1), p.at_z(3), p.sibling()]


class RingXY:
    def __init__(self, net, p, own, slot, part):
        self.net, self.p, self.part = net, p, part
        self.spot = lambda h, a, b: slot(h, b, a) if h == 0 else slot(h, a, b)
        self.me = [(p.x, p.y), (p.y, p.x)]
        self.first = [p.at_x, p.at_y]
        self.second = [p.at_y, p.at_x]
        if own is None:
            own, self.kept = (lambda h: self.spot(h, *self.me[h])), []
        else:
            self.kept = [net.copy(own(h), self.spot(h, *self.me[h])) for h in (0, 1)]
        self.near, self.far, self.side, self.last = {}, {}, {}, []
        for k in (1, 3):
            for h in (0, 1):
                here = self.spot(h, *self.me[h])
                self.near[h, k] = net.remote(own(h), here, self.first[h](k))
        for k in (1, 3):
            for h in (0, 1):
                here = self.spot(h, *self.me[h])
                self.side[h, 0, k] = net.remote(own(h), here, self.second[h](k))

    def send(self, h, a, block):
        for k in (1, 3):
            self.side[h, a, k] = self.net.remote(block, block, self.second[h](k))

    def relay(self, h, a):
        mine, other = self.me[h]
        for k in (1, 3):
            self.side[h, a, k].wait_recv()
            block = self.part(self.spot(h, mod(mine + a, 4), mod(other - k, 4)), k // 2)
            self.last.append(self.net.remote(block, block, self.second[h](k)))

    def forward(self):
        blocks = {}
        for k in (1, 3):
            for h in (0, 1):
                mine, other = self.me[h]
                self.near[h, k].wait_recv()
                blocks[h, k] = self.spot(h, mod(mine - k, 4), other)
                cut = self.part(blocks[h, k], k // 2)
                self.far[h, k] = self.net.remote(cut, cut, self.first[h](k))
        for (h, k), block in blocks.items():
            self.send(h, 4 - k, block)

    def middle(self):
        for h in (0, 1):
            self.relay(h, 0)
        for h in (0, 1):
            for k in (1, 3):
                self.far[h, k].wait_recv()
            mine, other = self.me[h]
            self.send(h, 2, self.spot(h, mod(mine + 2, 4), other))

    def finish(self):
        for a in (1, 3, 2):
            for h in (0, 1):
                self.relay(h, a)

    def arrive(self):
        for copy in self.last:
            copy.wait_recv()
        for copy in self.kept:
            copy.wait()

    def end(self):
        for copies in (self.near, self.far, self.side):
            for copy in copies.values():
                copy.wait_send()
        for copy in self.last:
            copy.wait_send()


class RingDP:
    def __init__(self, net, p, own, slot, part):
        self.net, self.p, self.slot, self.part = net, p, slot, part
        here = slot(p.dp)
        self.kept = [] if own is None else [net.copy(own, here)]
        own = here if own is None else own
        self.near = {k: net.remote(own, here, p.at_z(k)) for k in (1, 3)}
        self.swap = {0: [net.remote(own, here, p.sibling())]}
        self.far = {}

    def forward(self, *ks):
        net, p = self.net, self.p
        for k in ks or (1, 3):
            self.near[k].wait_recv()
            block = self.slot(mod(p.z - k, 4) * 2 + p.core)
            cut = self.part(block, k // 2)
            self.far[k] = net.remote(cut, cut, p.at_z(k))
            self.swap[k] = [net.remote(block, block, p.sibling())]

    def finish(self):
        net, p = self.net, self.p
        self.swap[2] = []
        for k in (1, 3):
            self.far[k].wait_recv()
            cut = self.part(self.slot(mod(p.z + 2, 4) * 2 + p.core), k // 2)
            self.swap[2].append(net.remote(cut, cut, p.sibling()))

    def arrive(self, k):
        if k == 0:
            for copy in self.kept:
                copy.wait()
            self.kept = []
        for copy in self.swap[k]:
            copy.wait_recv()

    def end(self, arrived=False):
        for copy in (*self.near.values(), *self.far.values()):
            copy.wait_send()
        for copies in self.swap.values():
            for copy in copies:
                copy.wait_send() if arrived else copy.wait()
        for copy in self.kept:
            copy.wait()


class RingSum:
    def __init__(self, net, peer, block, part, through, got):
        self.net, self.peer, self.block, self.part = net, peer, block, part
        self.through, self.got = through, got
        self.far, self.near = {}, []

    def start_far(self):
        for k in (1, 3):
            cut = self.part(self.block(2), k // 2)
            self.far[k] = self.net.remote(cut, self.through[k // 2], self.peer(k))

    def start_near(self, k):
        i = 1 - k // 2
        cut = self.part(self.block(k), i)
        self.near.append(self.net.remote(cut, self.part(self.got[k // 2], i), self.peer(k)))

    def start(self):
        self.start_far()
        for k in (1, 3):
            self.start_near(k)

    def forward(self):
        for k in (1, 3):
            i = k // 2
            self.far[k].wait_recv()
            cut = self.part(self.block(k), i)
            add_all(cut, [cut, self.through[i]])
            self.near.append(self.net.remote(cut, self.part(self.got[i], i), self.peer(k)))

    def end(self, out):
        for copy in self.far.values():
            copy.wait_send()
        for copy in self.near:
            copy.wait()
        add_all(out, [self.block(0), self.got[0], self.got[1]])


class SumDP:
    def __init__(self, net, p, part, cut, mine, sib, through, got, out, load=True):
        self.net, self.p, self.part, self.mine, self.sib, self.out = net, p, part, mine, sib, out
        self.ring = RingSum(net, p.at_z, lambda k: mine(mod(p.z + k, 4)), cut, through, got)
        self.load, self.copies = load, {}

    def swap(self, k):
        net, p = self.net, self.p
        z = mod(p.z + k, 4)
        self.copies[k] = [net.remote(self.part(2 * z + 1 - p.core), self.sib.at[z], p.sibling())]
        if self.load:
            self.copies[k].append(net.copy(self.part(2 * z + p.core), self.mine(z)))

    def join(self, k):
        for copy in self.copies[k]:
            copy.wait()
        z = mod(self.p.z + k, 4)
        add_all(self.mine(z), [self.mine(z), self.sib.at[z]])

    def begin(self):
        for k in (2, 1, 3, 0):
            self.swap(k)
        self.join(2)
        self.ring.start_far()
        for k in (1, 3):
            self.join(k)
            self.ring.start_near(k)
        self.join(0)

    def forward(self):
        self.ring.forward()

    def end(self):
        self.ring.end(self.out)


class SumXY:
    def __init__(self, net, p, cut, part, first, second, piece):
        self.p, self.piece = p, piece
        self.cut = cut
        x, y = (lambda k: mod(p.x + k, 4)), (lambda k: mod(p.y + k, 4))
        self.one = [
            RingSum(net, p.at_x, lambda k: cut(0, None, x(k)), part, *first[0]),
            RingSum(net, p.at_y, lambda k: cut(1, y(k), None), part, *first[1]),
        ]
        self.two = [
            RingSum(net, p.at_y, lambda k: cut(0, y(k), p.x), part, *second[0]),
            RingSum(net, p.at_x, lambda k: cut(1, p.y, x(k)), part, *second[1]),
        ]

    def start(self):
        for ring in self.one:
            ring.start()

    def forward(self):
        for ring in self.one:
            ring.forward()

    def turn(self):
        p = self.p
        for h, own in ((0, self.cut(0, None, p.x)), (1, self.cut(1, p.y, None))):
            self.one[h].end(own)
            self.two[h].start()

    def finish(self):
        for ring in self.two:
            ring.forward()

    def end(self):
        for h in (0, 1):
            self.two[h].end(self.piece(h))


def add_all(out, terms):
    *lead, rows, lanes = out.shape
    step_rows = min(rows, max(16, (24 * 1024 // lanes) // 16 * 16))
    while rows % step_rows:
        step_rows -= 16
    steps = rows // step_rows
    count = steps
    for n in lead:
        count *= n

    def step(i, carry):
        j, r = i // steps, lax.rem(i, steps)
        index = []
        for n in reversed(lead):
            index.insert(0, lax.rem(j, n))
            j = j // n
        at = (*index, pl.ds(pl.multiple_of(r * step_rows, 16), step_rows), slice(None))
        total = terms[0][at].astype(F32)
        for term in terms[1:]:
            total = total + term[at].astype(F32)
        out[at] = total.astype(out.dtype)
        return carry

    lax.fori_loop(0, count, step, 0)


def call(body, ident, outs, out_places, remotes, locals_, scratch, *args, vmem=56):
    return pl.pallas_call(
        body,
        out_shape=outs,
        in_specs=[ANY] * len(args),
        out_specs=out_places,
        scratch_shapes=[
            *scratch,
            pltpu.SemaphoreType.DMA((remotes,)),
            pltpu.SemaphoreType.DMA((remotes,)),
            pltpu.SemaphoreType.DMA((locals_,)),
        ],
        compiler_params=pltpu.CompilerParams(
            collective_id=ident, has_side_effects=True, vmem_limit_bytes=vmem << 20
        ),
    )(*args)


def shape(*dims, dtype=BF):
    return jax.ShapeDtypeStruct(dims, dtype)


def rows_of(n):
    return lambda ref, i: ref.at[pl.ds(0, n)] if i == 0 else ref.at[pl.ds(n, ref.shape[0] - n)]


def half(ref, h, n=64):
    return ref.at[pl.ds(h * n, n)]


def sum_dp_scratch(rows=BLOCK, lanes=D):
    return [
        pltpu.VMEM((ZN, rows, lanes), BF),
        pltpu.VMEM((ZN, rows, lanes), BF),
        pltpu.VMEM((rows // 2, lanes), BF),
        pltpu.VMEM((rows // 2, lanes), BF),
        pltpu.VMEM((rows, lanes), BF),
        pltpu.VMEM((rows, lanes), BF),
    ]


def sum_dp(net, p, part, scratch, out):
    mine, sib, t0, t1, g0, g1 = scratch
    cut = rows_of(sib.shape[1] // 2)
    return SumDP(net, p, part, cut, lambda z: mine.at[z], sib, (t0, t1), (g0, g1), out)


def ring_scratch(rows, lanes):
    return [pltpu.VMEM((3, n, rows, lanes), BF) for n in (2, 2, 4, 4)]


def ring_buffers(refs):
    return (refs[0], refs[1]), (refs[2], refs[3])


CHUNK = 256
CHUNKS = LENGTH // CHUNK
SCALE = HD ** (-0.5)


def span(j):
    return max(0, j * CHUNK - WINDOW), (j + 1) * CHUNK


def score_block(k, q_t, hi, j):
    low, high = span(j)
    s = jnp.dot(k[low:high, :], q_t[:, j * CHUNK : (j + 1) * CHUNK], preferred_element_type=F32)
    s = s * SCALE
    key = low + lax.broadcasted_iota(jnp.int32, s.shape, 0)
    query = j * CHUNK + lax.broadcasted_iota(jnp.int32, s.shape, 1)
    last = hi[low:high, :]
    last = jnp.concatenate([last] * (CHUNK // 128), axis=1)
    return jnp.where((query >= key) & (query <= last), s, NEG_LARGE)


def last_readers(lengths, pad):
    key = lax.broadcasted_iota(jnp.int32, (LENGTH, BLOCK), 0)
    end = jnp.int32(0)
    ends = []
    for i in range(4):
        end = end + lengths[0, i]
        ends.append(end)
    doc = jnp.full(key.shape, ends[3], jnp.int32)
    for end in reversed(ends[:3]):
        doc = jnp.where(key < end, end, doc)
    hi = jnp.minimum(key + (WINDOW - 1), doc - 1)
    return jnp.where(key >= LENGTH - pad[0, 0], key, hi)


def turn(values, cosine, sine):
    a, b = values[: HD // 2], values[HD // 2 :]
    return jnp.concatenate([a * cosine - b * sine, b * cosine + a * sine], axis=0)


def forward(
    x, pos, freq, gain_a, gain_m, w_query, w_key, w_value, w_out_t, w_gate, w_up, w_down_t, dd, lengths, pad
):
    def body(
        x, pos, freq, gain_a, gain_m, w_query, w_key, w_value, w_out_t, w_gate, w_up, w_down_t, dd, lengths, pad,
        seq, wdh, home_out, heads_out, part0, part1, ypart,
        q_t, k_t, v_t, top, total, cosine, sine, resid, dresid, da_t,
        rows, spot, w, w_t, wfp, k, att, wo, wf, cot_all, home, xv, hi, wqv, wkv, wvv, wgrp, wraw, wpiece, gain,
        hid, mixed, dgu, epart, e2, sib, t0, t1, g0, g1, grad_v, dat, heads, *rest,
    ):
        rings, (send, recv, local) = rest[:8], rest[8:]
        p = Place()
        net = Net(send, recv, local)
        net.m = 1
        load_x = net.copy(x, xv)
        at_rows = pl.ds(pl.multiple_of(p.y * 48, 16), 48)
        load_pieces = [
            net.copy(
                ref.at[at_rows, pl.ds(pl.multiple_of(f * FSH + p.x * 128, 128), 128)], wraw.at[f, i]
            )
            for i, ref in enumerate((w_gate, w_up, w_down_t))
            for f in range(DP)
        ]
        load_w = [net.copy(a, b) for a, b in ((w_query, wqv), (w_key, wkv), (w_value, wvv))]
        greet([p.at_ctx(i) for i in range(1, CTX)] + [p.at_dp(i) for i in range(1, DP)])
        rank = lax.rem(p.ctx, 2)

        def message(b):
            return pltpu.make_async_remote_copy(
                src_ref=att.at[:, pl.ds(b * BLOCK, BLOCK)],
                dst_ref=home.at[p.ctx],
                send_sem=send.at[b],
                recv_sem=recv.at[p.ctx],
                device_id=(p.dp, jnp.int32(b)),
                device_id_type=MESH,
            )

        def arrival(c):
            return pltpu.make_async_remote_copy(
                src_ref=att.at[:, pl.ds(0, BLOCK)],
                dst_ref=home.at[c],
                send_sem=send.at[c],
                recv_sem=recv.at[c],
                device_id=(p.dp, jnp.int32(c)),
                device_id_type=MESH,
            )

        def kept(b):
            return pltpu.make_async_copy(
                att.at[:, pl.ds(b * BLOCK, BLOCK)], home.at[p.ctx], local.at[0]
            )

        net.n = CTX
        load_x.wait()
        first = xv[...].astype(F32)
        inv = lax.rsqrt(jnp.mean(first * first, axis=-1, keepdims=True) + EPSILON)
        rows[p.ctx] = (first * inv).astype(BF)
        spot[p.ctx] = jnp.broadcast_to(pos[...].astype(F32), (16, BLOCK))
        spots = GatherXY(net, p, None, lambda h, y, x: spot.at[y * 4 + x, pl.ds(h * 8, 8)])
        tokens = RingXY(
            net, p, None, lambda h, y, x: rows.at[y * 4 + x, pl.ds(h * 64, 64)], rows_of(32)
        )

        gain[0] = jnp.broadcast_to(gain_a[...].astype(F32)[None], (BLOCK, SHARD)).T
        gain[1] = jnp.broadcast_to(gain_m[...].astype(F32)[None], (BLOCK, SHARD)).T
        for copy in load_w:
            copy.wait()
        scale = gain[0, :, :1]
        for g in range(HK):
            block = jnp.concatenate(
                [
                    wqv[:, g * 2 * HD : (g + 1) * 2 * HD],
                    wkv[:, g * HD : (g + 1) * HD],
                    wvv[:, g * HD : (g + 1) * HD],
                ],
                axis=1,
            )
            wgrp[g] = (block.astype(F32) * scale).astype(BF)
        job = RingDP(net, p, wgrp.at[p.ctx // 2], lambda i: w.at[i], rows_of(96))
        for copy in load_pieces:
            copy.wait()
        scale = gain[1, pl.ds(pl.multiple_of(p.y * 48, 16), 48), :]
        for f in range(DP):
            for i in (0, 1):
                wpiece[f, i] = (wraw[f, i].astype(F32) * scale).astype(BF)
            wpiece[f, 2] = wraw[f, 2]
        ffw = Exchange(net, p, lambda i: wpiece.at[i], lambda i: wfp.at[:, i])
        spots.forward()
        out = RingDP(net, p, w_out_t, lambda i: wo.at[i], rows_of(96))
        tokens.forward()
        hi[...] = last_readers(lengths, pad)
        tokens.middle()
        job.forward()
        out.forward()
        cot = RingDP(net, p, dd, lambda i: cot_all.at[i], rows_of(64))
        job.finish()
        tokens.finish()
        ffw.end()
        wts = RingXY(
            net,
            p,
            lambda h: wfp.at[:, pl.ds(4 * h, 4)],
            lambda h, y, x: wf.at[
                :,
                pl.ds(4 * h, 4),
                pl.ds(pl.multiple_of(y * 48, 16), 48),
                pl.ds(pl.multiple_of(x * 128, 128), 128),
            ],
            lambda ref, i: ref.at[:, pl.ds(2 * i, 2)],
        )
        for i in (0, 1, 3, 2):
            job.arrive(i)
        job.end(arrived=True)
        w_t[...] = w[...].reshape(D, GROUP).T
        spots.end()
        for j in range(CHUNKS):
            at = slice(j * CHUNK, (j + 1) * CHUNK)
            angles = freq[...] * jnp.concatenate(
                [spot[2 * j, :1, :], spot[2 * j + 1, :1, :]], axis=1
            )
            cosine[:, at], sine[:, at] = jnp.cos(angles), jnp.sin(angles)
        tokens.arrive()
        outs = [net.copy(rows, seq)]
        w_own = jnp.concatenate(
            [w_t[pl.ds(pl.multiple_of(rank * HD, 16), HD), :], w_t[2 * HD :, :]], axis=0
        )
        for j in range(CHUNKS):
            at = slice(j * CHUNK, (j + 1) * CHUNK)
            block = rows[2 * j : 2 * j + 2].reshape(CHUNK, D)
            cos, sin = cosine[:, at], sine[:, at]
            proj = dot(w_own, block, ((1,), (1,)))
            q_t[:, at] = turn(proj[:HD], cos, sin).astype(BF)
            key = turn(proj[HD : 2 * HD], cos, sin).astype(BF)
            k_t[:, at] = key
            k[at, :] = key.T
            v_t[:, at] = proj[2 * HD :].astype(BF)
            low, high = span(j)
            s = score_block(k, q_t, hi, j)
            m = jnp.max(s, axis=0, keepdims=True)
            e = jnp.exp(s - m)
            t = jnp.sum(e, axis=0, keepdims=True)
            prob = (e * (1.0 / t)).astype(BF)
            att[:, at] = jnp.dot(v_t[:, low:high], prob, preferred_element_type=F32).astype(BF)
            top[:, at] = m
            total[:, at] = t
            for b in (2 * j, 2 * j + 1):

                @pl.when(p.ctx == b)
                def _():
                    kept(b).start()

                @pl.when(p.ctx != b)
                def _():
                    message(b).start()

            if j == 1:
                wts.forward()
            if j == 2:
                out.finish()
                cot.forward()
            if j == 4:
                wts.middle()
            if j == 3:
                cot.finish()
                grp = Exchange(net, p, lambda i: wgrp.at[i], lambda i: wdh.at[i])
        wts.finish()
        for i in (0, 1, 3, 2):
            out.arrive(i)
        for b in range(CTX):

            @pl.when(p.ctx == b)
            def _():
                kept(b).wait()

            @pl.when(p.ctx != b)
            def _():
                message(b).wait_send()
                arrival(b).wait_recv()

        own = home[...].reshape(D, BLOCK).T
        y1 = xv[...].astype(F32) + dot(own, wo[...].reshape(D, D), ((1,), (1,)))
        resid[...] = y1
        inv = lax.rsqrt(jnp.mean(y1 * y1, axis=-1, keepdims=True) + EPSILON)
        hid[p.dp] = (y1 * inv).astype(BF)
        ring = RingDP(net, p, None, lambda i: hid.at[i], rows_of(64))
        for i in (0, 1, 3, 2):
            cot.arrive(i)
        w_gate, w_up, w_down = (wf.at[i] for i in range(3))
        sums = SumDP(
            net, p, lambda i: epart.at[i], rows_of(64), lambda z: epart.at[2 * z + p.core], sib,
            (t0, t1), (g0, g1), e2, load=False,
        )

        def work(k):
            z = mod(p.z + k, 4)
            pair = pl.ds(2 * z, 2)
            block = hid[pair].reshape(2 * BLOCK, D)
            wg, wu = w_gate[...].reshape(D, FSH), w_up[...].reshape(D, FSH)
            gate = jnp.dot(block, wg, preferred_element_type=F32)
            up = jnp.dot(block, wu, preferred_element_type=F32)
            sig = jax.nn.sigmoid(gate)
            act = gate * sig
            mixed[pair] = (act * up).astype(BF).reshape(2, BLOCK, FSH)
            wd = w_down[...].reshape(D, FSH)
            dmix = jnp.dot(cot_all[pair].reshape(2 * BLOCK, D), wd, preferred_element_type=F32)
            dg = (dmix * up * sig * (1.0 + gate * (1.0 - sig))).astype(BF)
            du = (dmix * act).astype(BF)
            dgu[pair, :, :FSH] = dg.reshape(2, BLOCK, FSH)
            dgu[pair, :, FSH:] = du.reshape(2, BLOCK, FSH)
            e = dot(dg, wg, ((1,), (1,))) + dot(du, wu, ((1,), (1,)))
            epart[pair] = e.astype(BF).reshape(2, BLOCK, D)
            sums.swap(k)

        wts.arrive()
        ring.arrive(0)
        work(0)
        ring.forward()
        ring.arrive(1)
        work(3)
        ring.finish()
        ring.arrive(3)
        work(1)
        sums.join(3)
        sums.ring.start_near(3)
        ring.arrive(2)
        work(2)
        sums.join(1)
        sums.ring.start_near(1)
        sums.join(2)
        sums.ring.start_far()
        outs.append(net.copy(home, home_out))

        def weights(left, right, *which):
            right = right[...].reshape(DP * BLOCK, FSH * len(which))
            for c in range(4):
                block = left[:, :, c * 384 : (c + 1) * 384].reshape(DP * BLOCK, 384).T
                grad = jnp.dot(block, right, preferred_element_type=F32).astype(BF)
                for n, i in enumerate(which):
                    part = grad[:, n * FSH : (n + 1) * FSH]
                    grad_v[i, 2 * c : 2 * c + 2] = part.reshape(2, SHARD, FSH)

        weights(hid, dgu, 0, 1)
        weights(cot_all, mixed, 2)

        def quarter(ref, i):
            return ref.at[:, pl.ds(2 * i, 2)]

        def column(k):
            lanes = pl.ds(pl.multiple_of(mod(p.x + k, 4) * 128, 128), 128)
            return grad_v.at[:, pl.ds(0, 4), :, lanes]

        def band(k):
            at = pl.ds(pl.multiple_of(mod(p.y + k, 4) * 48, 16), 48)
            return grad_v.at[:, pl.ds(4, 4), at, :]

        ring_x = RingSum(net, p.at_x, column, quarter, *ring_buffers(rings[:4]))
        ring_y = RingSum(net, p.at_y, band, quarter, *ring_buffers(rings[4:]))
        ring_x.start()
        ring_y.start()
        sums.join(0)
        sums.forward()
        sums.end()
        y1 = resid[...]
        inv = lax.rsqrt(jnp.mean(y1 * y1, axis=-1, keepdims=True) + EPSILON)
        u2 = y1 * inv
        e = e2[...]
        d = cot_all[p.dp].astype(F32) + inv * (e - u2 * jnp.mean(e * u2, axis=-1, keepdims=True))
        dresid[...] = d
        da = d.astype(BF)
        grad = jnp.dot(da, wo[...].reshape(D, D), preferred_element_type=F32).astype(BF)
        dat[...] = grad.T.reshape(CTX, HD, BLOCK)
        sent = [
            net.remote(dat.at[mod(p.ctx + i, CTX)], heads.at[p.ctx], p.at_ctx(i))
            for i in range(1, CTX)
        ]
        kept_dat = net.copy(dat.at[p.ctx], heads.at[p.ctx])
        ring_x.forward()
        ring_y.forward()
        da_t[...] = da.T.reshape(DP, SHARD, BLOCK)
        wd = w_down[...].reshape(D, FSH)
        for z in range(ZN):
            y = dot(mixed[2 * z : 2 * z + 2].reshape(2 * BLOCK, FSH), wd, ((1,), (1,)))
            epart[2 * z : 2 * z + 2] = y.astype(BF).reshape(2, BLOCK, D)
        outs.append(net.copy(epart, ypart))
        kept_dat.wait()
        for copy in sent:
            copy.wait()
        outs.append(net.copy(heads, heads_out))
        ring_x.end(column(0))
        outs.append(net.copy(column(0), part0))
        ring_y.end(band(0))
        outs.append(net.copy(band(0), part1))
        for part in (out, cot, ring):
            part.end(arrived=True)
        grp.end()
        tokens.end()
        wts.end()
        for copy in outs:
            copy.wait()

    block = (DP, BLOCK, D)
    head = shape(HD, LENGTH)
    line = shape(1, LENGTH, dtype=F32)
    angle = shape(HD // 2, LENGTH, dtype=F32)
    wide = shape(BLOCK, D, dtype=F32)
    return pl.pallas_call(
        body,
        out_shape=(
            shape(CTX, BLOCK, D),
            shape(DP, SHARD, GROUP),
            shape(CTX, HD, BLOCK),
            shape(CTX, HD, BLOCK),
            shape(3, 4, SHARD, 128),
            shape(3, 4, 48, FSH),
            shape(*block),
            head,
            head,
            head,
            line,
            line,
            angle,
            angle,
            wide,
            wide,
            shape(DP, SHARD, BLOCK),
        ),
        in_specs=[ANY, VMEM, VMEM, VMEM, VMEM, *[ANY] * 8, SMEM, SMEM],
        out_specs=[ANY] * 7 + [VMEM] * 10,
        scratch_shapes=[
            pltpu.VMEM((CTX, BLOCK, D), BF),
            pltpu.VMEM((CTX, 16, BLOCK), F32),
            pltpu.VMEM((DP, SHARD, GROUP), BF),
            pltpu.VMEM((GROUP, D), BF),
            pltpu.VMEM((3, DP, 48, 128), BF),
            pltpu.VMEM((LENGTH, HD), BF),
            pltpu.VMEM((HD, LENGTH), BF),
            pltpu.VMEM((DP, SHARD, D), BF),
            pltpu.VMEM((3, DP, SHARD, FSH), BF),
            pltpu.VMEM(block, BF),
            pltpu.VMEM((CTX, HD, BLOCK), BF),
            pltpu.VMEM((BLOCK, D), BF),
            pltpu.VMEM((LENGTH, BLOCK), jnp.int32),
            pltpu.VMEM((SHARD, D), BF),
            pltpu.VMEM((SHARD, HK * HD), BF),
            pltpu.VMEM((SHARD, HK * HD), BF),
            pltpu.VMEM((DP, SHARD, GROUP), BF),
            pltpu.VMEM((DP, 3, 48, 128), BF),
            pltpu.VMEM((DP, 3, 48, 128), BF),
            pltpu.VMEM((2, SHARD, BLOCK), F32),
            pltpu.VMEM(block, BF),
            pltpu.VMEM((DP, BLOCK, FSH), BF),
            pltpu.VMEM((DP, BLOCK, 2 * FSH), BF),
            pltpu.VMEM(block, BF),
            pltpu.VMEM((BLOCK, D), F32),
            pltpu.VMEM((ZN, BLOCK, D), BF),
            pltpu.VMEM((BLOCK // 2, D), BF),
            pltpu.VMEM((BLOCK // 2, D), BF),
            pltpu.VMEM((BLOCK, D), BF),
            pltpu.VMEM((BLOCK, D), BF),
            pltpu.VMEM((3, DP, SHARD, FSH), BF),
            pltpu.VMEM((CTX, HD, BLOCK), BF),
            pltpu.VMEM((CTX, HD, BLOCK), BF),
            *ring_scratch(SHARD, 128),
            *ring_scratch(48, FSH),
            pltpu.SemaphoreType.DMA((213,)),
            pltpu.SemaphoreType.DMA((213,)),
            pltpu.SemaphoreType.DMA((48,)),
        ],
        compiler_params=pltpu.CompilerParams(
            collective_id=2, has_side_effects=True, vmem_limit_bytes=60 << 20
        ),
    )(
        x, pos, freq, gain_a, gain_m, w_query, w_key, w_value, w_out_t, w_gate, w_up, w_down_t, dd, lengths, pad
    )


def backward(heads, att, da_t, part0, part1, ypart, wdh, seq, q_t, k_t, v_t, top, total, cosine, sine, lengths, pad):
    def body(
        heads, att, da_t, part0, part1, ypart, wdh, seq, q_t, k_t, v_t, top, total, cosine, sine, lengths, pad,
        e1, ysum, gff, gatt,
        hi, rows, k, v, q, do, do_t, dk, dv, out, wide, heads_v, att_all, da_all, dwj, full, away, comb,
        dwo, w0, f0, s0, back, wdh_v, dh1, wide0, wide1, piece, grads, *rest,
    ):
        rings, rest = rest[:8], rest[8:]
        j_sib, j_t0, j_t1, j_g0, j_g1, *rest = rest
        h_sib, h_t0, h_t1, h_g0, h_g1, *rest = rest
        y_scratch, (send, recv, local) = rest[:6], rest[6:]
        p = Place()
        net = Net(send, recv, local)
        group, rank = p.ctx // 2, lax.rem(p.ctx, 2)
        home = group == p.dp
        partner = (p.dp, p.ctx + 1 - 2 * rank)

        barrier = pltpu.get_barrier_semaphore()
        others = xy_peers(p) + [p.at_dp(i) for i in range(1, DP)]
        for peer in others:
            pl.semaphore_signal(barrier, inc=1, device_id=peer, device_id_type=MESH)
        for i in range(DP):
            for r in range(2):

                @pl.when(jnp.logical_not(home & (p.dp == i) & (rank == r)))
                def _():
                    peer = (jnp.int32(i), 2 * p.dp + r)
                    pl.semaphore_signal(barrier, inc=1, device_id=peer, device_id_type=MESH)

        pl.semaphore_wait(barrier, CTX + len(others) - home.astype(jnp.int32))

        slot = p.dp * 2 + rank

        def message(b, spot):
            return pltpu.make_async_remote_copy(
                src_ref=out.at[:, pl.ds(b * BLOCK, BLOCK)],
                dst_ref=back.at[spot],
                send_sem=send.at[b],
                recv_sem=recv.at[spot],
                device_id=(group, jnp.int32(b)),
                device_id_type=MESH,
            )

        def own(b):
            return pltpu.make_async_copy(
                out.at[:, pl.ds(b * BLOCK, BLOCK)], back.at[slot], local.at[0]
            )

        net.n, net.m = CTX, 1

        load_wide = [net.copy(part0, wide0), net.copy(part1, wide1)]
        load_heads = net.copy(heads, heads_v)
        das = Exchange(net, p, lambda i: da_t.at[i], lambda i: da_all.at[i])
        load_rows = net.copy(seq, rows)
        atts = RingDP(net, p, att, lambda i: att_all.at[i], rows_of(D // 2))
        load_wdh = net.copy(wdh, wdh_v)

        def quarter(ref, i):
            return ref.at[:, pl.ds(2 * i, 2)]

        def band(k):
            return wide0.at[:, :, pl.ds(pl.multiple_of(mod(p.y + k, 4) * 48, 16), 48), :]

        def column(k):
            return wide1.at[:, :, :, pl.ds(pl.multiple_of(mod(p.x + k, 4) * 128, 128), 128)]

        ring_y = RingSum(net, p.at_y, band, quarter, *ring_buffers(rings[:4]))
        ring_x = RingSum(net, p.at_x, column, quarter, *ring_buffers(rings[4:]))
        for copy in load_wide:
            copy.wait()
        ring_y.start()
        ring_x.start()
        res = sum_dp(net, p, lambda i: ypart.at[i], y_scratch, ysum)
        for i in (2, 1, 3, 0):
            res.swap(i)
        k[...] = k_t[...].T
        v[...] = v_t[...].T
        ring_y.forward()
        ring_x.forward()
        q[...] = q_t[...].T
        hi[...] = last_readers(lengths, pad)
        dk[...] = jnp.zeros_like(dk)
        dv[...] = jnp.zeros_like(dv)
        ring_y.end(piece.at[:, pl.ds(0, 4)])
        ring_x.end(piece.at[:, pl.ds(4, 4)])
        swap = Exchange(net, p, lambda i: piece.at[:, i], lambda i: grads.at[i])
        load_heads.wait()
        for b in range(CTX):
            do_t[:, b * BLOCK : (b + 1) * BLOCK] = heads_v[b]
        do[...] = do_t[...].T

        def chunk(j):
            low, high = span(j)
            at = slice(j * CHUNK, (j + 1) * CHUNK)
            s = score_block(k, q_t, hi, j)
            prob = jnp.exp(s - top[:, at]) * (1.0 / total[:, at])
            dp = jnp.dot(v[low:high, :], do_t[:, at], preferred_element_type=F32)
            inner = jnp.sum(prob * dp, axis=0, keepdims=True)
            ds = (prob * (dp - inner)).astype(BF)
            dq = jnp.dot(k_t[:, low:high], ds, preferred_element_type=F32) * SCALE
            dk[low:high, :] += jnp.dot(ds, q[at, :], preferred_element_type=F32)
            dv[low:high, :] += jnp.dot(prob.astype(BF), do[at, :], preferred_element_type=F32)
            cos, sin = cosine[:, at], -sine[:, at]
            out[:HD, at] = turn(dq, cos, sin).astype(BF)
            out[HD : 2 * HD, at] = turn(dk[at, :].T * SCALE, cos, sin).astype(BF)
            out[2 * HD :, at] = dv[at, :].T.astype(BF)
            for b in (2 * j, 2 * j + 1):
                here = home & (p.ctx == b)

                @pl.when(here)
                def _():
                    own(b).start()

                @pl.when(jnp.logical_not(here))
                def _():
                    message(b, slot).start()

        gather = None
        for j in reversed(range(CHUNKS)):
            chunk(j)
            if j == 5:
                swap.end()
                gather = RingXY(
                    net,
                    p,
                    lambda h: grads.at[pl.ds(4 * h, 4)],
                    lambda h, y, x: gff.at[
                        pl.ds(4 * h, 4),
                        :,
                        pl.ds(pl.multiple_of(y * 48, 16), 48),
                        pl.ds(pl.multiple_of(x * 128, 128), 128),
                    ],
                    rows_of(2),
                )
            if j == 3:
                atts.forward()
            if j == 2:
                for i in (2, 1, 3, 0):
                    res.join(i)

        mine = pl.multiple_of(rank * HD, 16)
        other = pl.multiple_of((1 - rank) * HD, 16)
        wide[pl.ds(mine, HD), :] = out[:HD, :]
        wide[pl.ds(other, HD), :] = jnp.zeros((HD, LENGTH), BF)
        wide[2 * HD :, :] = out[HD:, :]
        load_rows.wait()
        grad = jnp.dot(wide[...], rows[...].reshape(LENGTH, D), preferred_element_type=F32)
        dwj[...] = grad.T.astype(BF).reshape(DP, SHARD, GROUP)
        proj = SumDP(
            net, p, lambda i: dwj.at[i], rows_of(96), lambda z: dwj.at[2 * z + p.core], j_sib,
            (j_t0, j_t1), (j_g0, j_g1), full, load=False,
        )
        proj.begin()
        gather.forward()
        atts.finish()

        das.end()
        for i in (0, 1, 3, 2):
            atts.arrive(i)
        atts.end(arrived=True)
        grad = dot(da_all[0], att_all[0], ((1,), (1,)))
        for i in range(1, DP):
            grad += dot(da_all[i], att_all[i], ((1,), (1,)))
        dwo[...] = grad.astype(BF)
        wide_cuts = [net.copy(dwo.at[:, pl.ds(pl.multiple_of(p.x * 384, 128), 384)], w0)]
        for i in (1, 3, 2):
            lanes = pl.ds(pl.multiple_of(mod(p.x + i, 4) * 384, 128), 384)
            wide_cuts.append(net.remote(dwo.at[:, lanes], f0.at[i - 1], p.at_x(i)))
        gather.middle()
        proj.forward()

        load_wdh.wait()
        inp = SumDP(
            net, p, lambda i: dh1.at[i], rows_of(64), lambda z: dh1.at[2 * z + p.core], h_sib,
            (h_t0, h_t1), (h_g0, h_g1), e1, load=False,
        )
        for spot in range(CTX):

            @pl.when(jnp.logical_not(home & (slot == spot)))
            def _():
                message(0, spot).wait_recv()

        for b in range(CTX):
            here = home & (p.ctx == b)

            @pl.when(here)
            def _():
                own(b).wait()

            @pl.when(jnp.logical_not(here))
            def _():
                message(b, slot).wait_send()

        def inputs(step):
            z = mod(p.z + step, 4)
            turned = []
            for core in (0, 1):
                i = 2 * z + core
                first, second = back[2 * i].astype(F32), back[2 * i + 1].astype(F32)
                both = jnp.concatenate([first[:HD], second[:HD], first[HD:] + second[HD:]], axis=0)
                turned.append(both.T.astype(BF))
            turned = jnp.concatenate(turned, axis=0)
            grad = dot(turned, wdh_v[...].reshape(D, GROUP), ((1,), (1,)))
            dh1[pl.ds(2 * z, 2)] = grad.astype(BF).reshape(2, BLOCK, D)
            inp.swap(step)

        inputs(2)
        inputs(1)
        inp.join(2)
        inp.ring.start_far()
        inputs(3)
        inp.join(1)
        inp.ring.start_near(1)
        inputs(0)
        inp.join(3)
        inp.ring.start_near(3)
        proj.end()
        theirs = full.at[pl.ds(pl.multiple_of((1 - rank) * 96, 16), 96)]
        trade = net.remote(theirs, away, partner)
        for copy in wide_cuts:
            copy.wait()
        add_all(w0, [w0] + [f0.at[i] for i in range(3)])
        tall = []
        for i in (1, 3, 2):
            at = pl.ds(pl.multiple_of(mod(p.y + i, 4) * 48, 16), 48)
            tall.append(net.remote(w0.at[at], s0.at[i - 1], p.at_y(i)))
        gather.finish()
        inp.join(0)
        inp.forward()
        res.ring.start_far()
        for i in (1, 3):
            res.ring.start_near(i)
        trade.wait()
        add_all(
            comb.at[pl.ds(0, 96)], [full.at[pl.ds(pl.multiple_of(rank * 96, 16), 96)], away]
        )
        for copy in tall:
            copy.wait()
        at = pl.ds(pl.multiple_of(p.y * 48, 16), 48)
        add_all(comb.at[pl.ds(96, 48)], [w0.at[at]] + [s0.at[i] for i in range(3)])
        small = RingXY(
            net,
            p,
            lambda h: comb.at[pl.ds(80 * h, 80 - 16 * h)],
            lambda h, y, x: gatt.at[y * 4 + x, pl.ds(80 * h, 80 - 16 * h)],
            rows_of(48),
        )
        inp.end()
        small.forward()
        res.forward()
        small.middle()
        small.finish()
        res.end()
        for part in (gather, small):
            part.arrive()
            part.end()

    head = pltpu.VMEM((LENGTH, HD), BF)
    return pl.pallas_call(
        body,
        out_shape=(
            shape(BLOCK, D, dtype=F32),
            shape(BLOCK, D, dtype=F32),
            shape(DP, 3, SHARD, FSH),
            shape(CTX, 144, GROUP),
        ),
        in_specs=[ANY] * 8 + [VMEM] * 7 + [SMEM] * 2,
        out_specs=[VMEM, VMEM, ANY, ANY],
        scratch_shapes=[
            pltpu.VMEM((LENGTH, BLOCK), jnp.int32),
            pltpu.VMEM((CTX, BLOCK, D), BF),
            head,
            head,
            head,
            head,
            pltpu.VMEM((HD, LENGTH), BF),
            pltpu.VMEM((LENGTH, HD), F32),
            pltpu.VMEM((LENGTH, HD), F32),
            pltpu.VMEM((3 * HD, LENGTH), BF),
            pltpu.VMEM((GROUP, LENGTH), BF),
            pltpu.VMEM((CTX, HD, BLOCK), BF),
            pltpu.VMEM((DP, D, BLOCK), BF),
            pltpu.VMEM((DP, SHARD, BLOCK), BF),
            pltpu.VMEM((DP, SHARD, GROUP), BF),
            pltpu.VMEM((SHARD, GROUP), BF),
            pltpu.VMEM((96, GROUP), BF),
            pltpu.VMEM((144, GROUP), BF),
            pltpu.VMEM((SHARD, D), BF),
            pltpu.VMEM((SHARD, 384), BF),
            pltpu.VMEM((3, SHARD, 384), BF),
            pltpu.VMEM((3, 48, 384), BF),
            pltpu.VMEM((CTX, 3 * HD, BLOCK), BF),
            pltpu.VMEM((DP, SHARD, GROUP), BF),
            pltpu.VMEM((DP, BLOCK, D), BF),
            pltpu.VMEM((3, 4, SHARD, 128), BF),
            pltpu.VMEM((3, 4, 48, FSH), BF),
            pltpu.VMEM((3, DP, 48, 128), BF),
            pltpu.VMEM((DP, 3, 48, 128), BF),
            *ring_scratch(48, 128),
            *ring_scratch(48, 128),
            *sum_dp_scratch(SHARD, GROUP)[1:],
            *sum_dp_scratch()[1:],
            *sum_dp_scratch(),
            pltpu.SemaphoreType.DMA((169,)),
            pltpu.SemaphoreType.DMA((169,)),
            pltpu.SemaphoreType.DMA((24,)),
        ],
        compiler_params=pltpu.CompilerParams(
            collective_id=4, has_side_effects=True, vmem_limit_bytes=60 << 20
        ),
    )(heads, att, da_t, part0, part1, ypart, wdh, seq, q_t, k_t, v_t, top, total, cosine, sine, lengths, pad)


def finish(gff, gatt, gain_a, gain_m, w_gate, w_up, w_query, w_key, w_value):
    def body(
        gff, gatt, gain_a, gain_m, w_gate, w_up, w_query, w_key, w_value,
        gate, up, down, dq, dk, dv, do, dgain_a, dgain_m,
        gv, gv_att, wg, wu, wq, wk, wv, ov, oq, ok, ow, oo, load, store,
    ):
        lanes = [pl.ds(f * FSH, FSH) for f in range(DP)]
        loads, stores = [], []

        def fetch(*pairs):
            copies = [
                pltpu.make_async_copy(a, b, load.at[len(loads) + i]) for i, (a, b) in enumerate(pairs)
            ]
            loads.extend(copies)
            for copy in copies:
                copy.start()
            return copies

        def put(a, b):
            copy = pltpu.make_async_copy(a, b, store.at[len(stores)])
            stores.append(copy)
            copy.start()

        steps = [
            fetch(
                (gff.at[f], gv.at[f]),
                (w_gate.at[:, lanes[f]], wg.at[:, lanes[f]]),
                (w_up.at[:, lanes[f]], wu.at[:, lanes[f]]),
            )
            for f in range(DP)
        ]
        rest = fetch((gatt, gv_att), (w_query, wq), (w_key, wk), (w_value, wv))

        def column(gain):
            return jnp.broadcast_to(gain[...].astype(F32)[None], (BLOCK, SHARD)).T[:, :1]

        def line(total):
            return jnp.broadcast_to(total, (SHARD, BLOCK)).T[0]

        rows = column(gain_m)
        total = jnp.zeros((SHARD, FSH), F32)
        for f in range(DP):
            for copy in steps[f]:
                copy.wait()
            g, u = gv[f, 0].astype(F32), gv[f, 1].astype(F32)
            total += g * wg[:, lanes[f]].astype(F32) + u * wu[:, lanes[f]].astype(F32)
            ov[0, :, lanes[f]] = g * rows
            ov[1, :, lanes[f]] = u * rows
            ov[2, :, lanes[f]] = gv[f, 2].astype(F32)
            for i, out in enumerate((gate, up, down)):
                put(ov.at[i, :, lanes[f]], out.at[:, lanes[f]])
        dgain_m[...] = line(jnp.sum(total, axis=1, keepdims=True))
        for copy in rest:
            copy.wait()
        rows = column(gain_a)
        for c in range(CTX):
            y, x = divmod(c, 4)
            oo[y * 48 : (y + 1) * 48, x * 384 : (x + 1) * 384] = gv_att[c, 96:].astype(F32)
        put(oo, do)
        for g in range(HK):
            block = gv_att[2 * g : 2 * g + 2, :96].reshape(SHARD, GROUP).astype(F32)
            oq[:, g * 2 * HD : (g + 1) * 2 * HD] = block[:, : 2 * HD]
            ok[:, g * HD : (g + 1) * HD] = block[:, 2 * HD : 3 * HD]
            ow[:, g * HD : (g + 1) * HD] = block[:, 3 * HD :]
        total = jnp.zeros((SHARD, 1), F32)
        for grad, weight, out in ((oq, wq, dq), (ok, wk, dk), (ow, wv, dv)):
            total += jnp.sum(grad[...] * weight[...].astype(F32), axis=1, keepdims=True)
            grad[...] = grad[...] * rows
            put(grad, out)
        dgain_a[...] = line(total)
        for copy in stores:
            copy.wait()

    big = shape(SHARD, FF, dtype=F32)
    square = shape(SHARD, D, dtype=F32)
    small = shape(SHARD, HK * HD, dtype=F32)
    row = shape(SHARD, dtype=F32)
    return pl.pallas_call(
        body,
        out_shape=(big, big, big, square, small, small, square, row, row),
        in_specs=[ANY, ANY, VMEM, VMEM] + [ANY] * 5,
        out_specs=[ANY] * 7 + [VMEM] * 2,
        scratch_shapes=[
            pltpu.VMEM((DP, 3, SHARD, FSH), BF),
            pltpu.VMEM((CTX, 144, GROUP), BF),
            pltpu.VMEM((SHARD, FF), BF),
            pltpu.VMEM((SHARD, FF), BF),
            pltpu.VMEM((SHARD, D), BF),
            pltpu.VMEM((SHARD, HK * HD), BF),
            pltpu.VMEM((SHARD, HK * HD), BF),
            pltpu.VMEM((3, SHARD, FF), F32),
            pltpu.VMEM((SHARD, D), F32),
            pltpu.VMEM((SHARD, HK * HD), F32),
            pltpu.VMEM((SHARD, HK * HD), F32),
            pltpu.VMEM((SHARD, D), F32),
            pltpu.SemaphoreType.DMA((28,)),
            pltpu.SemaphoreType.DMA((28,)),
        ],
        compiler_params=pltpu.CompilerParams(vmem_limit_bytes=56 << 20),
    )(gff, gatt, gain_a, gain_m, w_gate, w_up, w_query, w_key, w_value)


def dot(left, right, contract):
    return lax.dot_general(left, right, (contract, ((), ())), preferred_element_type=F32)


def on_device(
    layer_input,
    cotangent,
    attn_gain,
    w_query,
    w_key,
    w_value,
    w_out,
    mlp_gain,
    w_gate,
    w_up,
    w_down,
    doc_lengths,
    rope_pos,
    pad_lengths,
):
    inputs = layer_input[0].astype(F32)
    inv_one = lax.rsqrt(jnp.mean(inputs * inputs, axis=-1, keepdims=True) + EPSILON)
    u1 = inputs * inv_one
    freq = np.float32(THETA_BASE) ** (-(np.arange(HD // 2, dtype=np.float32) * np.float32(2.0) / np.float32(HD)))
    pad = pad_lengths[:, None]
    (
        seq, wdh, att, heads, part0, part1, ypart,
        q_t, k_t, v_t, top, total, cosine, sine, resid, dresid, da_t,
    ) = forward(
        layer_input[0], rope_pos, jnp.asarray(freq[:, None]), attn_gain, mlp_gain,
        w_query, w_key, w_value, w_out.T, w_gate, w_up, w_down.T, cotangent[0], doc_lengths, pad,
    )
    e1, ysum, gff, gatt = backward(
        heads, att.reshape(D, BLOCK), da_t, part0, part1, ypart, wdh,
        seq, q_t, k_t, v_t, top, total, cosine, sine, doc_lengths, pad,
    )
    output = (resid + ysum).astype(BF)
    grad_in = dresid + inv_one * (e1 - u1 * jnp.mean(e1 * u1, axis=-1, keepdims=True))

    dwg, dwu, dwd, dwq, dwk, dwv, dwo, dgain_a, dgain_m = finish(
        gff, gatt, attn_gain, mlp_gain, w_gate, w_up, w_query, w_key, w_value
    )
    return (
        output[None],
        grad_in.astype(BF)[None],
        dgain_a,
        dwq,
        dwk,
        dwv,
        dwo.T,
        dgain_m,
        dwg,
        dwu,
        dwd.T,
    )


def solution(mesh):
    in_specs = (
        P("dp", "ctx", None),
        P("dp", "ctx", None),
        P("dp"),
        P("dp", None),
        P("dp", None),
        P("dp", None),
        P(None, "dp"),
        P("dp"),
        P("dp", None),
        P("dp", None),
        P(None, "dp"),
        P("dp", None),
        P("dp", "ctx"),
        P("dp"),
    )
    out_specs = (
        P("dp", "ctx", None),
        P("dp", "ctx", None),
        P("dp"),
        P("dp", None),
        P("dp", None),
        P("dp", None),
        P(None, "dp"),
        P("dp"),
        P("dp", None),
        P("dp", None),
        P(None, "dp"),
    )
    return jax.shard_map(
        on_device, mesh=mesh, in_specs=in_specs, out_specs=out_specs, check_vma=False
    )
```

```python
import functools

import jax
import jax.numpy as jnp
import numpy as np
from jax import lax
from jax.experimental import pallas as pl
from jax.experimental.pallas import tpu as pltpu
from jax.sharding import PartitionSpec as P

HQ = 16
HK = 8
HD = 96
WINDOW = 1024
D = 1536
FF = 4096
BLOCK = 128
LENGTH = 2048
DP = 8
CTX = 16
ZN = 4
SHARD = D // DP
FSH = FF // DP
GROUP = 4 * HD

EPSILON = 1e-05
THETA_BASE = 100000.0
NEG_LARGE = -1e30

BF = jnp.bfloat16
F32 = jnp.float32
MESH = pl.DeviceIdType.MESH
ANY = pl.BlockSpec(memory_space=pl.ANY)
VMEM = pl.BlockSpec(memory_space=pltpu.VMEM)
SMEM = pl.BlockSpec(memory_space=pltpu.SMEM)


def mod(a, n):
    return lax.rem(a + n, n)


class Place:
    def __init__(self):
        self.dp = lax.axis_index("dp")
        self.ctx = lax.axis_index("ctx")
        self.z, self.core = self.dp // 2, lax.rem(self.dp, 2)
        self.y, self.x = self.ctx // 4, lax.rem(self.ctx, 4)

    def at_x(self, k):
        return (self.dp, self.y * 4 + mod(self.x + k, 4))

    def at_y(self, k):
        return (self.dp, mod(self.y + k, 4) * 4 + self.x)

    def at_z(self, k):
        return (mod(self.z + k, 4) * 2 + self.core, self.ctx)

    def at_dp(self, k):
        return (mod(self.dp + k, DP), self.ctx)

    def at_ctx(self, k):
        return (self.dp, mod(self.ctx + k, CTX))

    def sibling(self):
        return (self.z * 2 + 1 - self.core, self.ctx)


class Net:
    def __init__(self, send, recv, local):
        self.send, self.recv, self.local = send, recv, local
        self.n, self.m = 0, 0

    def remote(self, src, dst, peer):
        assert self.n < self.send.shape[0]
        copy = pltpu.make_async_remote_copy(
            src_ref=src,
            dst_ref=dst,
            send_sem=self.send.at[self.n],
            recv_sem=self.recv.at[self.n],
            device_id=peer,
            device_id_type=MESH,
        )
        self.n += 1
        copy.start()
        return copy

    def copy(self, src, dst):
        assert self.m < self.local.shape[0]
        copy = pltpu.make_async_copy(src, dst, self.local.at[self.m])
        self.m += 1
        copy.start()
        return copy


def greet(peers):
    barrier = pltpu.get_barrier_semaphore()
    for peer in peers:
        pl.semaphore_signal(barrier, inc=1, device_id=peer, device_id_type=MESH)
    pl.semaphore_wait(barrier, len(peers))


def xy_peers(p):
    return [p.at_x(k) for k in (1, 2, 3)] + [p.at_y(k) for k in (1, 2, 3)]


def z_peers(p):
    return [p.at_z(k) for k in (1, 2, 3)] + [p.sibling()]


class GatherXY:
    def __init__(self, net, p, own, slot):
        self.net, self.p, self.slot = net, p, slot
        if own is None:
            own, self.kept = (lambda h: slot(h, p.y, p.x)), []
        else:
            self.kept = [net.copy(own(h), slot(h, p.y, p.x)) for h in (0, 1)]
        self.first, self.rest = {}, []
        for k in (1, 2, 3):
            for h in (0, 1):
                here = slot(h, p.y, p.x)
                along = net.remote(own(h), here, p.at_x(k) if h == 0 else p.at_y(k))
                self.first[h, k] = along
        for k in (1, 2, 3):
            for h in (0, 1):
                here = slot(h, p.y, p.x)
                self.rest.append(net.remote(own(h), here, p.at_y(k) if h == 0 else p.at_x(k)))

    def forward(self):
        net, p = self.net, self.p
        for k in (1, 3, 2):
            for h in (0, 1):
                self.first[h, k].wait_recv()
                if h == 0:
                    block = self.slot(0, p.y, mod(p.x - k, 4))
                else:
                    block = self.slot(1, mod(p.y - k, 4), p.x)
                for m in (1, 2, 3):
                    self.rest.append(net.remote(block, block, p.at_y(m) if h == 0 else p.at_x(m)))

    def end(self):
        for copy in self.first.values():
            copy.wait_send()
        for copy in self.rest:
            copy.wait()
        for copy in self.kept:
            copy.wait()


class Exchange:
    def __init__(self, net, p, src, slot):
        self.kept = net.copy(src(p.dp), slot(p.dp))
        self.sent = [net.remote(src(mod(p.dp + k, DP)), slot(p.dp), p.at_dp(k)) for k in range(1, DP)]

    def end(self):
        for copy in self.sent:
            copy.wait()
        self.kept.wait()


def near_peers(p):
    return [p.at_x(1), p.at_x(3), p.at_y(1), p.at_y(3)]


def near_z(p):
    return [p.at_z(1), p.at_z(3), p.sibling()]


class RingXY:
    def __init__(self, net, p, own, slot, part):
        self.net, self.p, self.part = net, p, part
        self.spot = lambda h, a, b: slot(h, b, a) if h == 0 else slot(h, a, b)
        self.me = [(p.x, p.y), (p.y, p.x)]
        self.first = [p.at_x, p.at_y]
        self.second = [p.at_y, p.at_x]
        if own is None:
            own, self.kept = (lambda h: self.spot(h, *self.me[h])), []
        else:
            self.kept = [net.copy(own(h), self.spot(h, *self.me[h])) for h in (0, 1)]
        self.near, self.far, self.side, self.last = {}, {}, {}, []
        for k in (1, 3):
            for h in (0, 1):
                here = self.spot(h, *self.me[h])
                self.near[h, k] = net.remote(own(h), here, self.first[h](k))
        for k in (1, 3):
            for h in (0, 1):
                here = self.spot(h, *self.me[h])
                self.side[h, 0, k] = net.remote(own(h), here, self.second[h](k))

    def send(self, h, a, block):
        for k in (1, 3):
            self.side[h, a, k] = self.net.remote(block, block, self.second[h](k))

    def relay(self, h, a):
        mine, other = self.me[h]
        for k in (1, 3):
            self.side[h, a, k].wait_recv()
            block = self.part(self.spot(h, mod(mine + a, 4), mod(other - k, 4)), k // 2)
            self.last.append(self.net.remote(block, block, self.second[h](k)))

    def forward(self):
        blocks = {}
        for k in (1, 3):
            for h in (0, 1):
                mine, other = self.me[h]
                self.near[h, k].wait_recv()
                blocks[h, k] = self.spot(h, mod(mine - k, 4), other)
                cut = self.part(blocks[h, k], k // 2)
                self.far[h, k] = self.net.remote(cut, cut, self.first[h](k))
        for (h, k), block in blocks.items():
            self.send(h, 4 - k, block)

    def middle(self):
        for h in (0, 1):
            self.relay(h, 0)
        for h in (0, 1):
            for k in (1, 3):
                self.far[h, k].wait_recv()
            mine, other = self.me[h]
            self.send(h, 2, self.spot(h, mod(mine + 2, 4), other))

    def finish(self):
        for a in (1, 3, 2):
            for h in (0, 1):
                self.relay(h, a)

    def arrive(self):
        for copy in self.last:
            copy.wait_recv()
        for copy in self.kept:
            copy.wait()

    def end(self):
        for copies in (self.near, self.far, self.side):
            for copy in copies.values():
                copy.wait_send()
        for copy in self.last:
            copy.wait_send()


class RingDP:
    def __init__(self, net, p, own, slot, part):
        self.net, self.p, self.slot, self.part = net, p, slot, part
        here = slot(p.dp)
        self.kept = [] if own is None else [net.copy(own, here)]
        own = here if own is None else own
        self.near = {k: net.remote(own, here, p.at_z(k)) for k in (1, 3)}
        self.swap = {0: [net.remote(own, here, p.sibling())]}
        self.far = {}

    def forward(self, *ks):
        net, p = self.net, self.p
        for k in ks or (1, 3):
            self.near[k].wait_recv()
            block = self.slot(mod(p.z - k, 4) * 2 + p.core)
            cut = self.part(block, k // 2)
            self.far[k] = net.remote(cut, cut, p.at_z(k))
            self.swap[k] = [net.remote(block, block, p.sibling())]

    def finish(self):
        net, p = self.net, self.p
        self.swap[2] = []
        for k in (1, 3):
            self.far[k].wait_recv()
            cut = self.part(self.slot(mod(p.z + 2, 4) * 2 + p.core), k // 2)
            self.swap[2].append(net.remote(cut, cut, p.sibling()))

    def arrive(self, k):
        if k == 0:
            for copy in self.kept:
                copy.wait()
            self.kept = []
        for copy in self.swap[k]:
            copy.wait_recv()

    def end(self, arrived=False):
        for copy in (*self.near.values(), *self.far.values()):
            copy.wait_send()
        for copies in self.swap.values():
            for copy in copies:
                copy.wait_send() if arrived else copy.wait()
        for copy in self.kept:
            copy.wait()


class RingSum:
    def __init__(self, net, peer, block, part, through, got):
        self.net, self.peer, self.block, self.part = net, peer, block, part
        self.through, self.got = through, got
        self.far, self.near = {}, []

    def start_far(self):
        for k in (1, 3):
            cut = self.part(self.block(2), k // 2)
            self.far[k] = self.net.remote(cut, self.through[k // 2], self.peer(k))

    def start_near(self, k):
        i = 1 - k // 2
        cut = self.part(self.block(k), i)
        self.near.append(self.net.remote(cut, self.part(self.got[k // 2], i), self.peer(k)))

    def start(self):
        self.start_far()
        for k in (1, 3):
            self.start_near(k)

    def forward(self):
        for k in (1, 3):
            i = k // 2
            self.far[k].wait_recv()
            cut = self.part(self.block(k), i)
            add_all(cut, [cut, self.through[i]])
            self.near.append(self.net.remote(cut, self.part(self.got[i], i), self.peer(k)))

    def end(self, out):
        for copy in self.far.values():
            copy.wait_send()
        for copy in self.near:
            copy.wait()
        add_all(out, [self.block(0), self.got[0], self.got[1]])


class SumDP:
    def __init__(self, net, p, part, cut, mine, sib, through, got, out, load=True):
        self.net, self.p, self.part, self.mine, self.sib, self.out = net, p, part, mine, sib, out
        self.ring = RingSum(net, p.at_z, lambda k: mine(mod(p.z + k, 4)), cut, through, got)
        self.load, self.copies = load, {}

    def swap(self, k):
        net, p = self.net, self.p
        z = mod(p.z + k, 4)
        self.copies[k] = [net.remote(self.part(2 * z + 1 - p.core), self.sib.at[z], p.sibling())]
        if self.load:
            self.copies[k].append(net.copy(self.part(2 * z + p.core), self.mine(z)))

    def join(self, k):
        for copy in self.copies[k]:
            copy.wait()
        z = mod(self.p.z + k, 4)
        add_all(self.mine(z), [self.mine(z), self.sib.at[z]])

    def begin(self):
        for k in (2, 1, 3, 0):
            self.swap(k)
        self.join(2)
        self.ring.start_far()
        for k in (1, 3):
            self.join(k)
            self.ring.start_near(k)
        self.join(0)

    def forward(self):
        self.ring.forward()

    def end(self):
        self.ring.end(self.out)


class SumXY:
    def __init__(self, net, p, cut, part, first, second, piece):
        self.p, self.piece = p, piece
        self.cut = cut
        x, y = (lambda k: mod(p.x + k, 4)), (lambda k: mod(p.y + k, 4))
        self.one = [
            RingSum(net, p.at_x, lambda k: cut(0, None, x(k)), part, *first[0]),
            RingSum(net, p.at_y, lambda k: cut(1, y(k), None), part, *first[1]),
        ]
        self.two = [
            RingSum(net, p.at_y, lambda k: cut(0, y(k), p.x), part, *second[0]),
            RingSum(net, p.at_x, lambda k: cut(1, p.y, x(k)), part, *second[1]),
        ]

    def start(self):
        for ring in self.one:
            ring.start()

    def forward(self):
        for ring in self.one:
            ring.forward()

    def turn(self):
        p = self.p
        for h, own in ((0, self.cut(0, None, p.x)), (1, self.cut(1, p.y, None))):
            self.one[h].end(own)
            self.two[h].start()

    def finish(self):
        for ring in self.two:
            ring.forward()

    def end(self):
        for h in (0, 1):
            self.two[h].end(self.piece(h))


def add_all(out, terms):
    *lead, rows, lanes = out.shape
    step_rows = min(rows, max(16, (24 * 1024 // lanes) // 16 * 16))
    while rows % step_rows:
        step_rows -= 16
    steps = rows // step_rows
    count = steps
    for n in lead:
        count *= n

    def step(i, carry):
        j, r = i // steps, lax.rem(i, steps)
        index = []
        for n in reversed(lead):
            index.insert(0, lax.rem(j, n))
            j = j // n
        at = (*index, pl.ds(pl.multiple_of(r * step_rows, 16), step_rows), slice(None))
        total = terms[0][at].astype(F32)
        for term in terms[1:]:
            total = total + term[at].astype(F32)
        out[at] = total.astype(out.dtype)
        return carry

    lax.fori_loop(0, count, step, 0)


def call(body, ident, outs, out_places, remotes, locals_, scratch, *args, vmem=56):
    return pl.pallas_call(
        body,
        out_shape=outs,
        in_specs=[ANY] * len(args),
        out_specs=out_places,
        scratch_shapes=[
            *scratch,
            pltpu.SemaphoreType.DMA((remotes,)),
            pltpu.SemaphoreType.DMA((remotes,)),
            pltpu.SemaphoreType.DMA((locals_,)),
        ],
        compiler_params=pltpu.CompilerParams(
            collective_id=ident, has_side_effects=True, vmem_limit_bytes=vmem << 20
        ),
    )(*args)


def shape(*dims, dtype=BF):
    return jax.ShapeDtypeStruct(dims, dtype)


def rows_of(n):
    return lambda ref, i: ref.at[pl.ds(0, n)] if i == 0 else ref.at[pl.ds(n, ref.shape[0] - n)]


def half(ref, h, n=64):
    return ref.at[pl.ds(h * n, n)]


def sum_dp_scratch(rows=BLOCK, lanes=D):
    return [
        pltpu.VMEM((ZN, rows, lanes), BF),
        pltpu.VMEM((ZN, rows, lanes), BF),
        pltpu.VMEM((rows // 2, lanes), BF),
        pltpu.VMEM((rows // 2, lanes), BF),
        pltpu.VMEM((rows, lanes), BF),
        pltpu.VMEM((rows, lanes), BF),
    ]


def sum_dp(net, p, part, scratch, out):
    mine, sib, t0, t1, g0, g1 = scratch
    cut = rows_of(sib.shape[1] // 2)
    return SumDP(net, p, part, cut, lambda z: mine.at[z], sib, (t0, t1), (g0, g1), out)


def ring_scratch(rows, lanes):
    return [pltpu.VMEM((3, n, rows, lanes), BF) for n in (2, 2, 4, 4)]


def ring_buffers(refs):
    return (refs[0], refs[1]), (refs[2], refs[3])


CHUNK = 256
CHUNKS = LENGTH // CHUNK
SCALE = HD ** (-0.5)


def span(j):
    return max(0, j * CHUNK - WINDOW), (j + 1) * CHUNK


def score_block(k, q_t, hi, j):
    low, high = span(j)
    s = jnp.dot(k[low:high, :], q_t[:, j * CHUNK : (j + 1) * CHUNK], preferred_element_type=F32)
    s = s * SCALE
    key = low + lax.broadcasted_iota(jnp.int32, s.shape, 0)
    query = j * CHUNK + lax.broadcasted_iota(jnp.int32, s.shape, 1)
    last = hi[low:high, :]
    last = jnp.concatenate([last] * (CHUNK // 128), axis=1)
    return jnp.where((query >= key) & (query <= last), s, NEG_LARGE)


def last_readers(lengths, pad):
    key = lax.broadcasted_iota(jnp.int32, (LENGTH, BLOCK), 0)
    end = jnp.int32(0)
    ends = []
    for i in range(4):
        end = end + lengths[0, i]
        ends.append(end)
    doc = jnp.full(key.shape, ends[3], jnp.int32)
    for end in reversed(ends[:3]):
        doc = jnp.where(key < end, end, doc)
    hi = jnp.minimum(key + (WINDOW - 1), doc - 1)
    return jnp.where(key >= LENGTH - pad[0, 0], key, hi)


def turn(values, cosine, sine):
    a, b = values[: HD // 2], values[HD // 2 :]
    return jnp.concatenate([a * cosine - b * sine, b * cosine + a * sine], axis=0)


def forward(
    x, pos, freq, gain_a, gain_m, w_query, w_key, w_value, w_out_t, w_gate, w_up, w_down_t, dd, lengths, pad
):
    def body(
        x, pos, freq, gain_a, gain_m, w_query, w_key, w_value, w_out_t, w_gate, w_up, w_down_t, dd, lengths, pad,
        seq, wdh, home_out, heads_out, part0, part1, ypart,
        q_t, k_t, v_t, top, total, cosine, sine, resid, dresid, da_t,
        rows, spot, w, w_t, wfp, k, att, wo, wf, cot_all, home, xv, hi, wqv, wkv, wvv, wgrp, wraw, wpiece, gain,
        hid, mixed, dgu, epart, e2, sib, t0, t1, g0, g1, grad_v, dat, heads, *rest,
    ):
        rings, (send, recv, local) = rest[:8], rest[8:]
        p = Place()
        net = Net(send, recv, local)
        net.m = 1
        load_x = net.copy(x, xv)
        at_rows = pl.ds(pl.multiple_of(p.y * 48, 16), 48)
        load_pieces = [
            net.copy(
                ref.at[at_rows, pl.ds(pl.multiple_of(f * FSH + p.x * 128, 128), 128)], wraw.at[f, i]
            )
            for i, ref in enumerate((w_gate, w_up, w_down_t))
            for f in range(DP)
        ]
        load_w = [net.copy(a, b) for a, b in ((w_query, wqv), (w_key, wkv), (w_value, wvv))]
        greet([p.at_ctx(i) for i in range(1, CTX)] + [p.at_dp(i) for i in range(1, DP)])
        rank = lax.rem(p.ctx, 2)

        def message(b):
            return pltpu.make_async_remote_copy(
                src_ref=att.at[:, pl.ds(b * BLOCK, BLOCK)],
                dst_ref=home.at[p.ctx],
                send_sem=send.at[b],
                recv_sem=recv.at[p.ctx],
                device_id=(p.dp, jnp.int32(b)),
                device_id_type=MESH,
            )

        def arrival(c):
            return pltpu.make_async_remote_copy(
                src_ref=att.at[:, pl.ds(0, BLOCK)],
                dst_ref=home.at[c],
                send_sem=send.at[c],
                recv_sem=recv.at[c],
                device_id=(p.dp, jnp.int32(c)),
                device_id_type=MESH,
            )

        def kept(b):
            return pltpu.make_async_copy(
                att.at[:, pl.ds(b * BLOCK, BLOCK)], home.at[p.ctx], local.at[0]
            )

        net.n = CTX
        load_x.wait()
        first = xv[...].astype(F32)
        inv = lax.rsqrt(jnp.mean(first * first, axis=-1, keepdims=True) + EPSILON)
        rows[p.ctx] = (first * inv).astype(BF)
        spot[p.ctx] = jnp.broadcast_to(pos[...].astype(F32), (16, BLOCK))
        spots = GatherXY(net, p, None, lambda h, y, x: spot.at[y * 4 + x, pl.ds(h * 8, 8)])
        tokens = RingXY(
            net, p, None, lambda h, y, x: rows.at[y * 4 + x, pl.ds(h * 64, 64)], rows_of(32)
        )

        gain[0] = jnp.broadcast_to(gain_a[...].astype(F32)[None], (BLOCK, SHARD)).T
        gain[1] = jnp.broadcast_to(gain_m[...].astype(F32)[None], (BLOCK, SHARD)).T
        for copy in load_w:
            copy.wait()
        scale = gain[0, :, :1]
        for g in range(HK):
            block = jnp.concatenate(
                [
                    wqv[:, g * 2 * HD : (g + 1) * 2 * HD],
                    wkv[:, g * HD : (g + 1) * HD],
                    wvv[:, g * HD : (g + 1) * HD],
                ],
                axis=1,
            )
            wgrp[g] = (block.astype(F32) * scale).astype(BF)
        job = RingDP(net, p, wgrp.at[p.ctx // 2], lambda i: w.at[i], rows_of(96))
        for copy in load_pieces:
            copy.wait()
        scale = gain[1, pl.ds(pl.multiple_of(p.y * 48, 16), 48), :]
        for f in range(DP):
            for i in (0, 1):
                wpiece[f, i] = (wraw[f, i].astype(F32) * scale).astype(BF)
            wpiece[f, 2] = wraw[f, 2]
        ffw = Exchange(net, p, lambda i: wpiece.at[i], lambda i: wfp.at[:, i])
        spots.forward()
        out = RingDP(net, p, w_out_t, lambda i: wo.at[i], rows_of(96))
        tokens.forward()
        hi[...] = last_readers(lengths, pad)
        tokens.middle()
        job.forward()
        out.forward()
        cot = RingDP(net, p, dd, lambda i: cot_all.at[i], rows_of(64))
        job.finish()
        tokens.finish()
        ffw.end()
        wts = RingXY(
            net,
            p,
            lambda h: wfp.at[:, pl.ds(4 * h, 4)],
            lambda h, y, x: wf.at[
                :,
                pl.ds(4 * h, 4),
                pl.ds(pl.multiple_of(y * 48, 16), 48),
                pl.ds(pl.multiple_of(x * 128, 128), 128),
            ],
            lambda ref, i: ref.at[:, pl.ds(2 * i, 2)],
        )
        for i in (0, 1, 3, 2):
            job.arrive(i)
        job.end(arrived=True)
        w_t[...] = w[...].reshape(D, GROUP).T
        spots.end()
        for j in range(CHUNKS):
            at = slice(j * CHUNK, (j + 1) * CHUNK)
            angles = freq[...] * jnp.concatenate(
                [spot[2 * j, :1, :], spot[2 * j + 1, :1, :]], axis=1
            )
            cosine[:, at], sine[:, at] = jnp.cos(angles), jnp.sin(angles)
        tokens.arrive()
        outs = [net.copy(rows, seq)]
        w_own = jnp.concatenate(
            [w_t[pl.ds(pl.multiple_of(rank * HD, 16), HD), :], w_t[2 * HD :, :]], axis=0
        )
        for j in range(CHUNKS):
            at = slice(j * CHUNK, (j + 1) * CHUNK)
            block = rows[2 * j : 2 * j + 2].reshape(CHUNK, D)
            cos, sin = cosine[:, at], sine[:, at]
            proj = dot(w_own, block, ((1,), (1,)))
            q_t[:, at] = turn(proj[:HD], cos, sin).astype(BF)
            key = turn(proj[HD : 2 * HD], cos, sin).astype(BF)
            k_t[:, at] = key
            k[at, :] = key.T
            v_t[:, at] = proj[2 * HD :].astype(BF)
            low, high = span(j)
            s = score_block(k, q_t, hi, j)
            m = jnp.max(s, axis=0, keepdims=True)
            e = jnp.exp(s - m)
            t = jnp.sum(e, axis=0, keepdims=True)
            prob = (e * (1.0 / t)).astype(BF)
            att[:, at] = jnp.dot(v_t[:, low:high], prob, preferred_element_type=F32).astype(BF)
            top[:, at] = m
            total[:, at] = t
            for b in (2 * j, 2 * j + 1):

                @pl.when(p.ctx == b)
                def _():
                    kept(b).start()

                @pl.when(p.ctx != b)
                def _():
                    message(b).start()

            if j == 1:
                wts.forward()
            if j == 2:
                out.finish()
                cot.forward()
            if j == 4:
                wts.middle()
            if j == 3:
                cot.finish()
        wts.finish()
        for i in (0, 1, 3, 2):
            out.arrive(i)
        for b in range(CTX):

            @pl.when(p.ctx == b)
            def _():
                kept(b).wait()

            @pl.when(p.ctx != b)
            def _():
                message(b).wait_send()
                arrival(b).wait_recv()

        own = home[...].reshape(D, BLOCK).T
        y1 = xv[...].astype(F32) + dot(own, wo[...].reshape(D, D), ((1,), (1,)))
        resid[...] = y1
        inv = lax.rsqrt(jnp.mean(y1 * y1, axis=-1, keepdims=True) + EPSILON)
        hid[p.dp] = (y1 * inv).astype(BF)
        ring = RingDP(net, p, None, lambda i: hid.at[i], rows_of(64))
        for i in (0, 1, 3, 2):
            cot.arrive(i)
        w_gate, w_up, w_down = (wf.at[i] for i in range(3))
        sums = SumDP(
            net, p, lambda i: epart.at[i], rows_of(64), lambda z: epart.at[2 * z + p.core], sib,
            (t0, t1), (g0, g1), e2, load=False,
        )

        def work(k):
            z = mod(p.z + k, 4)
            pair = pl.ds(2 * z, 2)
            block = hid[pair].reshape(2 * BLOCK, D)
            wg, wu = w_gate[...].reshape(D, FSH), w_up[...].reshape(D, FSH)
            gate = jnp.dot(block, wg, preferred_element_type=F32)
            up = jnp.dot(block, wu, preferred_element_type=F32)
            sig = jax.nn.sigmoid(gate)
            act = gate * sig
            mixed[pair] = (act * up).astype(BF).reshape(2, BLOCK, FSH)
            wd = w_down[...].reshape(D, FSH)
            dmix = jnp.dot(cot_all[pair].reshape(2 * BLOCK, D), wd, preferred_element_type=F32)
            dg = (dmix * up * sig * (1.0 + gate * (1.0 - sig))).astype(BF)
            du = (dmix * act).astype(BF)
            dgu[pair, :, :FSH] = dg.reshape(2, BLOCK, FSH)
            dgu[pair, :, FSH:] = du.reshape(2, BLOCK, FSH)
            e = dot(dg, wg, ((1,), (1,))) + dot(du, wu, ((1,), (1,)))
            epart[pair] = e.astype(BF).reshape(2, BLOCK, D)
            sums.swap(k)

        wts.arrive()
        ring.arrive(0)
        work(0)
        ring.forward()
        ring.arrive(1)
        work(3)
        ring.finish()
        ring.arrive(3)
        work(1)
        sums.join(3)
        sums.ring.start_near(3)
        ring.arrive(2)
        work(2)
        sums.join(1)
        sums.ring.start_near(1)
        sums.join(2)
        sums.ring.start_far()
        outs.append(net.copy(home, home_out))

        def weights(left, right, *which):
            right = right[...].reshape(DP * BLOCK, FSH * len(which))
            for c in range(4):
                block = left[:, :, c * 384 : (c + 1) * 384].reshape(DP * BLOCK, 384).T
                grad = jnp.dot(block, right, preferred_element_type=F32).astype(BF)
                for n, i in enumerate(which):
                    part = grad[:, n * FSH : (n + 1) * FSH]
                    grad_v[i, 2 * c : 2 * c + 2] = part.reshape(2, SHARD, FSH)

        weights(hid, dgu, 0, 1)
        weights(cot_all, mixed, 2)

        def quarter(ref, i):
            return ref.at[:, pl.ds(2 * i, 2)]

        def column(k):
            lanes = pl.ds(pl.multiple_of(mod(p.x + k, 4) * 128, 128), 128)
            return grad_v.at[:, pl.ds(0, 4), :, lanes]

        def band(k):
            at = pl.ds(pl.multiple_of(mod(p.y + k, 4) * 48, 16), 48)
            return grad_v.at[:, pl.ds(4, 4), at, :]

        ring_x = RingSum(net, p.at_x, column, quarter, *ring_buffers(rings[:4]))
        ring_y = RingSum(net, p.at_y, band, quarter, *ring_buffers(rings[4:]))
        ring_x.start()
        ring_y.start()
        sums.join(0)
        sums.forward()
        sums.end()
        y1 = resid[...]
        inv = lax.rsqrt(jnp.mean(y1 * y1, axis=-1, keepdims=True) + EPSILON)
        u2 = y1 * inv
        e = e2[...]
        d = cot_all[p.dp].astype(F32) + inv * (e - u2 * jnp.mean(e * u2, axis=-1, keepdims=True))
        dresid[...] = d
        da = d.astype(BF)
        grad = jnp.dot(da, wo[...].reshape(D, D), preferred_element_type=F32).astype(BF)
        dat[...] = grad.T.reshape(CTX, HD, BLOCK)
        sent = [
            net.remote(dat.at[mod(p.ctx + i, CTX)], heads.at[p.ctx], p.at_ctx(i))
            for i in range(1, CTX)
        ]
        kept_dat = net.copy(dat.at[p.ctx], heads.at[p.ctx])
        grp = Exchange(net, p, lambda i: wgrp.at[i], lambda i: wdh.at[i])
        ring_x.forward()
        ring_y.forward()
        da_t[...] = da.T.reshape(DP, SHARD, BLOCK)
        wd = w_down[...].reshape(D, FSH)
        for z in range(ZN):
            y = dot(mixed[2 * z : 2 * z + 2].reshape(2 * BLOCK, FSH), wd, ((1,), (1,)))
            epart[2 * z : 2 * z + 2] = y.astype(BF).reshape(2, BLOCK, D)
        outs.append(net.copy(epart, ypart))
        kept_dat.wait()
        for copy in sent:
            copy.wait()
        outs.append(net.copy(heads, heads_out))
        ring_x.end(column(0))
        outs.append(net.copy(column(0), part0))
        ring_y.end(band(0))
        outs.append(net.copy(band(0), part1))
        for part in (out, cot, ring):
            part.end(arrived=True)
        grp.end()
        tokens.end()
        wts.end()
        for copy in outs:
            copy.wait()

    block = (DP, BLOCK, D)
    head = shape(HD, LENGTH)
    line = shape(1, LENGTH, dtype=F32)
    angle = shape(HD // 2, LENGTH, dtype=F32)
    wide = shape(BLOCK, D, dtype=F32)
    return pl.pallas_call(
        body,
        out_shape=(
            shape(CTX, BLOCK, D),
            shape(DP, SHARD, GROUP),
            shape(CTX, HD, BLOCK),
            shape(CTX, HD, BLOCK),
            shape(3, 4, SHARD, 128),
            shape(3, 4, 48, FSH),
            shape(*block),
            head,
            head,
            head,
            line,
            line,
            angle,
            angle,
            wide,
            wide,
            shape(DP, SHARD, BLOCK),
        ),
        in_specs=[ANY, VMEM, VMEM, VMEM, VMEM, *[ANY] * 8, SMEM, SMEM],
        out_specs=[ANY] * 7 + [VMEM] * 10,
        scratch_shapes=[
            pltpu.VMEM((CTX, BLOCK, D), BF),
            pltpu.VMEM((CTX, 16, BLOCK), F32),
            pltpu.VMEM((DP, SHARD, GROUP), BF),
            pltpu.VMEM((GROUP, D), BF),
            pltpu.VMEM((3, DP, 48, 128), BF),
            pltpu.VMEM((LENGTH, HD), BF),
            pltpu.VMEM((HD, LENGTH), BF),
            pltpu.VMEM((DP, SHARD, D), BF),
            pltpu.VMEM((3, DP, SHARD, FSH), BF),
            pltpu.VMEM(block, BF),
            pltpu.VMEM((CTX, HD, BLOCK), BF),
            pltpu.VMEM((BLOCK, D), BF),
            pltpu.VMEM((LENGTH, BLOCK), jnp.int32),
            pltpu.VMEM((SHARD, D), BF),
            pltpu.VMEM((SHARD, HK * HD), BF),
            pltpu.VMEM((SHARD, HK * HD), BF),
            pltpu.VMEM((DP, SHARD, GROUP), BF),
            pltpu.VMEM((DP, 3, 48, 128), BF),
            pltpu.VMEM((DP, 3, 48, 128), BF),
            pltpu.VMEM((2, SHARD, BLOCK), F32),
            pltpu.VMEM(block, BF),
            pltpu.VMEM((DP, BLOCK, FSH), BF),
            pltpu.VMEM((DP, BLOCK, 2 * FSH), BF),
            pltpu.VMEM(block, BF),
            pltpu.VMEM((BLOCK, D), F32),
            pltpu.VMEM((ZN, BLOCK, D), BF),
            pltpu.VMEM((BLOCK // 2, D), BF),
            pltpu.VMEM((BLOCK // 2, D), BF),
            pltpu.VMEM((BLOCK, D), BF),
            pltpu.VMEM((BLOCK, D), BF),
            pltpu.VMEM((3, DP, SHARD, FSH), BF),
            pltpu.VMEM((CTX, HD, BLOCK), BF),
            pltpu.VMEM((CTX, HD, BLOCK), BF),
            *ring_scratch(SHARD, 128),
            *ring_scratch(48, FSH),
            pltpu.SemaphoreType.DMA((213,)),
            pltpu.SemaphoreType.DMA((213,)),
            pltpu.SemaphoreType.DMA((48,)),
        ],
        compiler_params=pltpu.CompilerParams(
            collective_id=2, has_side_effects=True, vmem_limit_bytes=60 << 20
        ),
    )(
        x, pos, freq, gain_a, gain_m, w_query, w_key, w_value, w_out_t, w_gate, w_up, w_down_t, dd, lengths, pad
    )


def backward(heads, att, da_t, part0, part1, ypart, wdh, seq, q_t, k_t, v_t, top, total, cosine, sine, lengths, pad):
    def body(
        heads, att, da_t, part0, part1, ypart, wdh, seq, q_t, k_t, v_t, top, total, cosine, sine, lengths, pad,
        e1, ysum, gff, gatt,
        hi, rows, k, v, q, do, do_t, dk, dv, out, wide, heads_v, att_all, da_all, dwj, full, away, comb,
        dwo, w0, f0, s0, back, wdh_v, dh1, wide0, wide1, piece, grads, *rest,
    ):
        rings, rest = rest[:8], rest[8:]
        j_sib, j_t0, j_t1, j_g0, j_g1, *rest = rest
        h_sib, h_t0, h_t1, h_g0, h_g1, *rest = rest
        y_scratch, (send, recv, local) = rest[:6], rest[6:]
        p = Place()
        net = Net(send, recv, local)
        group, rank = p.ctx // 2, lax.rem(p.ctx, 2)
        home = group == p.dp
        partner = (p.dp, p.ctx + 1 - 2 * rank)

        barrier = pltpu.get_barrier_semaphore()
        others = xy_peers(p) + [p.at_dp(i) for i in range(1, DP)]
        for peer in others:
            pl.semaphore_signal(barrier, inc=1, device_id=peer, device_id_type=MESH)
        for i in range(DP):
            for r in range(2):

                @pl.when(jnp.logical_not(home & (p.dp == i) & (rank == r)))
                def _():
                    peer = (jnp.int32(i), 2 * p.dp + r)
                    pl.semaphore_signal(barrier, inc=1, device_id=peer, device_id_type=MESH)

        pl.semaphore_wait(barrier, CTX + len(others) - home.astype(jnp.int32))

        slot = p.dp * 2 + rank

        def lanes_of(b):
            at = b * BLOCK
            return pl.ds(at if isinstance(b, int) else pl.multiple_of(at, BLOCK), BLOCK)

        def message(b, spot):
            return pltpu.make_async_remote_copy(
                src_ref=out.at[:, lanes_of(b)],
                dst_ref=back.at[spot],
                send_sem=send.at[b],
                recv_sem=recv.at[spot],
                device_id=(group, jnp.int32(b)),
                device_id_type=MESH,
            )

        def own(b):
            return pltpu.make_async_copy(
                out.at[:, lanes_of(b)], back.at[slot], local.at[0]
            )

        net.n, net.m = CTX, 1

        load_wide = [net.copy(part0, wide0), net.copy(part1, wide1)]
        load_heads = net.copy(heads, heads_v)
        das = Exchange(net, p, lambda i: da_t.at[i], lambda i: da_all.at[i])
        load_rows = net.copy(seq, rows)
        atts = RingDP(net, p, att, lambda i: att_all.at[i], rows_of(D // 2))
        load_wdh = net.copy(wdh, wdh_v)

        def quarter(ref, i):
            return ref.at[:, pl.ds(2 * i, 2)]

        def band(k):
            return wide0.at[:, :, pl.ds(pl.multiple_of(mod(p.y + k, 4) * 48, 16), 48), :]

        def column(k):
            return wide1.at[:, :, :, pl.ds(pl.multiple_of(mod(p.x + k, 4) * 128, 128), 128)]

        ring_y = RingSum(net, p.at_y, band, quarter, *ring_buffers(rings[:4]))
        ring_x = RingSum(net, p.at_x, column, quarter, *ring_buffers(rings[4:]))
        for copy in load_wide:
            copy.wait()
        ring_y.start()
        ring_x.start()
        res = sum_dp(net, p, lambda i: ypart.at[i], y_scratch, ysum)
        for i in (2, 1, 3, 0):
            res.swap(i)
        k[...] = k_t[...].T
        v[...] = v_t[...].T
        ring_y.forward()
        ring_x.forward()
        q[...] = q_t[...].T
        hi[...] = last_readers(lengths, pad)
        dk[...] = jnp.zeros_like(dk)
        dv[...] = jnp.zeros_like(dv)
        ring_y.end(piece.at[:, pl.ds(0, 4)])
        ring_x.end(piece.at[:, pl.ds(4, 4)])
        swap = Exchange(net, p, lambda i: piece.at[:, i], lambda i: grads.at[i])
        load_heads.wait()
        for b in range(CTX):
            do_t[:, b * BLOCK : (b + 1) * BLOCK] = heads_v[b]
        do[...] = do_t[...].T

        def chunk(j):
            low, high = span(j)
            at = slice(j * CHUNK, (j + 1) * CHUNK)
            s = score_block(k, q_t, hi, j)
            prob = jnp.exp(s - top[:, at]) * (1.0 / total[:, at])
            dp = jnp.dot(v[low:high, :], do_t[:, at], preferred_element_type=F32)
            inner = jnp.sum(prob * dp, axis=0, keepdims=True)
            ds = (prob * (dp - inner)).astype(BF)
            dq = jnp.dot(k_t[:, low:high], ds, preferred_element_type=F32) * SCALE
            dk[low:high, :] += jnp.dot(ds, q[at, :], preferred_element_type=F32)
            dv[low:high, :] += jnp.dot(prob.astype(BF), do[at, :], preferred_element_type=F32)
            cos, sin = cosine[:, at], -sine[:, at]
            out[:HD, at] = turn(dq, cos, sin).astype(BF)
            out[HD : 2 * HD, at] = turn(dk[at, :].T * SCALE, cos, sin).astype(BF)
            out[2 * HD :, at] = dv[at, :].T.astype(BF)

        def depart(first):
            for i in range(8):
                b = first + lax.rem(p.ctx + i, 8)
                here = home & (p.ctx == b)

                @pl.when(here)
                def _():
                    own(b).start()

                @pl.when(jnp.logical_not(here))
                def _():
                    message(b, slot).start()

        gather = None
        for j in reversed(range(CHUNKS)):
            chunk(j)
            if j in (4, 0):
                depart(2 * j)
            if j == 5:
                swap.end()
                gather = RingXY(
                    net,
                    p,
                    lambda h: grads.at[pl.ds(4 * h, 4)],
                    lambda h, y, x: gff.at[
                        pl.ds(4 * h, 4),
                        :,
                        pl.ds(pl.multiple_of(y * 48, 16), 48),
                        pl.ds(pl.multiple_of(x * 128, 128), 128),
                    ],
                    rows_of(2),
                )
            if j == 3:
                atts.forward()
            if j == 2:
                for i in (2, 1, 3, 0):
                    res.join(i)

        mine = pl.multiple_of(rank * HD, 16)
        other = pl.multiple_of((1 - rank) * HD, 16)
        wide[pl.ds(mine, HD), :] = out[:HD, :]
        wide[pl.ds(other, HD), :] = jnp.zeros((HD, LENGTH), BF)
        wide[2 * HD :, :] = out[HD:, :]
        load_rows.wait()
        grad = jnp.dot(wide[...], rows[...].reshape(LENGTH, D), preferred_element_type=F32)
        dwj[...] = grad.T.astype(BF).reshape(DP, SHARD, GROUP)
        proj = SumDP(
            net, p, lambda i: dwj.at[i], rows_of(96), lambda z: dwj.at[2 * z + p.core], j_sib,
            (j_t0, j_t1), (j_g0, j_g1), full, load=False,
        )
        proj.begin()
        gather.forward()
        atts.finish()

        das.end()
        for i in (0, 1, 3, 2):
            atts.arrive(i)
        atts.end(arrived=True)
        grad = dot(da_all[0], att_all[0], ((1,), (1,)))
        for i in range(1, DP):
            grad += dot(da_all[i], att_all[i], ((1,), (1,)))
        dwo[...] = grad.astype(BF)
        wide_cuts = [net.copy(dwo.at[:, pl.ds(pl.multiple_of(p.x * 384, 128), 384)], w0)]
        for i in (1, 3, 2):
            lanes = pl.ds(pl.multiple_of(mod(p.x + i, 4) * 384, 128), 384)
            wide_cuts.append(net.remote(dwo.at[:, lanes], f0.at[i - 1], p.at_x(i)))
        gather.middle()
        proj.forward()

        load_wdh.wait()
        inp = SumDP(
            net, p, lambda i: dh1.at[i], rows_of(64), lambda z: dh1.at[2 * z + p.core], h_sib,
            (h_t0, h_t1), (h_g0, h_g1), e1, load=False,
        )
        for spot in range(CTX):

            @pl.when(jnp.logical_not(home & (slot == spot)))
            def _():
                message(0, spot).wait_recv()

        for b in range(CTX):
            here = home & (p.ctx == b)

            @pl.when(here)
            def _():
                own(b).wait()

            @pl.when(jnp.logical_not(here))
            def _():
                message(b, slot).wait_send()

        def inputs(step):
            z = mod(p.z + step, 4)
            turned = []
            for core in (0, 1):
                i = 2 * z + core
                first, second = back[2 * i].astype(F32), back[2 * i + 1].astype(F32)
                both = jnp.concatenate([first[:HD], second[:HD], first[HD:] + second[HD:]], axis=0)
                turned.append(both.T.astype(BF))
            turned = jnp.concatenate(turned, axis=0)
            grad = dot(turned, wdh_v[...].reshape(D, GROUP), ((1,), (1,)))
            dh1[pl.ds(2 * z, 2)] = grad.astype(BF).reshape(2, BLOCK, D)
            inp.swap(step)

        inputs(2)
        inputs(1)
        inp.join(2)
        inp.ring.start_far()
        inputs(3)
        inp.join(1)
        inp.ring.start_near(1)
        inputs(0)
        inp.join(3)
        inp.ring.start_near(3)
        proj.end()
        theirs = full.at[pl.ds(pl.multiple_of((1 - rank) * 96, 16), 96)]
        trade = net.remote(theirs, away, partner)
        for copy in wide_cuts:
            copy.wait()
        add_all(w0, [w0] + [f0.at[i] for i in range(3)])
        tall = []
        for i in (1, 3, 2):
            at = pl.ds(pl.multiple_of(mod(p.y + i, 4) * 48, 16), 48)
            tall.append(net.remote(w0.at[at], s0.at[i - 1], p.at_y(i)))
        gather.finish()
        inp.join(0)
        inp.forward()
        res.ring.start_far()
        for i in (1, 3):
            res.ring.start_near(i)
        trade.wait()
        add_all(
            comb.at[pl.ds(0, 96)], [full.at[pl.ds(pl.multiple_of(rank * 96, 16), 96)], away]
        )
        for copy in tall:
            copy.wait()
        at = pl.ds(pl.multiple_of(p.y * 48, 16), 48)
        add_all(comb.at[pl.ds(96, 48)], [w0.at[at]] + [s0.at[i] for i in range(3)])
        small = RingXY(
            net,
            p,
            lambda h: comb.at[pl.ds(80 * h, 80 - 16 * h)],
            lambda h, y, x: gatt.at[y * 4 + x, pl.ds(80 * h, 80 - 16 * h)],
            rows_of(48),
        )
        inp.end()
        small.forward()
        res.forward()
        small.middle()
        small.finish()
        res.end()
        for part in (gather, small):
            part.arrive()
            part.end()

    head = pltpu.VMEM((LENGTH, HD), BF)
    return pl.pallas_call(
        body,
        out_shape=(
            shape(BLOCK, D, dtype=F32),
            shape(BLOCK, D, dtype=F32),
            shape(DP, 3, SHARD, FSH),
            shape(CTX, 144, GROUP),
        ),
        in_specs=[ANY] * 8 + [VMEM] * 7 + [SMEM] * 2,
        out_specs=[VMEM, VMEM, ANY, ANY],
        scratch_shapes=[
            pltpu.VMEM((LENGTH, BLOCK), jnp.int32),
            pltpu.VMEM((CTX, BLOCK, D), BF),
            head,
            head,
            head,
            head,
            pltpu.VMEM((HD, LENGTH), BF),
            pltpu.VMEM((LENGTH, HD), F32),
            pltpu.VMEM((LENGTH, HD), F32),
            pltpu.VMEM((3 * HD, LENGTH), BF),
            pltpu.VMEM((GROUP, LENGTH), BF),
            pltpu.VMEM((CTX, HD, BLOCK), BF),
            pltpu.VMEM((DP, D, BLOCK), BF),
            pltpu.VMEM((DP, SHARD, BLOCK), BF),
            pltpu.VMEM((DP, SHARD, GROUP), BF),
            pltpu.VMEM((SHARD, GROUP), BF),
            pltpu.VMEM((96, GROUP), BF),
            pltpu.VMEM((144, GROUP), BF),
            pltpu.VMEM((SHARD, D), BF),
            pltpu.VMEM((SHARD, 384), BF),
            pltpu.VMEM((3, SHARD, 384), BF),
            pltpu.VMEM((3, 48, 384), BF),
            pltpu.VMEM((CTX, 3 * HD, BLOCK), BF),
            pltpu.VMEM((DP, SHARD, GROUP), BF),
            pltpu.VMEM((DP, BLOCK, D), BF),
            pltpu.VMEM((3, 4, SHARD, 128), BF),
            pltpu.VMEM((3, 4, 48, FSH), BF),
            pltpu.VMEM((3, DP, 48, 128), BF),
            pltpu.VMEM((DP, 3, 48, 128), BF),
            *ring_scratch(48, 128),
            *ring_scratch(48, 128),
            *sum_dp_scratch(SHARD, GROUP)[1:],
            *sum_dp_scratch()[1:],
            *sum_dp_scratch(),
            pltpu.SemaphoreType.DMA((169,)),
            pltpu.SemaphoreType.DMA((169,)),
            pltpu.SemaphoreType.DMA((24,)),
        ],
        compiler_params=pltpu.CompilerParams(
            collective_id=4, has_side_effects=True, vmem_limit_bytes=60 << 20
        ),
    )(heads, att, da_t, part0, part1, ypart, wdh, seq, q_t, k_t, v_t, top, total, cosine, sine, lengths, pad)


def finish(gff, gatt, gain_a, gain_m, w_gate, w_up, w_query, w_key, w_value):
    def body(
        gff, gatt, gain_a, gain_m, w_gate, w_up, w_query, w_key, w_value,
        gate, up, down, dq, dk, dv, do, dgain_a, dgain_m,
        gv, gv_att, wg, wu, wq, wk, wv, ov, oq, ok, ow, oo, load, store,
    ):
        lanes = [pl.ds(f * FSH, FSH) for f in range(DP)]
        loads, stores = [], []

        def fetch(*pairs):
            copies = [
                pltpu.make_async_copy(a, b, load.at[len(loads) + i]) for i, (a, b) in enumerate(pairs)
            ]
            loads.extend(copies)
            for copy in copies:
                copy.start()
            return copies

        def put(a, b):
            copy = pltpu.make_async_copy(a, b, store.at[len(stores)])
            stores.append(copy)
            copy.start()

        steps = [
            fetch(
                (gff.at[f], gv.at[f]),
                (w_gate.at[:, lanes[f]], wg.at[:, lanes[f]]),
                (w_up.at[:, lanes[f]], wu.at[:, lanes[f]]),
            )
            for f in range(DP)
        ]
        rest = fetch((gatt, gv_att), (w_query, wq), (w_key, wk), (w_value, wv))

        def column(gain):
            return jnp.broadcast_to(gain[...].astype(F32)[None], (BLOCK, SHARD)).T[:, :1]

        def line(total):
            return jnp.broadcast_to(total, (SHARD, BLOCK)).T[0]

        rows = column(gain_m)
        total = jnp.zeros((SHARD, FSH), F32)
        for f in range(DP):
            for copy in steps[f]:
                copy.wait()
            g, u = gv[f, 0].astype(F32), gv[f, 1].astype(F32)
            total += g * wg[:, lanes[f]].astype(F32) + u * wu[:, lanes[f]].astype(F32)
            ov[0, :, lanes[f]] = g * rows
            ov[1, :, lanes[f]] = u * rows
            ov[2, :, lanes[f]] = gv[f, 2].astype(F32)
            for i, out in enumerate((gate, up, down)):
                put(ov.at[i, :, lanes[f]], out.at[:, lanes[f]])
        dgain_m[...] = line(jnp.sum(total, axis=1, keepdims=True))
        for copy in rest:
            copy.wait()
        rows = column(gain_a)
        for c in range(CTX):
            y, x = divmod(c, 4)
            oo[y * 48 : (y + 1) * 48, x * 384 : (x + 1) * 384] = gv_att[c, 96:].astype(F32)
        put(oo, do)
        for g in range(HK):
            block = gv_att[2 * g : 2 * g + 2, :96].reshape(SHARD, GROUP).astype(F32)
            oq[:, g * 2 * HD : (g + 1) * 2 * HD] = block[:, : 2 * HD]
            ok[:, g * HD : (g + 1) * HD] = block[:, 2 * HD : 3 * HD]
            ow[:, g * HD : (g + 1) * HD] = block[:, 3 * HD :]
        total = jnp.zeros((SHARD, 1), F32)
        for grad, weight, out in ((oq, wq, dq), (ok, wk, dk), (ow, wv, dv)):
            total += jnp.sum(grad[...] * weight[...].astype(F32), axis=1, keepdims=True)
            grad[...] = grad[...] * rows
            put(grad, out)
        dgain_a[...] = line(total)
        for copy in stores:
            copy.wait()

    big = shape(SHARD, FF, dtype=F32)
    square = shape(SHARD, D, dtype=F32)
    small = shape(SHARD, HK * HD, dtype=F32)
    row = shape(SHARD, dtype=F32)
    return pl.pallas_call(
        body,
        out_shape=(big, big, big, square, small, small, square, row, row),
        in_specs=[ANY, ANY, VMEM, VMEM] + [ANY] * 5,
        out_specs=[ANY] * 7 + [VMEM] * 2,
        scratch_shapes=[
            pltpu.VMEM((DP, 3, SHARD, FSH), BF),
            pltpu.VMEM((CTX, 144, GROUP), BF),
            pltpu.VMEM((SHARD, FF), BF),
            pltpu.VMEM((SHARD, FF), BF),
            pltpu.VMEM((SHARD, D), BF),
            pltpu.VMEM((SHARD, HK * HD), BF),
            pltpu.VMEM((SHARD, HK * HD), BF),
            pltpu.VMEM((3, SHARD, FF), F32),
            pltpu.VMEM((SHARD, D), F32),
            pltpu.VMEM((SHARD, HK * HD), F32),
            pltpu.VMEM((SHARD, HK * HD), F32),
            pltpu.VMEM((SHARD, D), F32),
            pltpu.SemaphoreType.DMA((28,)),
            pltpu.SemaphoreType.DMA((28,)),
        ],
        compiler_params=pltpu.CompilerParams(vmem_limit_bytes=56 << 20),
    )(gff, gatt, gain_a, gain_m, w_gate, w_up, w_query, w_key, w_value)


def dot(left, right, contract):
    return lax.dot_general(left, right, (contract, ((), ())), preferred_element_type=F32)


def on_device(
    layer_input,
    cotangent,
    attn_gain,
    w_query,
    w_key,
    w_value,
    w_out,
    mlp_gain,
    w_gate,
    w_up,
    w_down,
    doc_lengths,
    rope_pos,
    pad_lengths,
):
    inputs = layer_input[0].astype(F32)
    inv_one = lax.rsqrt(jnp.mean(inputs * inputs, axis=-1, keepdims=True) + EPSILON)
    u1 = inputs * inv_one
    freq = np.float32(THETA_BASE) ** (-(np.arange(HD // 2, dtype=np.float32) * np.float32(2.0) / np.float32(HD)))
    pad = pad_lengths[:, None]
    (
        seq, wdh, att, heads, part0, part1, ypart,
        q_t, k_t, v_t, top, total, cosine, sine, resid, dresid, da_t,
    ) = forward(
        layer_input[0], rope_pos, jnp.asarray(freq[:, None]), attn_gain, mlp_gain,
        w_query, w_key, w_value, w_out.T, w_gate, w_up, w_down.T, cotangent[0], doc_lengths, pad,
    )
    e1, ysum, gff, gatt = backward(
        heads, att.reshape(D, BLOCK), da_t, part0, part1, ypart, wdh,
        seq, q_t, k_t, v_t, top, total, cosine, sine, doc_lengths, pad,
    )
    output = (resid + ysum).astype(BF)
    grad_in = dresid + inv_one * (e1 - u1 * jnp.mean(e1 * u1, axis=-1, keepdims=True))

    dwg, dwu, dwd, dwq, dwk, dwv, dwo, dgain_a, dgain_m = finish(
        gff, gatt, attn_gain, mlp_gain, w_gate, w_up, w_query, w_key, w_value
    )
    return (
        output[None],
        grad_in.astype(BF)[None],
        dgain_a,
        dwq,
        dwk,
        dwv,
        dwo.T,
        dgain_m,
        dwg,
        dwu,
        dwd.T,
    )


def solution(mesh):
    in_specs = (
        P("dp", "ctx", None),
        P("dp", "ctx", None),
        P("dp"),
        P("dp", None),
        P("dp", None),
        P("dp", None),
        P(None, "dp"),
        P("dp"),
        P("dp", None),
        P("dp", None),
        P(None, "dp"),
        P("dp", None),
        P("dp", "ctx"),
        P("dp"),
    )
    out_specs = (
        P("dp", "ctx", None),
        P("dp", "ctx", None),
        P("dp"),
        P("dp", None),
        P("dp", None),
        P("dp", None),
        P(None, "dp"),
        P("dp"),
        P("dp", None),
        P("dp", None),
        P(None, "dp"),
    )
    return jax.shard_map(
        on_device, mesh=mesh, in_specs=in_specs, out_specs=out_specs, check_vma=False
    )
```

```python
import functools

import jax
import jax.numpy as jnp
import numpy as np
from jax import lax
from jax.experimental import pallas as pl
from jax.experimental.pallas import tpu as pltpu
from jax.sharding import PartitionSpec as P

HQ = 16
HK = 8
HD = 96
WINDOW = 1024
D = 1536
FF = 4096
BLOCK = 128
LENGTH = 2048
DP = 8
CTX = 16
ZN = 4
SHARD = D // DP
FSH = FF // DP
GROUP = 4 * HD

EPSILON = 1e-05
THETA_BASE = 100000.0
NEG_LARGE = -1e30

BF = jnp.bfloat16
F32 = jnp.float32
MESH = pl.DeviceIdType.MESH
ANY = pl.BlockSpec(memory_space=pl.ANY)
VMEM = pl.BlockSpec(memory_space=pltpu.VMEM)
SMEM = pl.BlockSpec(memory_space=pltpu.SMEM)


def mod(a, n):
    return lax.rem(a + n, n)


class Place:
    def __init__(self):
        self.dp = lax.axis_index("dp")
        self.ctx = lax.axis_index("ctx")
        self.z, self.core = self.dp // 2, lax.rem(self.dp, 2)
        self.y, self.x = self.ctx // 4, lax.rem(self.ctx, 4)

    def at_x(self, k):
        return (self.dp, self.y * 4 + mod(self.x + k, 4))

    def at_y(self, k):
        return (self.dp, mod(self.y + k, 4) * 4 + self.x)

    def at_z(self, k):
        return (mod(self.z + k, 4) * 2 + self.core, self.ctx)

    def at_dp(self, k):
        return (mod(self.dp + k, DP), self.ctx)

    def at_ctx(self, k):
        return (self.dp, mod(self.ctx + k, CTX))

    def sibling(self):
        return (self.z * 2 + 1 - self.core, self.ctx)


class Sent:
    def __init__(self, copy, net, i):
        self.copy, self.net, self.i = copy, net, i

    def wait_send(self):
        self.copy.wait_send()
        self.net.free.append(self.i)

    def wait_recv(self):
        self.copy.wait_recv()

    def wait(self):
        self.wait_send()
        self.wait_recv()


class Net:
    def __init__(self, send, recv, local):
        self.send, self.recv, self.local = send, recv, local
        self.n, self.m, self.top, self.free = 0, 0, CTX, []

    def remote(self, src, dst, peer):
        assert self.n < self.recv.shape[0]
        if not self.free:
            assert self.top < self.send.shape[0], self.top
            self.free.append(self.top)
            self.top += 1
        i = self.free.pop()
        copy = pltpu.make_async_remote_copy(
            src_ref=src,
            dst_ref=dst,
            send_sem=self.send.at[i],
            recv_sem=self.recv.at[self.n],
            device_id=peer,
            device_id_type=MESH,
        )
        self.n += 1
        copy.start()
        return Sent(copy, self, i)

    def copy(self, src, dst):
        assert self.m < self.local.shape[0]
        copy = pltpu.make_async_copy(src, dst, self.local.at[self.m])
        self.m += 1
        copy.start()
        return copy


def greet(peers):
    barrier = pltpu.get_barrier_semaphore()
    for peer in peers:
        pl.semaphore_signal(barrier, inc=1, device_id=peer, device_id_type=MESH)
    pl.semaphore_wait(barrier, len(peers))


def xy_peers(p):
    return [p.at_x(k) for k in (1, 2, 3)] + [p.at_y(k) for k in (1, 2, 3)]


def z_peers(p):
    return [p.at_z(k) for k in (1, 2, 3)] + [p.sibling()]


class GatherXY:
    def __init__(self, net, p, own, slot):
        self.net, self.p, self.slot = net, p, slot
        if own is None:
            own, self.kept = (lambda h: slot(h, p.y, p.x)), []
        else:
            self.kept = [net.copy(own(h), slot(h, p.y, p.x)) for h in (0, 1)]
        self.first, self.rest = {}, []
        for k in (1, 2, 3):
            for h in (0, 1):
                here = slot(h, p.y, p.x)
                along = net.remote(own(h), here, p.at_x(k) if h == 0 else p.at_y(k))
                self.first[h, k] = along
        for k in (1, 2, 3):
            for h in (0, 1):
                here = slot(h, p.y, p.x)
                self.rest.append(net.remote(own(h), here, p.at_y(k) if h == 0 else p.at_x(k)))

    def forward(self):
        net, p = self.net, self.p
        for k in (1, 3, 2):
            for h in (0, 1):
                self.first[h, k].wait_recv()
                if h == 0:
                    block = self.slot(0, p.y, mod(p.x - k, 4))
                else:
                    block = self.slot(1, mod(p.y - k, 4), p.x)
                for m in (1, 2, 3):
                    self.rest.append(net.remote(block, block, p.at_y(m) if h == 0 else p.at_x(m)))

    def end(self):
        for copy in self.first.values():
            copy.wait_send()
        for copy in self.rest:
            copy.wait()
        for copy in self.kept:
            copy.wait()


class Exchange:
    def __init__(self, net, p, src, slot):
        self.kept = net.copy(src(p.dp), slot(p.dp))
        self.sent = [net.remote(src(mod(p.dp + k, DP)), slot(p.dp), p.at_dp(k)) for k in range(1, DP)]

    def end(self):
        for copy in self.sent:
            copy.wait()
        self.kept.wait()


def near_peers(p):
    return [p.at_x(1), p.at_x(3), p.at_y(1), p.at_y(3)]


def near_z(p):
    return [p.at_z(1), p.at_z(3), p.sibling()]


class RingXY:
    def __init__(self, net, p, own, slot, part):
        self.net, self.p, self.part = net, p, part
        self.spot = lambda h, a, b: slot(h, b, a) if h == 0 else slot(h, a, b)
        self.me = [(p.x, p.y), (p.y, p.x)]
        self.first = [p.at_x, p.at_y]
        self.second = [p.at_y, p.at_x]
        if own is None:
            own, self.kept = (lambda h: self.spot(h, *self.me[h])), []
        else:
            self.kept = [net.copy(own(h), self.spot(h, *self.me[h])) for h in (0, 1)]
        self.near, self.far, self.side, self.last = {}, {}, {}, []
        for k in (1, 3):
            for h in (0, 1):
                here = self.spot(h, *self.me[h])
                self.near[h, k] = net.remote(own(h), here, self.first[h](k))
        for k in (1, 3):
            for h in (0, 1):
                here = self.spot(h, *self.me[h])
                self.side[h, 0, k] = net.remote(own(h), here, self.second[h](k))

    def send(self, h, a, block):
        for k in (1, 3):
            self.side[h, a, k] = self.net.remote(block, block, self.second[h](k))

    def relay(self, h, a):
        mine, other = self.me[h]
        for k in (1, 3):
            self.side[h, a, k].wait_recv()
            block = self.part(self.spot(h, mod(mine + a, 4), mod(other - k, 4)), k // 2)
            self.last.append(self.net.remote(block, block, self.second[h](k)))

    def forward(self):
        blocks = {}
        for k in (1, 3):
            for h in (0, 1):
                mine, other = self.me[h]
                self.near[h, k].wait_recv()
                blocks[h, k] = self.spot(h, mod(mine - k, 4), other)
                cut = self.part(blocks[h, k], k // 2)
                self.far[h, k] = self.net.remote(cut, cut, self.first[h](k))
        for (h, k), block in blocks.items():
            self.send(h, 4 - k, block)

    def middle(self):
        for h in (0, 1):
            self.relay(h, 0)
        for h in (0, 1):
            for k in (1, 3):
                self.far[h, k].wait_recv()
            mine, other = self.me[h]
            self.send(h, 2, self.spot(h, mod(mine + 2, 4), other))

    def finish(self):
        for a in (1, 3, 2):
            for h in (0, 1):
                self.relay(h, a)

    def arrive(self):
        for copy in self.last:
            copy.wait_recv()
        for copy in self.kept:
            copy.wait()

    def end(self):
        for copies in (self.near, self.far, self.side):
            for copy in copies.values():
                copy.wait_send()
        for copy in self.last:
            copy.wait_send()


class RingDP:
    def __init__(self, net, p, own, slot, part):
        self.net, self.p, self.slot, self.part = net, p, slot, part
        here = slot(p.dp)
        self.kept = [] if own is None else [net.copy(own, here)]
        own = here if own is None else own
        self.near = {k: net.remote(own, here, p.at_z(k)) for k in (1, 3)}
        self.swap = {0: [net.remote(own, here, p.sibling())]}
        self.far = {}

    def forward(self, *ks):
        net, p = self.net, self.p
        for k in ks or (1, 3):
            self.near[k].wait_recv()
            block = self.slot(mod(p.z - k, 4) * 2 + p.core)
            cut = self.part(block, k // 2)
            self.far[k] = net.remote(cut, cut, p.at_z(k))
            self.swap[k] = [net.remote(block, block, p.sibling())]

    def finish(self):
        net, p = self.net, self.p
        self.swap[2] = []
        for k in (1, 3):
            self.far[k].wait_recv()
            cut = self.part(self.slot(mod(p.z + 2, 4) * 2 + p.core), k // 2)
            self.swap[2].append(net.remote(cut, cut, p.sibling()))

    def arrive(self, k):
        if k == 0:
            for copy in self.kept:
                copy.wait()
            self.kept = []
        for copy in self.swap[k]:
            copy.wait_recv()

    def end(self, arrived=False):
        for copy in (*self.near.values(), *self.far.values()):
            copy.wait_send()
        for copies in self.swap.values():
            for copy in copies:
                copy.wait_send() if arrived else copy.wait()
        for copy in self.kept:
            copy.wait()


class RingSum:
    def __init__(self, net, peer, block, part, through, got):
        self.net, self.peer, self.block, self.part = net, peer, block, part
        self.through, self.got = through, got
        self.far, self.near = {}, []

    def start_far(self):
        for k in (1, 3):
            cut = self.part(self.block(2), k // 2)
            self.far[k] = self.net.remote(cut, self.through[k // 2], self.peer(k))

    def start_near(self, k):
        i = 1 - k // 2
        cut = self.part(self.block(k), i)
        self.near.append(self.net.remote(cut, self.part(self.got[k // 2], i), self.peer(k)))

    def start(self):
        self.start_far()
        for k in (1, 3):
            self.start_near(k)

    def forward(self):
        for k in (1, 3):
            i = k // 2
            self.far[k].wait_recv()
            cut = self.part(self.block(k), i)
            add_all(cut, [cut, self.through[i]])
            self.near.append(self.net.remote(cut, self.part(self.got[i], i), self.peer(k)))

    def end(self, out):
        for copy in self.far.values():
            copy.wait_send()
        for copy in self.near:
            copy.wait()
        add_all(out, [self.block(0), self.got[0], self.got[1]])


class SumDP:
    def __init__(self, net, p, part, cut, mine, sib, through, got, out, load=True):
        self.net, self.p, self.part, self.mine, self.sib, self.out = net, p, part, mine, sib, out
        self.ring = RingSum(net, p.at_z, lambda k: mine(mod(p.z + k, 4)), cut, through, got)
        self.load, self.copies = load, {}

    def swap(self, k):
        net, p = self.net, self.p
        z = mod(p.z + k, 4)
        self.copies[k] = [net.remote(self.part(2 * z + 1 - p.core), self.sib.at[z], p.sibling())]
        if self.load:
            self.copies[k].append(net.copy(self.part(2 * z + p.core), self.mine(z)))

    def join(self, k):
        for copy in self.copies[k]:
            copy.wait()
        z = mod(self.p.z + k, 4)
        add_all(self.mine(z), [self.mine(z), self.sib.at[z]])

    def begin(self):
        for k in (2, 1, 3, 0):
            self.swap(k)
        self.join(2)
        self.ring.start_far()
        for k in (1, 3):
            self.join(k)
            self.ring.start_near(k)
        self.join(0)

    def forward(self):
        self.ring.forward()

    def end(self):
        self.ring.end(self.out)


class SumXY:
    def __init__(self, net, p, cut, part, first, second, piece):
        self.p, self.piece = p, piece
        self.cut = cut
        x, y = (lambda k: mod(p.x + k, 4)), (lambda k: mod(p.y + k, 4))
        self.one = [
            RingSum(net, p.at_x, lambda k: cut(0, None, x(k)), part, *first[0]),
            RingSum(net, p.at_y, lambda k: cut(1, y(k), None), part, *first[1]),
        ]
        self.two = [
            RingSum(net, p.at_y, lambda k: cut(0, y(k), p.x), part, *second[0]),
            RingSum(net, p.at_x, lambda k: cut(1, p.y, x(k)), part, *second[1]),
        ]

    def start(self):
        for ring in self.one:
            ring.start()

    def forward(self):
        for ring in self.one:
            ring.forward()

    def turn(self):
        p = self.p
        for h, own in ((0, self.cut(0, None, p.x)), (1, self.cut(1, p.y, None))):
            self.one[h].end(own)
            self.two[h].start()

    def finish(self):
        for ring in self.two:
            ring.forward()

    def end(self):
        for h in (0, 1):
            self.two[h].end(self.piece(h))


def add_all(out, terms):
    *lead, rows, lanes = out.shape
    step_rows = min(rows, max(16, (24 * 1024 // lanes) // 16 * 16))
    while rows % step_rows:
        step_rows -= 16
    steps = rows // step_rows
    count = steps
    for n in lead:
        count *= n

    def step(i, carry):
        j, r = i // steps, lax.rem(i, steps)
        index = []
        for n in reversed(lead):
            index.insert(0, lax.rem(j, n))
            j = j // n
        at = (*index, pl.ds(pl.multiple_of(r * step_rows, 16), step_rows), slice(None))
        total = terms[0][at].astype(F32)
        for term in terms[1:]:
            total = total + term[at].astype(F32)
        out[at] = total.astype(out.dtype)
        return carry

    lax.fori_loop(0, count, step, 0)


def call(body, ident, outs, out_places, remotes, locals_, scratch, *args, vmem=56):
    return pl.pallas_call(
        body,
        out_shape=outs,
        in_specs=[ANY] * len(args),
        out_specs=out_places,
        scratch_shapes=[
            *scratch,
            pltpu.SemaphoreType.DMA((remotes,)),
            pltpu.SemaphoreType.DMA((remotes,)),
            pltpu.SemaphoreType.DMA((locals_,)),
        ],
        compiler_params=pltpu.CompilerParams(
            collective_id=ident, has_side_effects=True, vmem_limit_bytes=vmem << 20
        ),
    )(*args)


def shape(*dims, dtype=BF):
    return jax.ShapeDtypeStruct(dims, dtype)


def rows_of(n):
    return lambda ref, i: ref.at[pl.ds(0, n)] if i == 0 else ref.at[pl.ds(n, ref.shape[0] - n)]


def half(ref, h, n=64):
    return ref.at[pl.ds(h * n, n)]


def sum_dp_scratch(rows=BLOCK, lanes=D):
    return [
        pltpu.VMEM((ZN, rows, lanes), BF),
        pltpu.VMEM((ZN, rows, lanes), BF),
        pltpu.VMEM((rows // 2, lanes), BF),
        pltpu.VMEM((rows // 2, lanes), BF),
        pltpu.VMEM((rows, lanes), BF),
        pltpu.VMEM((rows, lanes), BF),
    ]


def sum_dp(net, p, part, scratch, out):
    mine, sib, t0, t1, g0, g1 = scratch
    cut = rows_of(sib.shape[1] // 2)
    return SumDP(net, p, part, cut, lambda z: mine.at[z], sib, (t0, t1), (g0, g1), out)


def ring_scratch(rows, lanes):
    return [pltpu.VMEM((3, n, rows, lanes), BF) for n in (2, 2, 4, 4)]


def ring_buffers(refs):
    return (refs[0], refs[1]), (refs[2], refs[3])


CHUNK = 256
CHUNKS = LENGTH // CHUNK
SCALE = HD ** (-0.5)


def span(j):
    return max(0, j * CHUNK - WINDOW), (j + 1) * CHUNK


def score_block(k, q_t, hi, j):
    low, high = span(j)
    s = jnp.dot(k[low:high, :], q_t[:, j * CHUNK : (j + 1) * CHUNK], preferred_element_type=F32)
    s = s * SCALE
    key = low + lax.broadcasted_iota(jnp.int32, s.shape, 0)
    query = j * CHUNK + lax.broadcasted_iota(jnp.int32, s.shape, 1)
    last = hi[low:high, :]
    last = jnp.concatenate([last] * (CHUNK // 128), axis=1)
    return jnp.where((query >= key) & (query <= last), s, NEG_LARGE)


def last_readers(lengths, pad):
    key = lax.broadcasted_iota(jnp.int32, (LENGTH, BLOCK), 0)
    end = jnp.int32(0)
    ends = []
    for i in range(4):
        end = end + lengths[0, i]
        ends.append(end)
    doc = jnp.full(key.shape, ends[3], jnp.int32)
    for end in reversed(ends[:3]):
        doc = jnp.where(key < end, end, doc)
    hi = jnp.minimum(key + (WINDOW - 1), doc - 1)
    return jnp.where(key >= LENGTH - pad[0, 0], key, hi)


def turn(values, cosine, sine):
    a, b = values[: HD // 2], values[HD // 2 :]
    return jnp.concatenate([a * cosine - b * sine, b * cosine + a * sine], axis=0)


def forward(
    x, pos, freq, gain_a, gain_m, w_query, w_key, w_value, w_out_t, w_gate, w_up, w_down_t, dd, lengths, pad
):
    def body(
        x, pos, freq, gain_a, gain_m, w_query, w_key, w_value, w_out_t, w_gate, w_up, w_down_t, dd, lengths, pad,
        seq, wdh, home_out, heads_out, part0, part1, ypart,
        q_t, k_t, v_t, top, total, cosine, sine, resid, dresid, da_t,
        rows, spot, w, w_t, wfp, k, att, wo, wf, cot_all, home, xv, hi, wqv, wkv, wvv, wgrp, wraw, wpiece, gain,
        hid, mixed, dgu, epart, e2, sib, t0, t1, g0, g1, grad_v, dat, heads, *rest,
    ):
        rings, (send, recv, local) = rest[:8], rest[8:]
        p = Place()
        net = Net(send, recv, local)
        net.m = 1
        load_x = net.copy(x, xv)
        at_rows = pl.ds(pl.multiple_of(p.y * 48, 16), 48)
        load_pieces = [
            net.copy(
                ref.at[at_rows, pl.ds(pl.multiple_of(f * FSH + p.x * 128, 128), 128)], wraw.at[f, i]
            )
            for i, ref in enumerate((w_gate, w_up, w_down_t))
            for f in range(DP)
        ]
        load_w = [net.copy(a, b) for a, b in ((w_query, wqv), (w_key, wkv), (w_value, wvv))]
        greet([p.at_ctx(i) for i in range(1, CTX)] + [p.at_dp(i) for i in range(1, DP)])
        rank = lax.rem(p.ctx, 2)

        def message(b):
            return pltpu.make_async_remote_copy(
                src_ref=att.at[:, pl.ds(b * BLOCK, BLOCK)],
                dst_ref=home.at[p.ctx],
                send_sem=send.at[b],
                recv_sem=recv.at[p.ctx],
                device_id=(p.dp, jnp.int32(b)),
                device_id_type=MESH,
            )

        def arrival(c):
            return pltpu.make_async_remote_copy(
                src_ref=att.at[:, pl.ds(0, BLOCK)],
                dst_ref=home.at[c],
                send_sem=send.at[c],
                recv_sem=recv.at[c],
                device_id=(p.dp, jnp.int32(c)),
                device_id_type=MESH,
            )

        def kept(b):
            return pltpu.make_async_copy(
                att.at[:, pl.ds(b * BLOCK, BLOCK)], home.at[p.ctx], local.at[0]
            )

        net.n = CTX
        load_x.wait()
        first = xv[...].astype(F32)
        inv = lax.rsqrt(jnp.mean(first * first, axis=-1, keepdims=True) + EPSILON)
        rows[p.ctx] = (first * inv).astype(BF)
        spot[p.ctx] = jnp.broadcast_to(pos[...].astype(F32), (16, BLOCK))
        spots = GatherXY(net, p, None, lambda h, y, x: spot.at[y * 4 + x, pl.ds(h * 8, 8)])
        tokens = RingXY(
            net, p, None, lambda h, y, x: rows.at[y * 4 + x, pl.ds(h * 64, 64)], rows_of(32)
        )

        gain[0] = jnp.broadcast_to(gain_a[...].astype(F32)[None], (BLOCK, SHARD)).T
        gain[1] = jnp.broadcast_to(gain_m[...].astype(F32)[None], (BLOCK, SHARD)).T
        for copy in load_w:
            copy.wait()
        scale = gain[0, :, :1]
        for g in range(HK):
            block = jnp.concatenate(
                [
                    wqv[:, g * 2 * HD : (g + 1) * 2 * HD],
                    wkv[:, g * HD : (g + 1) * HD],
                    wvv[:, g * HD : (g + 1) * HD],
                ],
                axis=1,
            )
            wgrp[g] = (block.astype(F32) * scale).astype(BF)
        job = RingDP(net, p, wgrp.at[p.ctx // 2], lambda i: w.at[i], rows_of(96))
        for copy in load_pieces:
            copy.wait()
        scale = gain[1, pl.ds(pl.multiple_of(p.y * 48, 16), 48), :]
        for f in range(DP):
            for i in (0, 1):
                wpiece[f, i] = (wraw[f, i].astype(F32) * scale).astype(BF)
            wpiece[f, 2] = wraw[f, 2]
        ffw = Exchange(net, p, lambda i: wpiece.at[i], lambda i: wfp.at[:, i])
        spots.forward()
        out = RingDP(net, p, w_out_t, lambda i: wo.at[i], rows_of(96))
        tokens.forward()
        hi[...] = last_readers(lengths, pad)
        tokens.middle()
        job.forward()
        out.forward()
        cot = RingDP(net, p, dd, lambda i: cot_all.at[i], rows_of(64))
        job.finish()
        tokens.finish()
        ffw.end()
        wts = RingXY(
            net,
            p,
            lambda h: wfp.at[:, pl.ds(4 * h, 4)],
            lambda h, y, x: wf.at[
                :,
                pl.ds(4 * h, 4),
                pl.ds(pl.multiple_of(y * 48, 16), 48),
                pl.ds(pl.multiple_of(x * 128, 128), 128),
            ],
            lambda ref, i: ref.at[:, pl.ds(2 * i, 2)],
        )
        for i in (0, 1, 3, 2):
            job.arrive(i)
        job.end(arrived=True)
        w_t[...] = w[...].reshape(D, GROUP).T
        spots.end()
        for j in range(CHUNKS):
            at = slice(j * CHUNK, (j + 1) * CHUNK)
            angles = freq[...] * jnp.concatenate(
                [spot[2 * j, :1, :], spot[2 * j + 1, :1, :]], axis=1
            )
            cosine[:, at], sine[:, at] = jnp.cos(angles), jnp.sin(angles)
        tokens.arrive()
        tokens.end()
        outs = [net.copy(rows, seq)]
        w_own = jnp.concatenate(
            [w_t[pl.ds(pl.multiple_of(rank * HD, 16), HD), :], w_t[2 * HD :, :]], axis=0
        )
        for j in range(CHUNKS):
            at = slice(j * CHUNK, (j + 1) * CHUNK)
            block = rows[2 * j : 2 * j + 2].reshape(CHUNK, D)
            cos, sin = cosine[:, at], sine[:, at]
            proj = dot(w_own, block, ((1,), (1,)))
            q_t[:, at] = turn(proj[:HD], cos, sin).astype(BF)
            key = turn(proj[HD : 2 * HD], cos, sin).astype(BF)
            k_t[:, at] = key
            k[at, :] = key.T
            v_t[:, at] = proj[2 * HD :].astype(BF)
            low, high = span(j)
            s = score_block(k, q_t, hi, j)
            m = jnp.max(s, axis=0, keepdims=True)
            e = jnp.exp(s - m)
            t = jnp.sum(e, axis=0, keepdims=True)
            prob = (e * (1.0 / t)).astype(BF)
            att[:, at] = jnp.dot(v_t[:, low:high], prob, preferred_element_type=F32).astype(BF)
            top[:, at] = m
            total[:, at] = t
            for b in (2 * j, 2 * j + 1):

                @pl.when(p.ctx == b)
                def _():
                    kept(b).start()

                @pl.when(p.ctx != b)
                def _():
                    message(b).start()

            if j == 1:
                wts.forward()
            if j == 2:
                out.finish()
                cot.forward()
            if j == 4:
                wts.middle()
            if j == 3:
                cot.finish()
        wts.finish()
        for i in (0, 1, 3, 2):
            out.arrive(i)
        for b in range(CTX):

            @pl.when(p.ctx == b)
            def _():
                kept(b).wait()

            @pl.when(p.ctx != b)
            def _():
                message(b).wait_send()
                arrival(b).wait_recv()

        own = home[...].reshape(D, BLOCK).T
        y1 = xv[...].astype(F32) + dot(own, wo[...].reshape(D, D), ((1,), (1,)))
        resid[...] = y1
        inv = lax.rsqrt(jnp.mean(y1 * y1, axis=-1, keepdims=True) + EPSILON)
        hid[p.dp] = (y1 * inv).astype(BF)
        ring = RingDP(net, p, None, lambda i: hid.at[i], rows_of(64))
        for i in (0, 1, 3, 2):
            cot.arrive(i)
        w_gate, w_up, w_down = (wf.at[i] for i in range(3))
        sums = SumDP(
            net, p, lambda i: epart.at[i], rows_of(64), lambda z: epart.at[2 * z + p.core], sib,
            (t0, t1), (g0, g1), e2, load=False,
        )

        def work(k):
            z = mod(p.z + k, 4)
            pair = pl.ds(2 * z, 2)
            block = hid[pair].reshape(2 * BLOCK, D)
            wg, wu = w_gate[...].reshape(D, FSH), w_up[...].reshape(D, FSH)
            gate = jnp.dot(block, wg, preferred_element_type=F32)
            up = jnp.dot(block, wu, preferred_element_type=F32)
            sig = jax.nn.sigmoid(gate)
            act = gate * sig
            mixed[pair] = (act * up).astype(BF).reshape(2, BLOCK, FSH)
            wd = w_down[...].reshape(D, FSH)
            dmix = jnp.dot(cot_all[pair].reshape(2 * BLOCK, D), wd, preferred_element_type=F32)
            dg = (dmix * up * sig * (1.0 + gate * (1.0 - sig))).astype(BF)
            du = (dmix * act).astype(BF)
            dgu[pair, :, :FSH] = dg.reshape(2, BLOCK, FSH)
            dgu[pair, :, FSH:] = du.reshape(2, BLOCK, FSH)
            e = dot(dg, wg, ((1,), (1,))) + dot(du, wu, ((1,), (1,)))
            epart[pair] = e.astype(BF).reshape(2, BLOCK, D)
            sums.swap(k)

        wts.arrive()
        wts.end()
        ring.arrive(0)
        work(0)
        ring.forward()
        ring.arrive(1)
        work(3)
        ring.finish()
        ring.arrive(3)
        work(1)
        sums.join(3)
        sums.ring.start_near(3)
        ring.arrive(2)
        work(2)
        sums.join(1)
        sums.ring.start_near(1)
        sums.join(2)
        sums.ring.start_far()
        outs.append(net.copy(home, home_out))

        def weights(left, right, *which):
            right = right[...].reshape(DP * BLOCK, FSH * len(which))
            for c in range(4):
                block = left[:, :, c * 384 : (c + 1) * 384].reshape(DP * BLOCK, 384).T
                grad = jnp.dot(block, right, preferred_element_type=F32).astype(BF)
                for n, i in enumerate(which):
                    part = grad[:, n * FSH : (n + 1) * FSH]
                    grad_v[i, 2 * c : 2 * c + 2] = part.reshape(2, SHARD, FSH)

        weights(hid, dgu, 0, 1)
        weights(cot_all, mixed, 2)

        def quarter(ref, i):
            return ref.at[:, pl.ds(2 * i, 2)]

        def column(k):
            lanes = pl.ds(pl.multiple_of(mod(p.x + k, 4) * 128, 128), 128)
            return grad_v.at[:, pl.ds(0, 4), :, lanes]

        def band(k):
            at = pl.ds(pl.multiple_of(mod(p.y + k, 4) * 48, 16), 48)
            return grad_v.at[:, pl.ds(4, 4), at, :]

        ring_x = RingSum(net, p.at_x, column, quarter, *ring_buffers(rings[:4]))
        ring_y = RingSum(net, p.at_y, band, quarter, *ring_buffers(rings[4:]))
        ring_x.start()
        ring_y.start()
        sums.join(0)
        sums.forward()
        sums.end()
        y1 = resid[...]
        inv = lax.rsqrt(jnp.mean(y1 * y1, axis=-1, keepdims=True) + EPSILON)
        u2 = y1 * inv
        e = e2[...]
        d = cot_all[p.dp].astype(F32) + inv * (e - u2 * jnp.mean(e * u2, axis=-1, keepdims=True))
        dresid[...] = d
        da = d.astype(BF)
        grad = jnp.dot(da, wo[...].reshape(D, D), preferred_element_type=F32).astype(BF)
        dat[...] = grad.T.reshape(CTX, HD, BLOCK)
        sent = [
            net.remote(dat.at[mod(p.ctx + i, CTX)], heads.at[p.ctx], p.at_ctx(i))
            for i in range(1, CTX)
        ]
        kept_dat = net.copy(dat.at[p.ctx], heads.at[p.ctx])
        grp = Exchange(net, p, lambda i: wgrp.at[i], lambda i: wdh.at[i])
        ring_x.forward()
        ring_y.forward()
        da_t[...] = da.T.reshape(DP, SHARD, BLOCK)
        wd = w_down[...].reshape(D, FSH)
        for z in range(ZN):
            y = dot(mixed[2 * z : 2 * z + 2].reshape(2 * BLOCK, FSH), wd, ((1,), (1,)))
            epart[2 * z : 2 * z + 2] = y.astype(BF).reshape(2, BLOCK, D)
        outs.append(net.copy(epart, ypart))
        kept_dat.wait()
        for copy in sent:
            copy.wait()
        outs.append(net.copy(heads, heads_out))
        ring_x.end(column(0))
        outs.append(net.copy(column(0), part0))
        ring_y.end(band(0))
        outs.append(net.copy(band(0), part1))
        for part in (out, cot, ring):
            part.end(arrived=True)
        grp.end()
        for copy in outs:
            copy.wait()

    block = (DP, BLOCK, D)
    head = shape(HD, LENGTH)
    line = shape(1, LENGTH, dtype=F32)
    angle = shape(HD // 2, LENGTH, dtype=F32)
    wide = shape(BLOCK, D, dtype=F32)
    return pl.pallas_call(
        body,
        out_shape=(
            shape(CTX, BLOCK, D),
            shape(DP, SHARD, GROUP),
            shape(CTX, HD, BLOCK),
            shape(CTX, HD, BLOCK),
            shape(3, 4, SHARD, 128),
            shape(3, 4, 48, FSH),
            shape(*block),
            head,
            head,
            head,
            line,
            line,
            angle,
            angle,
            wide,
            wide,
            shape(DP, SHARD, BLOCK),
        ),
        in_specs=[ANY, VMEM, VMEM, VMEM, VMEM, *[ANY] * 8, SMEM, SMEM],
        out_specs=[ANY] * 7 + [VMEM] * 10,
        scratch_shapes=[
            pltpu.VMEM((CTX, BLOCK, D), BF),
            pltpu.VMEM((CTX, 16, BLOCK), F32),
            pltpu.VMEM((DP, SHARD, GROUP), BF),
            pltpu.VMEM((GROUP, D), BF),
            pltpu.VMEM((3, DP, 48, 128), BF),
            pltpu.VMEM((LENGTH, HD), BF),
            pltpu.VMEM((HD, LENGTH), BF),
            pltpu.VMEM((DP, SHARD, D), BF),
            pltpu.VMEM((3, DP, SHARD, FSH), BF),
            pltpu.VMEM(block, BF),
            pltpu.VMEM((CTX, HD, BLOCK), BF),
            pltpu.VMEM((BLOCK, D), BF),
            pltpu.VMEM((LENGTH, BLOCK), jnp.int32),
            pltpu.VMEM((SHARD, D), BF),
            pltpu.VMEM((SHARD, HK * HD), BF),
            pltpu.VMEM((SHARD, HK * HD), BF),
            pltpu.VMEM((DP, SHARD, GROUP), BF),
            pltpu.VMEM((DP, 3, 48, 128), BF),
            pltpu.VMEM((DP, 3, 48, 128), BF),
            pltpu.VMEM((2, SHARD, BLOCK), F32),
            pltpu.VMEM(block, BF),
            pltpu.VMEM((DP, BLOCK, FSH), BF),
            pltpu.VMEM((DP, BLOCK, 2 * FSH), BF),
            pltpu.VMEM(block, BF),
            pltpu.VMEM((BLOCK, D), F32),
            pltpu.VMEM((ZN, BLOCK, D), BF),
            pltpu.VMEM((BLOCK // 2, D), BF),
            pltpu.VMEM((BLOCK // 2, D), BF),
            pltpu.VMEM((BLOCK, D), BF),
            pltpu.VMEM((BLOCK, D), BF),
            pltpu.VMEM((3, DP, SHARD, FSH), BF),
            pltpu.VMEM((CTX, HD, BLOCK), BF),
            pltpu.VMEM((CTX, HD, BLOCK), BF),
            *ring_scratch(SHARD, 128),
            *ring_scratch(48, FSH),
            pltpu.SemaphoreType.DMA((113,)),
            pltpu.SemaphoreType.DMA((213,)),
            pltpu.SemaphoreType.DMA((48,)),
        ],
        compiler_params=pltpu.CompilerParams(
            collective_id=2, has_side_effects=True, vmem_limit_bytes=60 << 20
        ),
    )(
        x, pos, freq, gain_a, gain_m, w_query, w_key, w_value, w_out_t, w_gate, w_up, w_down_t, dd, lengths, pad
    )


def backward(heads, att, da_t, part0, part1, ypart, wdh, seq, q_t, k_t, v_t, top, total, cosine, sine, lengths, pad):
    def body(
        heads, att, da_t, part0, part1, ypart, wdh, seq, q_t, k_t, v_t, top, total, cosine, sine, lengths, pad,
        e1, ysum, gff, gatt,
        hi, rows, k, v, q, do, do_t, dk, dv, out, wide, heads_v, att_all, da_all, dwj, full, away, comb,
        dwo, w0, f0, s0, back, wdh_v, dh1, wide0, wide1, piece, grads, *rest,
    ):
        rings, rest = rest[:8], rest[8:]
        j_sib, j_t0, j_t1, j_g0, j_g1, *rest = rest
        h_sib, h_t0, h_t1, h_g0, h_g1, *rest = rest
        y_scratch, (send, recv, local) = rest[:6], rest[6:]
        p = Place()
        net = Net(send, recv, local)
        group, rank = p.ctx // 2, lax.rem(p.ctx, 2)
        home = group == p.dp
        partner = (p.dp, p.ctx + 1 - 2 * rank)

        barrier = pltpu.get_barrier_semaphore()
        others = xy_peers(p) + [p.at_dp(i) for i in range(1, DP)]
        for peer in others:
            pl.semaphore_signal(barrier, inc=1, device_id=peer, device_id_type=MESH)
        for i in range(DP):
            for r in range(2):

                @pl.when(jnp.logical_not(home & (p.dp == i) & (rank == r)))
                def _():
                    peer = (jnp.int32(i), 2 * p.dp + r)
                    pl.semaphore_signal(barrier, inc=1, device_id=peer, device_id_type=MESH)

        pl.semaphore_wait(barrier, CTX + len(others) - home.astype(jnp.int32))

        slot = p.dp * 2 + rank

        def lanes_of(b):
            at = b * BLOCK
            return pl.ds(at if isinstance(b, int) else pl.multiple_of(at, BLOCK), BLOCK)

        def message(b, spot):
            return pltpu.make_async_remote_copy(
                src_ref=out.at[:, lanes_of(b)],
                dst_ref=back.at[spot],
                send_sem=send.at[b],
                recv_sem=recv.at[spot],
                device_id=(group, jnp.int32(b)),
                device_id_type=MESH,
            )

        def own(b):
            return pltpu.make_async_copy(
                out.at[:, lanes_of(b)], back.at[slot], local.at[0]
            )

        net.n, net.m = CTX, 1

        load_wide = [net.copy(part0, wide0), net.copy(part1, wide1)]
        load_heads = net.copy(heads, heads_v)
        das = Exchange(net, p, lambda i: da_t.at[i], lambda i: da_all.at[i])
        load_rows = net.copy(seq, rows)
        atts = RingDP(net, p, att, lambda i: att_all.at[i], rows_of(D // 2))
        load_wdh = net.copy(wdh, wdh_v)

        def quarter(ref, i):
            return ref.at[:, pl.ds(2 * i, 2)]

        def band(k):
            return wide0.at[:, :, pl.ds(pl.multiple_of(mod(p.y + k, 4) * 48, 16), 48), :]

        def column(k):
            return wide1.at[:, :, :, pl.ds(pl.multiple_of(mod(p.x + k, 4) * 128, 128), 128)]

        ring_y = RingSum(net, p.at_y, band, quarter, *ring_buffers(rings[:4]))
        ring_x = RingSum(net, p.at_x, column, quarter, *ring_buffers(rings[4:]))
        for copy in load_wide:
            copy.wait()
        ring_y.start()
        ring_x.start()
        res = sum_dp(net, p, lambda i: ypart.at[i], y_scratch, ysum)
        for i in (2, 1, 3, 0):
            res.swap(i)
        k[...] = k_t[...].T
        v[...] = v_t[...].T
        ring_y.forward()
        ring_x.forward()
        q[...] = q_t[...].T
        hi[...] = last_readers(lengths, pad)
        dk[...] = jnp.zeros_like(dk)
        dv[...] = jnp.zeros_like(dv)
        ring_y.end(piece.at[:, pl.ds(0, 4)])
        ring_x.end(piece.at[:, pl.ds(4, 4)])
        swap = Exchange(net, p, lambda i: piece.at[:, i], lambda i: grads.at[i])
        load_heads.wait()
        for b in range(CTX):
            do_t[:, b * BLOCK : (b + 1) * BLOCK] = heads_v[b]
        do[...] = do_t[...].T

        def chunk(j):
            low, high = span(j)
            at = slice(j * CHUNK, (j + 1) * CHUNK)
            s = score_block(k, q_t, hi, j)
            prob = jnp.exp(s - top[:, at]) * (1.0 / total[:, at])
            dp = jnp.dot(v[low:high, :], do_t[:, at], preferred_element_type=F32)
            inner = jnp.sum(prob * dp, axis=0, keepdims=True)
            ds = (prob * (dp - inner)).astype(BF)
            dq = jnp.dot(k_t[:, low:high], ds, preferred_element_type=F32) * SCALE
            dk[low:high, :] += jnp.dot(ds, q[at, :], preferred_element_type=F32)
            dv[low:high, :] += jnp.dot(prob.astype(BF), do[at, :], preferred_element_type=F32)
            cos, sin = cosine[:, at], -sine[:, at]
            out[:HD, at] = turn(dq, cos, sin).astype(BF)
            out[HD : 2 * HD, at] = turn(dk[at, :].T * SCALE, cos, sin).astype(BF)
            out[2 * HD :, at] = dv[at, :].T.astype(BF)

        def depart(first):
            for i in range(8):
                b = first + lax.rem(p.ctx + i, 8)
                here = home & (p.ctx == b)

                @pl.when(here)
                def _():
                    own(b).start()

                @pl.when(jnp.logical_not(here))
                def _():
                    message(b, slot).start()

        gather = None
        for j in reversed(range(CHUNKS)):
            chunk(j)
            if j in (4, 0):
                depart(2 * j)
            if j == 5:
                swap.end()
                gather = RingXY(
                    net,
                    p,
                    lambda h: grads.at[pl.ds(4 * h, 4)],
                    lambda h, y, x: gff.at[
                        pl.ds(4 * h, 4),
                        :,
                        pl.ds(pl.multiple_of(y * 48, 16), 48),
                        pl.ds(pl.multiple_of(x * 128, 128), 128),
                    ],
                    rows_of(2),
                )
            if j == 3:
                atts.forward()
            if j == 2:
                for i in (2, 1, 3, 0):
                    res.join(i)

        mine = pl.multiple_of(rank * HD, 16)
        other = pl.multiple_of((1 - rank) * HD, 16)
        wide[pl.ds(mine, HD), :] = out[:HD, :]
        wide[pl.ds(other, HD), :] = jnp.zeros((HD, LENGTH), BF)
        wide[2 * HD :, :] = out[HD:, :]
        load_rows.wait()
        grad = jnp.dot(wide[...], rows[...].reshape(LENGTH, D), preferred_element_type=F32)
        dwj[...] = grad.T.astype(BF).reshape(DP, SHARD, GROUP)
        proj = SumDP(
            net, p, lambda i: dwj.at[i], rows_of(96), lambda z: dwj.at[2 * z + p.core], j_sib,
            (j_t0, j_t1), (j_g0, j_g1), full, load=False,
        )
        proj.begin()
        gather.forward()
        atts.finish()

        das.end()
        for i in (0, 1, 3, 2):
            atts.arrive(i)
        atts.end(arrived=True)
        grad = dot(da_all[0], att_all[0], ((1,), (1,)))
        for i in range(1, DP):
            grad += dot(da_all[i], att_all[i], ((1,), (1,)))
        dwo[...] = grad.astype(BF)
        wide_cuts = [net.copy(dwo.at[:, pl.ds(pl.multiple_of(p.x * 384, 128), 384)], w0)]
        for i in (1, 3, 2):
            lanes = pl.ds(pl.multiple_of(mod(p.x + i, 4) * 384, 128), 384)
            wide_cuts.append(net.remote(dwo.at[:, lanes], f0.at[i - 1], p.at_x(i)))
        gather.middle()
        proj.forward()

        load_wdh.wait()
        inp = SumDP(
            net, p, lambda i: dh1.at[i], rows_of(64), lambda z: dh1.at[2 * z + p.core], h_sib,
            (h_t0, h_t1), (h_g0, h_g1), e1, load=False,
        )
        for spot in range(CTX):

            @pl.when(jnp.logical_not(home & (slot == spot)))
            def _():
                message(0, spot).wait_recv()

        for b in range(CTX):
            here = home & (p.ctx == b)

            @pl.when(here)
            def _():
                own(b).wait()

            @pl.when(jnp.logical_not(here))
            def _():
                message(b, slot).wait_send()

        def inputs(step):
            z = mod(p.z + step, 4)
            turned = []
            for core in (0, 1):
                i = 2 * z + core
                first, second = back[2 * i].astype(F32), back[2 * i + 1].astype(F32)
                both = jnp.concatenate([first[:HD], second[:HD], first[HD:] + second[HD:]], axis=0)
                turned.append(both.T.astype(BF))
            turned = jnp.concatenate(turned, axis=0)
            grad = dot(turned, wdh_v[...].reshape(D, GROUP), ((1,), (1,)))
            dh1[pl.ds(2 * z, 2)] = grad.astype(BF).reshape(2, BLOCK, D)
            inp.swap(step)

        inputs(2)
        inputs(1)
        inp.join(2)
        inp.ring.start_far()
        inputs(3)
        inp.join(1)
        inp.ring.start_near(1)
        inputs(0)
        inp.join(3)
        inp.ring.start_near(3)
        proj.end()
        theirs = full.at[pl.ds(pl.multiple_of((1 - rank) * 96, 16), 96)]
        trade = net.remote(theirs, away, partner)
        for copy in wide_cuts:
            copy.wait()
        add_all(w0, [w0] + [f0.at[i] for i in range(3)])
        tall = []
        for i in (1, 3, 2):
            at = pl.ds(pl.multiple_of(mod(p.y + i, 4) * 48, 16), 48)
            tall.append(net.remote(w0.at[at], s0.at[i - 1], p.at_y(i)))
        gather.finish()
        inp.join(0)
        inp.forward()
        res.ring.start_far()
        for i in (1, 3):
            res.ring.start_near(i)
        trade.wait()
        add_all(
            comb.at[pl.ds(0, 96)], [full.at[pl.ds(pl.multiple_of(rank * 96, 16), 96)], away]
        )
        for copy in tall:
            copy.wait()
        at = pl.ds(pl.multiple_of(p.y * 48, 16), 48)
        add_all(comb.at[pl.ds(96, 48)], [w0.at[at]] + [s0.at[i] for i in range(3)])
        small = RingXY(
            net,
            p,
            lambda h: comb.at[pl.ds(80 * h, 80 - 16 * h)],
            lambda h, y, x: gatt.at[y * 4 + x, pl.ds(80 * h, 80 - 16 * h)],
            rows_of(48),
        )
        inp.end()
        small.forward()
        res.forward()
        small.middle()
        small.finish()
        res.end()
        for part in (gather, small):
            part.arrive()
            part.end()

    head = pltpu.VMEM((LENGTH, HD), BF)
    return pl.pallas_call(
        body,
        out_shape=(
            shape(BLOCK, D, dtype=F32),
            shape(BLOCK, D, dtype=F32),
            shape(DP, 3, SHARD, FSH),
            shape(CTX, 144, GROUP),
        ),
        in_specs=[ANY] * 8 + [VMEM] * 7 + [SMEM] * 2,
        out_specs=[VMEM, VMEM, ANY, ANY],
        scratch_shapes=[
            pltpu.VMEM((LENGTH, BLOCK), jnp.int32),
            pltpu.VMEM((CTX, BLOCK, D), BF),
            head,
            head,
            head,
            head,
            pltpu.VMEM((HD, LENGTH), BF),
            pltpu.VMEM((LENGTH, HD), F32),
            pltpu.VMEM((LENGTH, HD), F32),
            pltpu.VMEM((3 * HD, LENGTH), BF),
            pltpu.VMEM((GROUP, LENGTH), BF),
            pltpu.VMEM((CTX, HD, BLOCK), BF),
            pltpu.VMEM((DP, D, BLOCK), BF),
            pltpu.VMEM((DP, SHARD, BLOCK), BF),
            pltpu.VMEM((DP, SHARD, GROUP), BF),
            pltpu.VMEM((SHARD, GROUP), BF),
            pltpu.VMEM((96, GROUP), BF),
            pltpu.VMEM((144, GROUP), BF),
            pltpu.VMEM((SHARD, D), BF),
            pltpu.VMEM((SHARD, 384), BF),
            pltpu.VMEM((3, SHARD, 384), BF),
            pltpu.VMEM((3, 48, 384), BF),
            pltpu.VMEM((CTX, 3 * HD, BLOCK), BF),
            pltpu.VMEM((DP, SHARD, GROUP), BF),
            pltpu.VMEM((DP, BLOCK, D), BF),
            pltpu.VMEM((3, 4, SHARD, 128), BF),
            pltpu.VMEM((3, 4, 48, FSH), BF),
            pltpu.VMEM((3, DP, 48, 128), BF),
            pltpu.VMEM((DP, 3, 48, 128), BF),
            *ring_scratch(48, 128),
            *ring_scratch(48, 128),
            *sum_dp_scratch(SHARD, GROUP)[1:],
            *sum_dp_scratch()[1:],
            *sum_dp_scratch(),
            pltpu.SemaphoreType.DMA((102,)),
            pltpu.SemaphoreType.DMA((169,)),
            pltpu.SemaphoreType.DMA((24,)),
        ],
        compiler_params=pltpu.CompilerParams(
            collective_id=4, has_side_effects=True, vmem_limit_bytes=60 << 20
        ),
    )(heads, att, da_t, part0, part1, ypart, wdh, seq, q_t, k_t, v_t, top, total, cosine, sine, lengths, pad)


def finish(gff, gatt, gain_a, gain_m, w_gate, w_up, w_query, w_key, w_value):
    def body(
        gff, gatt, gain_a, gain_m, w_gate, w_up, w_query, w_key, w_value,
        gate, up, down, dq, dk, dv, do, dgain_a, dgain_m,
        gv, gv_att, wg, wu, wq, wk, wv, ov, oq, ok, ow, oo, load, store,
    ):
        lanes = [pl.ds(f * FSH, FSH) for f in range(DP)]
        loads, stores = [], []

        def fetch(*pairs):
            copies = [
                pltpu.make_async_copy(a, b, load.at[len(loads) + i]) for i, (a, b) in enumerate(pairs)
            ]
            loads.extend(copies)
            for copy in copies:
                copy.start()
            return copies

        def put(a, b):
            copy = pltpu.make_async_copy(a, b, store.at[len(stores)])
            stores.append(copy)
            copy.start()

        steps = [
            fetch(
                (gff.at[f], gv.at[f]),
                (w_gate.at[:, lanes[f]], wg.at[:, lanes[f]]),
                (w_up.at[:, lanes[f]], wu.at[:, lanes[f]]),
            )
            for f in range(DP)
        ]
        rest = fetch((gatt, gv_att), (w_query, wq), (w_key, wk), (w_value, wv))

        def column(gain):
            return jnp.broadcast_to(gain[...].astype(F32)[None], (BLOCK, SHARD)).T[:, :1]

        def line(total):
            return jnp.broadcast_to(total, (SHARD, BLOCK)).T[0]

        rows = column(gain_m)
        total = jnp.zeros((SHARD, FSH), F32)
        for f in range(DP):
            for copy in steps[f]:
                copy.wait()
            g, u = gv[f, 0].astype(F32), gv[f, 1].astype(F32)
            total += g * wg[:, lanes[f]].astype(F32) + u * wu[:, lanes[f]].astype(F32)
            ov[0, :, lanes[f]] = g * rows
            ov[1, :, lanes[f]] = u * rows
            ov[2, :, lanes[f]] = gv[f, 2].astype(F32)
            for i, out in enumerate((gate, up, down)):
                put(ov.at[i, :, lanes[f]], out.at[:, lanes[f]])
        dgain_m[...] = line(jnp.sum(total, axis=1, keepdims=True))
        for copy in rest:
            copy.wait()
        rows = column(gain_a)
        for c in range(CTX):
            y, x = divmod(c, 4)
            oo[y * 48 : (y + 1) * 48, x * 384 : (x + 1) * 384] = gv_att[c, 96:].astype(F32)
        put(oo, do)
        for g in range(HK):
            block = gv_att[2 * g : 2 * g + 2, :96].reshape(SHARD, GROUP).astype(F32)
            oq[:, g * 2 * HD : (g + 1) * 2 * HD] = block[:, : 2 * HD]
            ok[:, g * HD : (g + 1) * HD] = block[:, 2 * HD : 3 * HD]
            ow[:, g * HD : (g + 1) * HD] = block[:, 3 * HD :]
        total = jnp.zeros((SHARD, 1), F32)
        for grad, weight, out in ((oq, wq, dq), (ok, wk, dk), (ow, wv, dv)):
            total += jnp.sum(grad[...] * weight[...].astype(F32), axis=1, keepdims=True)
            grad[...] = grad[...] * rows
            put(grad, out)
        dgain_a[...] = line(total)
        for copy in stores:
            copy.wait()

    big = shape(SHARD, FF, dtype=F32)
    square = shape(SHARD, D, dtype=F32)
    small = shape(SHARD, HK * HD, dtype=F32)
    row = shape(SHARD, dtype=F32)
    return pl.pallas_call(
        body,
        out_shape=(big, big, big, square, small, small, square, row, row),
        in_specs=[ANY, ANY, VMEM, VMEM] + [ANY] * 5,
        out_specs=[ANY] * 7 + [VMEM] * 2,
        scratch_shapes=[
            pltpu.VMEM((DP, 3, SHARD, FSH), BF),
            pltpu.VMEM((CTX, 144, GROUP), BF),
            pltpu.VMEM((SHARD, FF), BF),
            pltpu.VMEM((SHARD, FF), BF),
            pltpu.VMEM((SHARD, D), BF),
            pltpu.VMEM((SHARD, HK * HD), BF),
            pltpu.VMEM((SHARD, HK * HD), BF),
            pltpu.VMEM((3, SHARD, FF), F32),
            pltpu.VMEM((SHARD, D), F32),
            pltpu.VMEM((SHARD, HK * HD), F32),
            pltpu.VMEM((SHARD, HK * HD), F32),
            pltpu.VMEM((SHARD, D), F32),
            pltpu.SemaphoreType.DMA((28,)),
            pltpu.SemaphoreType.DMA((28,)),
        ],
        compiler_params=pltpu.CompilerParams(vmem_limit_bytes=56 << 20),
    )(gff, gatt, gain_a, gain_m, w_gate, w_up, w_query, w_key, w_value)


def dot(left, right, contract):
    return lax.dot_general(left, right, (contract, ((), ())), preferred_element_type=F32)


def on_device(
    layer_input,
    cotangent,
    attn_gain,
    w_query,
    w_key,
    w_value,
    w_out,
    mlp_gain,
    w_gate,
    w_up,
    w_down,
    doc_lengths,
    rope_pos,
    pad_lengths,
):
    inputs = layer_input[0].astype(F32)
    inv_one = lax.rsqrt(jnp.mean(inputs * inputs, axis=-1, keepdims=True) + EPSILON)
    u1 = inputs * inv_one
    freq = np.float32(THETA_BASE) ** (-(np.arange(HD // 2, dtype=np.float32) * np.float32(2.0) / np.float32(HD)))
    pad = pad_lengths[:, None]
    (
        seq, wdh, att, heads, part0, part1, ypart,
        q_t, k_t, v_t, top, total, cosine, sine, resid, dresid, da_t,
    ) = forward(
        layer_input[0], rope_pos, jnp.asarray(freq[:, None]), attn_gain, mlp_gain,
        w_query, w_key, w_value, w_out.T, w_gate, w_up, w_down.T, cotangent[0], doc_lengths, pad,
    )
    e1, ysum, gff, gatt = backward(
        heads, att.reshape(D, BLOCK), da_t, part0, part1, ypart, wdh,
        seq, q_t, k_t, v_t, top, total, cosine, sine, doc_lengths, pad,
    )
    output = (resid + ysum).astype(BF)
    grad_in = dresid + inv_one * (e1 - u1 * jnp.mean(e1 * u1, axis=-1, keepdims=True))

    dwg, dwu, dwd, dwq, dwk, dwv, dwo, dgain_a, dgain_m = finish(
        gff, gatt, attn_gain, mlp_gain, w_gate, w_up, w_query, w_key, w_value
    )
    return (
        output[None],
        grad_in.astype(BF)[None],
        dgain_a,
        dwq,
        dwk,
        dwv,
        dwo.T,
        dgain_m,
        dwg,
        dwu,
        dwd.T,
    )


def solution(mesh):
    in_specs = (
        P("dp", "ctx", None),
        P("dp", "ctx", None),
        P("dp"),
        P("dp", None),
        P("dp", None),
        P("dp", None),
        P(None, "dp"),
        P("dp"),
        P("dp", None),
        P("dp", None),
        P(None, "dp"),
        P("dp", None),
        P("dp", "ctx"),
        P("dp"),
    )
    out_specs = (
        P("dp", "ctx", None),
        P("dp", "ctx", None),
        P("dp"),
        P("dp", None),
        P("dp", None),
        P("dp", None),
        P(None, "dp"),
        P("dp"),
        P("dp", None),
        P("dp", None),
        P(None, "dp"),
    )
    return jax.shard_map(
        on_device, mesh=mesh, in_specs=in_specs, out_specs=out_specs, check_vma=False
    )
```
